32 devices in a mesh: frames: 8 (over y, x, core), rows: 4 (over z).
Axes of the slice: x: 2, y: 2, z: 4, core: 2. Of those that a mesh axis runs over, the one named last changes fastest.
Arguments:
- input_feature_maps: float32 [96, 16, 16, 1024], P('frames', 'rows'), may hold values from -6 to 6
- sequence_slot_lookup: int32 [96], P('frames'), may hold values from 0 to 31, as said below
- sequence_span_lookup: int32 [96], P('frames'), may hold values from 8 to 32, as said below
- opening_reducer: bfloat16 [1024, 512], replicated, may hold values from -0.1875 to 0.1875
- downsampling_filter: bfloat16 [3, 3, 512, 512], replicated, may hold values from -0.09375 to 0.09375
- opening_expander: bfloat16 [512, 2048], replicated, may hold values from -0.25 to 0.25
- skip_projection: bfloat16 [1024, 2048], replicated, may hold values from -0.1875 to 0.1875
- closing_reducer: bfloat16 [2048, 512], replicated, may hold values from -0.125 to 0.125
- excite_reducer: bfloat16 [512, 32], replicated, may hold values from -0.25 to 0.25
- excite_spatial_filter: bfloat16 [3, 3, 32, 32], replicated, may hold values from -0.375 to 0.375
- excite_expander: bfloat16 [32, 512], replicated, may hold values from -4 to 4
- time_taps: bfloat16 [3, 384], replicated, may hold values from 0.19921875 to 0.796875
- spatial_filters: bfloat16 [3, 3, 3, 128, 128], replicated, may hold values from -0.1875 to 0.1875
- closing_expander: bfloat16 [512, 2048], replicated, may hold values from -0.25 to 0.25
- narrow_norm_gains: float32 [4, 512], replicated, may hold values from 0.5 to 1.5
- narrow_norm_biases: float32 [4, 512], replicated, may hold values from -3 to 3
- wide_norm_gains: float32 [3, 2048], replicated, may hold values from 0.5 to 1.5
- wide_norm_biases: float32 [3, 2048], replicated, may hold values from -3 to 3
- loss_slope_wrt_final: float32 [96, 8, 8, 2048], P('frames', 'rows'), may hold values from -6 to 6
Outputs:
- layer_output: float32 [96, 8, 8, 2048], P('frames', 'rows')
- grad_pixels: float32 [96, 16, 16, 1024], P('frames', 'rows')
- grad_narrower: float32 [1024, 512], P(None, 'rows')
- grad_strider: float32 [3, 3, 512, 512], P(None, None, None, 'rows')
- grad_widener: float32 [512, 2048], P(None, 'rows')
- grad_shortcut: float32 [1024, 2048], P(None, 'rows')
- grad_squeezer: float32 [2048, 512], P(None, 'rows')
- grad_condenser: float32 [512, 32], P(None, 'rows')
- grad_stencil: float32 [3, 3, 32, 32], P(None, None, None, 'rows')
- grad_exciter: float32 [32, 512], P(None, 'rows')
- grad_temporal: float32 [3, 384], P(None, 'rows')
- grad_kernels: float32 [3, 3, 3, 128, 128], P(None, None, None, None, 'rows')
- grad_restorer: float32 [512, 2048], P(None, 'rows')
- grad_scaling: float32 [4, 512], replicated
- grad_biasing: float32 [4, 512], replicated
- grad_amplitudes: float32 [3, 2048], replicated
- baseline_gradient: float32 [3, 2048], replicated
The draws below stay inside these ranges and needn't reach their ends.
Inputs may be any that keep to these rules, and one draw needn't show every extreme that they name: `sequence_slot_lookup`: the offset of each frame within its clip. Clips are runs of 8 or 32 frames laid end to end from frame 0; each aligned run of 96 frames holds one clip of 32 frames and eight of 8. `sequence_span_lookup`: the length of the clip that holds each frame, consistent with sequence_slot_lookup.
All inputs are finite; a program needn't handle non-finite values.
Results may differ from the reference program's by a relative error of at most 0.0003.
Values sent between devices are 32-bit elements; how exact they have to be, the bound alone decides.
A program may use at most 192 MiB of HBM per device.

```python
import jax
import jax.numpy as jnp
from jax import lax

C_IN = 1024
MID = 512
RESULT_FEATURES = 2048
RED = 32
GRP = 128
HEIGHT = 16
WIDTH = 16
FRAMES = 96


def clip_table(key):
    unit_count = FRAMES // 96
    unit_keys = jax.random.fold_in(key, 11)
    long_slots = jax.random.randint(unit_keys, (unit_count,), 0, 9).astype(jnp.int32)
    position = jnp.arange(FRAMES, dtype=jnp.int32)
    within = position % 96
    long_start = jnp.take(long_slots, position // 96) * 8
    in_long = (within >= long_start) & (within < long_start + 32)
    short_place = jnp.where(within < long_start, within % 8, (within - 32) % 8)
    offsets = jnp.where(in_long, within - long_start, short_place).astype(jnp.int32)
    lengths = jnp.where(in_long, 32, 8).astype(jnp.int32)
    return (offsets, lengths)


def draw_sequence_slot_lookup(key, part):
    offsets, lengths = clip_table(key)
    return offsets


def draw_sequence_span_lookup(key, part):
    offsets, lengths = clip_table(key)
    return lengths


def steps_of(own_key, shape, pieces, smallest, largest):
    factor_of = 1.0
    for dim, parts in pieces:
        heights = jax.random.uniform(jax.random.fold_in(jax.random.fold_in(own_key, 6), dim), (parts,), jnp.float32, smallest / len(pieces), largest / len(pieces))
        factor_of = factor_of * jnp.repeat(jnp.exp(heights), shape[dim] // parts).reshape((-1,) + (1,) * (len(shape) - 1 - dim))
    return factor_of


def normal_values(own_key, shape, scale, most, pieces=(), kind=jnp.bfloat16):
    level = steps_of(own_key, shape, pieces, -0.22, 0.18) if pieces else 1.0
    result = jax.random.normal(own_key, shape, jnp.float32) * scale * level
    return jnp.minimum(jnp.maximum(result, -most), most).astype(kind)


def setup_inputs(seed: int = 0) -> dict:
    key_of = jax.random.split(jax.random.key(seed), 20)
    return {
        "input_feature_maps": normal_values(key_of[0], (FRAMES, HEIGHT, WIDTH, C_IN), 1.0, 6.0, ((0, 8), (1, 4)), jnp.float32),
        "sequence_slot_lookup": draw_sequence_slot_lookup(jax.random.fold_in(key_of[19], 71), 0),
        "sequence_span_lookup": draw_sequence_span_lookup(jax.random.fold_in(key_of[19], 71), 0),
        "opening_reducer": normal_values(key_of[3], (C_IN, MID), C_IN ** -0.5, 0.1875),
        "downsampling_filter": normal_values(key_of[4], (3, 3, MID, MID), (9 * MID) ** -0.5, 0.09375),
        "opening_expander": normal_values(key_of[5], (MID, RESULT_FEATURES), MID ** -0.5, 0.25),
        "skip_projection": normal_values(key_of[6], (C_IN, RESULT_FEATURES), C_IN ** -0.5, 0.1875),
        "closing_reducer": normal_values(key_of[7], (RESULT_FEATURES, MID), RESULT_FEATURES ** -0.5, 0.125),
        "excite_reducer": normal_values(key_of[8], (MID, RED), MID ** -0.5, 0.25),
        "excite_spatial_filter": normal_values(key_of[9], (3, 3, RED, RED), (9 * RED) ** -0.5, 0.375),
        "excite_expander": normal_values(key_of[10], (RED, MID), 1.0, 4.0),
        "time_taps": jnp.clip(jax.random.uniform(key_of[11], (3, 3 * GRP), jnp.float32, 0.19921875, 0.796875), 0.19921875, 0.796875).astype(jnp.bfloat16),
        "spatial_filters": normal_values(key_of[12], (3, 3, 3, GRP, GRP), (9 * GRP) ** -0.5, 0.1875),
        "closing_expander": normal_values(key_of[13], (MID, RESULT_FEATURES), MID ** -0.5, 0.25),
        "narrow_norm_gains": jnp.clip(1.0 + 0.1 * jax.random.normal(key_of[14], (4, MID), jnp.float32), 0.5, 1.5),
        "narrow_norm_biases": normal_values(key_of[15], (4, MID), 0.5, 3.0, (), jnp.float32),
        "wide_norm_gains": jnp.clip(1.0 + 0.1 * jax.random.normal(key_of[16], (3, RESULT_FEATURES), jnp.float32), 0.5, 1.5),
        "wide_norm_biases": normal_values(key_of[17], (3, RESULT_FEATURES), 0.5, 3.0, (), jnp.float32),
        "loss_slope_wrt_final": normal_values(key_of[18], (FRAMES, HEIGHT // 2, WIDTH // 2, RESULT_FEATURES), 1.0, 6.0, ((0, 8), (1, 4)), jnp.float32),
    }


HIGHEST = lax.Precision.HIGHEST
EPSILON = 1e-05
LAYOUT = ('NHWC', 'HWIO', 'NHWC')

@jax.custom_vjp
def low(v):
    return lax.optimization_barrier(v.astype(jnp.bfloat16)).astype(jnp.float32)

@jax.custom_vjp
def low_back(v):
    return v

def low_keep(v):
    return (low(v), None)

def low_pass(kept, grad):
    return (grad,)

def back_keep(v):
    return (v, None)

def back_low(kept, grad):
    return (low(grad),)
low.defvjp(low_keep, low_pass)
low_back.defvjp(back_keep, back_low)

def logistic_squash(value):
    return value * jax.nn.sigmoid(value)

def standardize_features(field, gain, bias):
    center = lax.optimization_barrier(jnp.mean(field, axis=(0, 1, 2)))
    variance = lax.optimization_barrier(jnp.mean(field * field, axis=(0, 1, 2))) - center * center
    return (field - center) * lax.rsqrt(variance + EPSILON) * gain + bias

def pointwise_mapping(active, matrix):
    return jnp.einsum('fhwc,cd->fhwd', active, matrix, precision=HIGHEST)

def conv_same(field, kernel, stride):
    return lax.conv_general_dilated(field, kernel, (stride, stride), ((1, 1), (1, 1)), dimension_numbers=LAYOUT, precision=HIGHEST)

def time_mix(field, weights, earlier_boundary_filter, later_boundary_filter):
    zero_frame = jnp.zeros_like(field[:1])
    earlier = jnp.concatenate([zero_frame, field[:-1]], 0)
    later = jnp.concatenate([field[1:], zero_frame], 0)
    return weights[0] * earlier_boundary_filter * earlier + weights[1] * field + weights[2] * later_boundary_filter * later

def evaluate_model(input_feature_maps, opening_reducer, downsampling_filter, opening_expander, skip_projection, closing_reducer, excite_reducer, excite_spatial_filter, excite_expander, time_taps, spatial_filters, closing_expander, narrow_norm_gains, narrow_norm_biases, wide_norm_gains, wide_norm_biases, earlier_boundary_filter, later_boundary_filter):
    hidden_one = logistic_squash(standardize_features(pointwise_mapping(input_feature_maps, opening_reducer), narrow_norm_gains[0], narrow_norm_biases[0]))
    later_intermediate = logistic_squash(standardize_features(conv_same(hidden_one, downsampling_filter, 2), narrow_norm_gains[1], narrow_norm_biases[1]))
    main_branch = standardize_features(pointwise_mapping(later_intermediate, opening_expander), wide_norm_gains[0], wide_norm_biases[0])
    side_branch = standardize_features(pointwise_mapping(input_feature_maps[:, ::2, ::2], skip_projection), wide_norm_gains[1], wide_norm_biases[1])
    above_adjacent = logistic_squash(main_branch + side_branch)
    hidden = logistic_squash(standardize_features(pointwise_mapping(above_adjacent, closing_reducer), narrow_norm_gains[2], narrow_norm_biases[2]))
    reduced = pointwise_mapping(hidden, excite_reducer)
    following = jnp.concatenate([reduced[1:], jnp.zeros_like(reduced[:1])], 0) * later_boundary_filter
    motion = (conv_same(following, excite_spatial_filter, 1) - reduced) * later_boundary_filter
    pooled = lax.optimization_barrier(jnp.mean(motion, axis=(1, 2)))
    gating = jax.nn.sigmoid(jnp.dot(pooled, excite_expander, precision=HIGHEST))
    excited = hidden * (1.0 + gating[:, None, None, :])
    branches = [excited[..., :GRP]]
    for index in range(3):
        source = excited[..., (index + 1) * GRP:(index + 2) * GRP]
        if index > 0:
            source = source + branches[-1]
        mixed = time_mix(source, time_taps[:, index * GRP:(index + 1) * GRP], earlier_boundary_filter, later_boundary_filter)
        branches.append(conv_same(mixed, spatial_filters[index], 1))
    logistic_outcomes = logistic_squash(standardize_features(jnp.concatenate(branches, -1), narrow_norm_gains[3], narrow_norm_biases[3]))
    return logistic_squash(standardize_features(pointwise_mapping(logistic_outcomes, closing_expander), wide_norm_gains[2], wide_norm_biases[2]) + above_adjacent)

def reference(input_feature_maps, sequence_slot_lookup, sequence_span_lookup, opening_reducer, downsampling_filter, opening_expander, skip_projection, closing_reducer, excite_reducer, excite_spatial_filter, excite_expander, time_taps, spatial_filters, closing_expander, narrow_norm_gains, narrow_norm_biases, wide_norm_gains, wide_norm_biases, loss_slope_wrt_final):
    earlier_boundary_filter = (sequence_slot_lookup > 0).astype(jnp.float32)[:, None, None, None]
    later_boundary_filter = (sequence_slot_lookup < sequence_span_lookup - 1).astype(jnp.float32)[:, None, None, None]
    weight_lookup = tuple((single_item.astype(jnp.float32) for single_item in (opening_reducer, downsampling_filter, opening_expander, skip_projection, closing_reducer, excite_reducer, excite_spatial_filter, excite_expander, time_taps, spatial_filters, closing_expander, narrow_norm_gains, narrow_norm_biases, wide_norm_gains, wide_norm_biases)))

    def run(field, *weights):
        return evaluate_model(field, *weights, earlier_boundary_filter, later_boundary_filter)
    output, pull = jax.vjp(run, input_feature_maps.astype(jnp.float32), *weight_lookup)
    grads = pull(loss_slope_wrt_final.astype(jnp.float32))
    return (output, grads[0], grads[1], grads[2], grads[3], grads[4], grads[5], grads[6], grads[7], grads[8], grads[9], grads[10], grads[11], grads[12], grads[13], grads[14], grads[15])
```

```python
import jax
import jax.numpy as jnp
from jax import lax
from jax.experimental import pallas as pl
from jax.experimental.pallas import tpu as pltpu
from jax.sharding import PartitionSpec as P

HIGHEST = lax.Precision.HIGH
MESH = pl.DeviceIdType.MESH
EPSILON = 1e-05
LAYOUT = ("NHWC", "HWIO", "NHWC")


def with_halo(block, sides, width):
    for axis, dim in sides:
        count = lax.axis_size(axis)
        forward = [(i, i + 1) for i in range(count - 1)]
        backward = [(target, source) for source, target in forward]
        low = lax.ppermute(
            lax.slice_in_dim(block, block.shape[dim] - width, None, axis=dim), axis, forward
        )
        high = lax.ppermute(lax.slice_in_dim(block, 0, width, axis=dim), axis, backward)
        block = jnp.concatenate([low, block, high], axis=dim)
    return block


def from_behind(block, axis, distance):
    devices = range(lax.axis_size(axis))
    route = [(i - distance, i) for i in devices if i - distance in devices]
    return lax.ppermute(block, axis, route)


def logistic_squash(value):
    return value * jax.nn.sigmoid(value)


def unit_slope(value):
    logistic = jax.nn.sigmoid(value)
    return logistic * (1.0 + value * (1.0 - logistic))


def pointwise_mapping(active, matrix):
    return jnp.einsum("fhwc,cd->fhwd", active, matrix, precision=HIGHEST)


def project_back(grads, matrix):
    return jnp.einsum("fhwd,cd->fhwc", grads, matrix, precision=HIGHEST)


def outer_sum(active, grads):
    return jnp.einsum("fhwc,fhwd->cd", active, grads, precision=HIGHEST)


def conv_valid(padded, kernel):
    return lax.conv_general_dilated(
        padded, kernel, (1, 1), ((0, 0), (1, 1)), dimension_numbers=LAYOUT, precision=HIGHEST
    )


def conv_stride(padded, kernel):
    return lax.conv_general_dilated(
        padded, kernel, (2, 2), ((0, 0), (1, 1)), dimension_numbers=LAYOUT, precision=HIGHEST
    )


def kernel_grad(padded, kernel, grads):
    result, pull_back = jax.vjp(lambda weights: conv_valid(padded, weights), kernel)
    return pull_back(grads)[0]


def flipped(kernel):
    return jnp.transpose(kernel[::-1, ::-1], (0, 1, 3, 2))


def row_padded(field):
    return with_halo(field, (("rows", 1),), 1)


def frame_padded(field):
    return with_halo(field, (("frames", 0),), 1)


def time_mix(padded, weights, earlier_boundary_filter, later_boundary_filter):
    return (
        weights[0] * earlier_boundary_filter * padded[:-2]
        + weights[1] * padded[1:-1]
        + weights[2] * later_boundary_filter * padded[2:]
    )


def exchange_slots(source, slots, send, recv, me, count, device):
    copies = []
    for step in range(1, count):
        copy = pltpu.make_async_remote_copy(
            src_ref=source,
            dst_ref=slots.at[me],
            send_sem=send.at[step],
            recv_sem=recv.at[me],
            device_id=device(lax.rem(me + step, count)),
            device_id_type=MESH,
        )
        copy.start()
        copies.append(copy)
    slots[me] = source[...]
    for step in range(1, count):
        origin = lax.rem(me + count - step, count)
        pltpu.make_async_remote_copy(
            src_ref=source,
            dst_ref=slots.at[origin],
            send_sem=send.at[step],
            recv_sem=recv.at[origin],
            device_id=device(origin),
            device_id_type=MESH,
        ).wait_recv()
    for copy in copies:
        copy.wait_send()
    total = slots[0]
    for place in range(1, count):
        total = total + slots[place]
    return total


def sum_kernel(frames, rows, x_ref, o_ref, part, row_slots, frame_slots, rs, rr, fs, fr):
    f = lax.axis_index("frames")
    r = lax.axis_index("rows")
    barrier = pltpu.get_barrier_semaphore()
    for step in range(1, rows):
        pl.semaphore_signal(
            barrier, inc=1, device_id=(f, lax.rem(r + step, rows)), device_id_type=MESH
        )
    for step in range(1, frames):
        pl.semaphore_signal(
            barrier, inc=1, device_id=(lax.rem(f + step, frames), r), device_id_type=MESH
        )
    pl.semaphore_wait(barrier, rows + frames - 2)
    part[...] = exchange_slots(x_ref, row_slots, rs, rr, r, rows, lambda place: (f, place))
    o_ref[...] = exchange_slots(part, frame_slots, fs, fr, f, frames, lambda place: (place, r))


def global_sum(pieces, call):
    frames, rows = lax.axis_size("frames"), lax.axis_size("rows")
    sizes = [piece.size // 128 for piece in pieces]
    block = jnp.concatenate([piece.reshape(-1, 128) for piece in pieces], 0)
    total = pl.pallas_call(
        lambda *refs: sum_kernel(frames, rows, *refs),
        out_shape=jax.ShapeDtypeStruct(block.shape, jnp.float32),
        in_specs=[pl.BlockSpec(memory_space=pltpu.VMEM)],
        out_specs=pl.BlockSpec(memory_space=pltpu.VMEM),
        scratch_shapes=[
            pltpu.VMEM(block.shape, jnp.float32),
            pltpu.VMEM((rows,) + block.shape, jnp.float32),
            pltpu.VMEM((frames,) + block.shape, jnp.float32),
            pltpu.SemaphoreType.DMA((rows,)),
            pltpu.SemaphoreType.DMA((rows,)),
            pltpu.SemaphoreType.DMA((frames,)),
            pltpu.SemaphoreType.DMA((frames,)),
        ],
        compiler_params=pltpu.CompilerParams(collective_id=call, has_side_effects=True),
    )(block)
    results = []
    start = 0
    for piece, size in zip(pieces, sizes):
        results.append(total[start : start + size].reshape(piece.shape))
        start += size
    return results


def global_count(field):
    return (
        field.shape[0]
        * field.shape[1]
        * field.shape[2]
        * lax.axis_size("frames")
        * lax.axis_size("rows")
    )


def norm_forward(field, call):
    totals, squares = global_sum(
        (jnp.sum(field, axis=(0, 1, 2)), jnp.sum(field * field, axis=(0, 1, 2))), call
    )
    number = global_count(field)
    center = totals / number
    spread = lax.rsqrt(squares / number - center * center + EPSILON)
    return ((field - center) * spread, spread)


def norm_backward(grads, normed, spread, gain, call):
    bias_grad, gain_grad = global_sum(
        (jnp.sum(grads, axis=(0, 1, 2)), jnp.sum(grads * normed, axis=(0, 1, 2))), call
    )
    number = global_count(grads)
    field_grad = gain * spread * (grads - bias_grad / number - normed * (gain_grad / number))
    return (field_grad, gain_grad, bias_grad)


def layer_one(
    input_feature_maps,
    opening_reducer,
    downsampling_filter,
    opening_expander,
    skip_projection,
    narrow_norm_gains,
    narrow_norm_biases,
    wide_norm_gains,
    wide_norm_biases,
):
    normed_a, spread_a = norm_forward(pointwise_mapping(input_feature_maps, opening_reducer), 0)
    before_a = normed_a * narrow_norm_gains[0] + narrow_norm_biases[0]
    hidden_a = logistic_squash(before_a)
    upper_rim = from_behind(hidden_a[:, -1:], "rows", 1)
    padded_a = jnp.concatenate([upper_rim, hidden_a], 1)
    normed_b, spread_b = norm_forward(conv_stride(padded_a, downsampling_filter), 1)
    before_b = normed_b * narrow_norm_gains[1] + narrow_norm_biases[1]
    hidden_b = logistic_squash(before_b)
    standardized_current, spread_c = norm_forward(pointwise_mapping(hidden_b, opening_expander), 2)
    sampled = input_feature_maps[:, ::2, ::2]
    standardized_prior, spread_p = norm_forward(pointwise_mapping(sampled, skip_projection), 3)
    accumulated_total = (
        standardized_current * wide_norm_gains[0]
        + wide_norm_biases[0]
        + (standardized_prior * wide_norm_gains[1] + wide_norm_biases[1])
    )
    return {
        "normed_a": normed_a,
        "spread_a": spread_a,
        "before_a": before_a,
        "padded_a": padded_a,
        "normed_b": normed_b,
        "spread_b": spread_b,
        "before_b": before_b,
        "hidden_b": hidden_b,
        "normed_c": standardized_current,
        "spread_c": spread_c,
        "sampled": sampled,
        "normed_p": standardized_prior,
        "spread_p": spread_p,
        "summed": accumulated_total,
        "output": logistic_squash(accumulated_total),
    }


def layer_one_back(
    kept,
    out_grad,
    input_feature_maps,
    opening_reducer,
    downsampling_filter,
    opening_expander,
    skip_projection,
    narrow_norm_gains,
    wide_norm_gains,
):
    total_grad = out_grad * unit_slope(kept["summed"])
    grad_c, amp_c, base_c = norm_backward(
        total_grad, kept["normed_c"], kept["spread_c"], wide_norm_gains[0], 7)
    grad_p, amp_p, base_p = norm_backward(
        total_grad, kept["normed_p"], kept["spread_p"], wide_norm_gains[1], 8)
    grad_widener = outer_sum(kept["hidden_b"], grad_c)
    grad_shortcut = outer_sum(kept["sampled"], grad_p)
    before_b_grad = project_back(grad_c, opening_expander) * unit_slope(kept["before_b"])
    grad_b, scale_b, offset_b = norm_backward(
        before_b_grad, kept["normed_b"], kept["spread_b"], narrow_norm_gains[1], 9)
    strided, pull_stride = jax.vjp(conv_stride, kept["padded_a"], downsampling_filter)
    padded_grad, grad_strider = pull_stride(grad_b)
    lower_rim = from_behind(padded_grad[:, 0:1], "rows", -1)
    hidden_grad = padded_grad[:, 1:] + jnp.concatenate(
        [jnp.zeros_like(padded_grad[:, 1:-1]), lower_rim], 1
    )
    before_a_grad = hidden_grad * unit_slope(kept["before_a"])
    grad_a, scale_a, offset_a = norm_backward(
        before_a_grad, kept["normed_a"], kept["spread_a"], narrow_norm_gains[0], 10)
    grad_narrower = outer_sum(input_feature_maps, grad_a)
    sample_grad = project_back(grad_p, skip_projection)
    frame_count, row_count, column_count, channel_count = sample_grad.shape
    spread_out = jnp.pad(
        sample_grad[:, :, None, :, None, :], ((0, 0), (0, 0), (0, 1), (0, 0), (0, 1), (0, 0))
    )
    spread_out = spread_out.reshape(frame_count, 2 * row_count, 2 * column_count, channel_count)
    input_grad = project_back(grad_a, opening_reducer) + spread_out
    return {
        "input": input_grad,
        "narrower": grad_narrower,
        "strider": grad_strider,
        "widener": grad_widener,
        "shortcut": grad_shortcut,
        "scales": (scale_a, scale_b),
        "offsets": (offset_a, offset_b),
        "amps": (amp_c, amp_p),
        "bases": (base_c, base_p),
    }


def layer_two(
    above_adjacent,
    closing_reducer,
    excite_reducer,
    excite_spatial_filter,
    excite_expander,
    time_taps,
    spatial_filters,
    closing_expander,
    narrow_norm_gains,
    narrow_norm_biases,
    wide_norm_gains,
    wide_norm_biases,
    earlier_boundary_filter,
    later_boundary_filter,
):
    normed_a, spread_a = norm_forward(pointwise_mapping(above_adjacent, closing_reducer), 4)
    before_a = normed_a * narrow_norm_gains[2] + narrow_norm_biases[2]
    hidden = logistic_squash(before_a)
    reduced = pointwise_mapping(hidden, excite_reducer)
    incoming = from_behind(reduced[0:1], "frames", -1)
    following = jnp.concatenate([reduced[1:], incoming], 0) * later_boundary_filter
    follow_pad = row_padded(following)
    motion = (conv_valid(follow_pad, excite_spatial_filter) - reduced) * later_boundary_filter
    area = motion.shape[1] * motion.shape[2] * lax.axis_size("rows")
    pooled = lax.psum(jnp.sum(motion, axis=(1, 2)), "rows") / area
    gating = jax.nn.sigmoid(jnp.dot(pooled, excite_expander, precision=HIGHEST))
    excited = hidden * (1.0 + gating[:, None, None, :])
    width = excited.shape[-1] // 4
    branches = [excited[..., :width]]
    source_pads = []
    mixed_pads = []
    for index in range(3):
        source = excited[..., (index + 1) * width : (index + 2) * width]
        if index > 0:
            source = source + branches[-1]
        source_pad = frame_padded(source)
        mixed = time_mix(
            source_pad,
            time_taps[:, index * width : (index + 1) * width],
            earlier_boundary_filter,
            later_boundary_filter,
        )
        mixed_pad = row_padded(mixed)
        branches.append(conv_valid(mixed_pad, spatial_filters[index]))
        source_pads.append(source_pad)
        mixed_pads.append(mixed_pad)
    normed_b, spread_b = norm_forward(jnp.concatenate(branches, -1), 5)
    before_b = normed_b * narrow_norm_gains[3] + narrow_norm_biases[3]
    logistic_outcomes = logistic_squash(before_b)
    standardized_current, spread_c = norm_forward(
        pointwise_mapping(logistic_outcomes, closing_expander), 6)
    accumulated_total = (
        standardized_current * wide_norm_gains[2] + wide_norm_biases[2] + above_adjacent
    )
    return {
        "normed_a": normed_a,
        "spread_a": spread_a,
        "before_a": before_a,
        "hidden": hidden,
        "reduced": reduced,
        "follow_pad": follow_pad,
        "pooled": pooled,
        "gating": gating,
        "source_pads": source_pads,
        "mixed_pads": mixed_pads,
        "normed_b": normed_b,
        "spread_b": spread_b,
        "before_b": before_b,
        "squashed": logistic_outcomes,
        "normed_c": standardized_current,
        "spread_c": spread_c,
        "summed": accumulated_total,
        "output": logistic_squash(accumulated_total),
    }


def layer_two_back(
    kept,
    out_grad,
    above_adjacent,
    closing_reducer,
    excite_reducer,
    excite_spatial_filter,
    excite_expander,
    time_taps,
    spatial_filters,
    closing_expander,
    narrow_norm_gains,
    wide_norm_gains,
    earlier_boundary_filter,
    later_boundary_filter,
):
    total_grad = out_grad * unit_slope(kept["summed"])
    grad_c, amp_c, base_c = norm_backward(
        total_grad, kept["normed_c"], kept["spread_c"], wide_norm_gains[2], 11)
    grad_restorer = outer_sum(kept["squashed"], grad_c)
    before_b_grad = project_back(grad_c, closing_expander) * unit_slope(kept["before_b"])
    merged_grad, scale_b, offset_b = norm_backward(
        before_b_grad, kept["normed_b"], kept["spread_b"], narrow_norm_gains[3], 12)
    width = merged_grad.shape[-1] // 4
    group_grads = [merged_grad[..., :width], None, None, None]
    kernel_grads = [None, None, None]
    tap_grads = [None, None, None]
    carried = jnp.zeros_like(merged_grad[..., :width])
    for index in (2, 1, 0):
        branch_grad = merged_grad[..., (index + 1) * width : (index + 2) * width] + carried
        kernel_grads[index] = kernel_grad(
            kept["mixed_pads"][index], spatial_filters[index], branch_grad
        )
        mixed_grad = conv_valid(row_padded(branch_grad), flipped(spatial_filters[index]))
        source_pad = kept["source_pads"][index]
        tap_grads[index] = jnp.stack(
            [
                jnp.sum(mixed_grad * earlier_boundary_filter * source_pad[:-2], axis=(0, 1, 2)),
                jnp.sum(mixed_grad * source_pad[1:-1], axis=(0, 1, 2)),
                jnp.sum(mixed_grad * later_boundary_filter * source_pad[2:], axis=(0, 1, 2)),
            ]
        )
        group_taps = time_taps[:, index * width : (index + 1) * width]
        carried = time_mix(
            frame_padded(mixed_grad),
            group_taps[::-1],
            earlier_boundary_filter,
            later_boundary_filter,
        )
        group_grads[index + 1] = carried
    excited_grad = jnp.concatenate(group_grads, -1)
    gating = kept["gating"]
    hidden = kept["hidden"]
    hidden_grad = excited_grad * (1.0 + gating[:, None, None, :])
    gate_part = jnp.sum(excited_grad * hidden, axis=(1, 2)) * gating * (1.0 - gating)
    grad_exciter = jnp.dot(kept["pooled"].T, gate_part, precision=HIGHEST)
    logit_grad = lax.psum(gate_part, "rows")
    reduced = kept["reduced"]
    area = reduced.shape[1] * reduced.shape[2] * lax.axis_size("rows")
    pooled_grad = jnp.dot(logit_grad, excite_expander.T, precision=HIGHEST) / area
    motion_grad = jnp.broadcast_to(
        pooled_grad[:, None, None, :] * later_boundary_filter, reduced.shape
    )
    grad_stencil = kernel_grad(kept["follow_pad"], excite_spatial_filter, motion_grad)
    follow_grad = (
        conv_valid(row_padded(motion_grad), flipped(excite_spatial_filter)) * later_boundary_filter
    )
    outgoing = from_behind(follow_grad[-1:], "frames", 1)
    reduced_grad = jnp.concatenate([outgoing, follow_grad[:-1]], 0) - motion_grad
    grad_condenser = outer_sum(hidden, reduced_grad)
    hidden_grad = hidden_grad + project_back(reduced_grad, excite_reducer)
    before_a_grad = hidden_grad * unit_slope(kept["before_a"])
    grad_a, scale_a, offset_a = norm_backward(
        before_a_grad, kept["normed_a"], kept["spread_a"], narrow_norm_gains[2], 13)
    grad_squeezer = outer_sum(above_adjacent, grad_a)
    upper_grad = total_grad + project_back(grad_a, closing_reducer)
    return {
        "upper": upper_grad,
        "squeezer": grad_squeezer,
        "condenser": grad_condenser,
        "stencil": grad_stencil,
        "exciter": grad_exciter,
        "temporal": jnp.concatenate(tap_grads, 1),
        "kernels": jnp.stack(kernel_grads),
        "restorer": grad_restorer,
        "scales": (scale_a, scale_b),
        "offsets": (offset_a, offset_b),
        "amp": amp_c,
        "base": base_c,
    }


def flat(matrix):
    return matrix.reshape(-1, matrix.shape[-1])


def unflat(piece, model):
    return piece.reshape(model.shape[:-1] + (piece.shape[-1],))


def shards(
    input_feature_maps,
    sequence_slot_lookup,
    sequence_span_lookup,
    opening_reducer,
    downsampling_filter,
    opening_expander,
    skip_projection,
    closing_reducer,
    excite_reducer,
    excite_spatial_filter,
    excite_expander,
    time_taps,
    spatial_filters,
    closing_expander,
    narrow_norm_gains,
    narrow_norm_biases,
    wide_norm_gains,
    wide_norm_biases,
    loss_slope_wrt_final,
):
    opening_reducer = opening_reducer.astype(jnp.float32)
    downsampling_filter = downsampling_filter.astype(jnp.float32)
    opening_expander = opening_expander.astype(jnp.float32)
    skip_projection = skip_projection.astype(jnp.float32)
    closing_reducer = closing_reducer.astype(jnp.float32)
    excite_reducer = excite_reducer.astype(jnp.float32)
    excite_spatial_filter = excite_spatial_filter.astype(jnp.float32)
    excite_expander = excite_expander.astype(jnp.float32)
    time_taps = time_taps.astype(jnp.float32)
    spatial_filters = spatial_filters.astype(jnp.float32)
    closing_expander = closing_expander.astype(jnp.float32)
    earlier_boundary_filter = (sequence_slot_lookup > 0).astype(jnp.float32)[:, None, None, None]
    later_boundary_filter = (sequence_slot_lookup < sequence_span_lookup - 1).astype(jnp.float32)[
        :, None, None, None
    ]
    first = layer_one(
        input_feature_maps,
        opening_reducer,
        downsampling_filter,
        opening_expander,
        skip_projection,
        narrow_norm_gains,
        narrow_norm_biases,
        wide_norm_gains,
        wide_norm_biases,
    )
    above_adjacent = first["output"]
    again, incoming_grad = above_adjacent, loss_slope_wrt_final
    second = layer_two(
        again,
        closing_reducer,
        excite_reducer,
        excite_spatial_filter,
        excite_expander,
        time_taps,
        spatial_filters,
        closing_expander,
        narrow_norm_gains,
        narrow_norm_biases,
        wide_norm_gains,
        wide_norm_biases,
        earlier_boundary_filter,
        later_boundary_filter,
    )
    second_backward = layer_two_back(
        second,
        incoming_grad,
        again,
        closing_reducer,
        excite_reducer,
        excite_spatial_filter,
        excite_expander,
        time_taps,
        spatial_filters,
        closing_expander,
        narrow_norm_gains,
        wide_norm_gains,
        earlier_boundary_filter,
        later_boundary_filter,
    )
    first_backward = layer_one_back(
        first,
        second_backward["upper"],
        input_feature_maps,
        opening_reducer,
        downsampling_filter,
        opening_expander,
        skip_projection,
        narrow_norm_gains,
        wide_norm_gains,
    )
    pieces = (
        lax.psum_scatter(flat(first_backward["narrower"]), "rows", scatter_dimension=1, tiled=True),
        lax.psum_scatter(flat(first_backward["strider"]), "rows", scatter_dimension=1, tiled=True),
        lax.psum_scatter(flat(first_backward["widener"]), "rows", scatter_dimension=1, tiled=True),
        lax.psum_scatter(flat(first_backward["shortcut"]), "rows", scatter_dimension=1, tiled=True),
        lax.psum_scatter(
            flat(second_backward["squeezer"]), "rows", scatter_dimension=1, tiled=True
        ),
        lax.psum_scatter(
            flat(second_backward["condenser"]), "rows", scatter_dimension=1, tiled=True
        ),
        lax.psum_scatter(flat(second_backward["stencil"]), "rows", scatter_dimension=1, tiled=True),
        lax.psum_scatter(flat(second_backward["exciter"]), "rows", scatter_dimension=1, tiled=True),
        lax.psum_scatter(
            flat(second_backward["temporal"]), "rows", scatter_dimension=1, tiled=True
        ),
        lax.psum_scatter(flat(second_backward["kernels"]), "rows", scatter_dimension=1, tiled=True),
        lax.psum_scatter(
            flat(second_backward["restorer"]), "rows", scatter_dimension=1, tiled=True
        ),
    )
    totals = lax.psum(
        (
            pieces[0],
            pieces[1],
            pieces[2],
            pieces[3],
            pieces[4],
            pieces[5],
            pieces[6],
            pieces[7],
            pieces[8],
            pieces[9],
            pieces[10],
        ),
        "frames",
    )
    grad_scaling = jnp.stack(
        [
            first_backward["scales"][0],
            first_backward["scales"][1],
            second_backward["scales"][0],
            second_backward["scales"][1],
        ]
    )
    grad_biasing = jnp.stack(
        [
            first_backward["offsets"][0],
            first_backward["offsets"][1],
            second_backward["offsets"][0],
            second_backward["offsets"][1],
        ]
    )
    grad_amplitudes = jnp.stack(
        [first_backward["amps"][0], first_backward["amps"][1], second_backward["amp"]]
    )
    baseline_gradient = jnp.stack(
        [first_backward["bases"][0], first_backward["bases"][1], second_backward["base"]]
    )
    return (
        second["output"],
        first_backward["input"],
        unflat(totals[0], opening_reducer),
        unflat(totals[1], downsampling_filter),
        unflat(totals[2], opening_expander),
        unflat(totals[3], skip_projection),
        unflat(totals[4], closing_reducer),
        unflat(totals[5], excite_reducer),
        unflat(totals[6], excite_spatial_filter),
        unflat(totals[7], excite_expander),
        unflat(totals[8], time_taps),
        unflat(totals[9], spatial_filters),
        unflat(totals[10], closing_expander),
        grad_scaling,
        grad_biasing,
        grad_amplitudes,
        baseline_gradient,
    )


def solution(mesh):
    return jax.shard_map(
        shards,
        mesh=mesh,
        in_specs=(
            P("frames", "rows", None, None),
            P("frames"),
            P("frames"),
            P(),
            P(),
            P(),
            P(),
            P(),
            P(),
            P(),
            P(),
            P(),
            P(),
            P(),
            P(),
            P(),
            P(),
            P(),
            P("frames", "rows", None, None),
        ),
        out_specs=(
            P("frames", "rows", None, None),
            P("frames", "rows", None, None),
            P(None, "rows"),
            P(None, None, None, "rows"),
            P(None, "rows"),
            P(None, "rows"),
            P(None, "rows"),
            P(None, "rows"),
            P(None, None, None, "rows"),
            P(None, "rows"),
            P(None, "rows"),
            P(None, None, None, None, "rows"),
            P(None, "rows"),
            P(),
            P(),
            P(),
            P(),
        ),
        check_vma=False,
    )
```

```python
import math
from types import SimpleNamespace

import jax
import jax.numpy as jnp
from jax import lax
from jax.experimental import pallas as pl
from jax.experimental.pallas import tpu as pltpu
from jax.sharding import PartitionSpec as P

HIGHEST = lax.Precision.HIGH
MESH = pl.DeviceIdType.MESH
EPSILON = 1e-05
LAYOUT = ("NHWC", "HWIO", "NHWC")


def with_halo(block, sides, width):
    for axis, dim in sides:
        count = lax.axis_size(axis)
        forward = [(i, i + 1) for i in range(count - 1)]
        backward = [(target, source) for source, target in forward]
        low = lax.ppermute(
            lax.slice_in_dim(block, block.shape[dim] - width, None, axis=dim), axis, forward
        )
        high = lax.ppermute(lax.slice_in_dim(block, 0, width, axis=dim), axis, backward)
        block = jnp.concatenate([low, block, high], axis=dim)
    return block


def from_behind(block, axis, distance):
    devices = range(lax.axis_size(axis))
    route = [(i - distance, i) for i in devices if i - distance in devices]
    return lax.ppermute(block, axis, route)


def logistic_squash(value):
    return value * jax.nn.sigmoid(value)


def unit_slope(value):
    logistic = jax.nn.sigmoid(value)
    return logistic * (1.0 + value * (1.0 - logistic))


def pointwise_mapping(active, matrix):
    return jnp.einsum("fhwc,cd->fhwd", active, matrix, precision=HIGHEST)


def project_back(grads, matrix):
    return jnp.einsum("fhwd,cd->fhwc", grads, matrix, precision=HIGHEST)


def outer_sum(active, grads):
    return jnp.einsum("fhwc,fhwd->cd", active, grads, precision=HIGHEST)


def conv_valid(padded, kernel):
    return lax.conv_general_dilated(
        padded, kernel, (1, 1), ((0, 0), (1, 1)), dimension_numbers=LAYOUT, precision=HIGHEST
    )


def conv_stride(padded, kernel):
    return lax.conv_general_dilated(
        padded, kernel, (2, 2), ((0, 0), (1, 1)), dimension_numbers=LAYOUT, precision=HIGHEST
    )


def kernel_grad(padded, kernel, grads):
    result, pull_back = jax.vjp(lambda weights: conv_valid(padded, weights), kernel)
    return pull_back(grads)[0]


def flipped(kernel):
    return jnp.transpose(kernel[::-1, ::-1], (0, 1, 3, 2))


def row_padded(field):
    return with_halo(field, (("rows", 1),), 1)


def frame_padded(field):
    return with_halo(field, (("frames", 0),), 1)


def time_mix(padded, weights, earlier_boundary_filter, later_boundary_filter):
    return (
        weights[0] * earlier_boundary_filter * padded[:-2]
        + weights[1] * padded[1:-1]
        + weights[2] * later_boundary_filter * padded[2:]
    )


def exchange_slots(source, slots, send, recv, me, count, device):
    copies = []
    for step in range(1, count):
        copy = pltpu.make_async_remote_copy(
            src_ref=source,
            dst_ref=slots.at[me],
            send_sem=send.at[step],
            recv_sem=recv.at[me],
            device_id=device(lax.rem(me + step, count)),
            device_id_type=MESH,
        )
        copy.start()
        copies.append(copy)
    slots[me] = source[...]
    for step in range(1, count):
        origin = lax.rem(me + count - step, count)
        pltpu.make_async_remote_copy(
            src_ref=source,
            dst_ref=slots.at[origin],
            send_sem=send.at[step],
            recv_sem=recv.at[origin],
            device_id=device(origin),
            device_id_type=MESH,
        ).wait_recv()
    for copy in copies:
        copy.wait_send()
    total = slots[0]
    for place in range(1, count):
        total = total + slots[place]
    return total


def sum_kernel(frames, rows, x_ref, o_ref, part, row_slots, frame_slots, rs, rr, fs, fr):
    f = lax.axis_index("frames")
    r = lax.axis_index("rows")
    barrier = pltpu.get_barrier_semaphore()
    for step in range(1, rows):
        pl.semaphore_signal(
            barrier, inc=1, device_id=(f, lax.rem(r + step, rows)), device_id_type=MESH
        )
    for step in range(1, frames):
        pl.semaphore_signal(
            barrier, inc=1, device_id=(lax.rem(f + step, frames), r), device_id_type=MESH
        )
    pl.semaphore_wait(barrier, rows + frames - 2)
    part[...] = exchange_slots(x_ref, row_slots, rs, rr, r, rows, lambda place: (f, place))
    o_ref[...] = exchange_slots(part, frame_slots, fs, fr, f, frames, lambda place: (place, r))


def global_sum(pieces, call):
    frames, rows = lax.axis_size("frames"), lax.axis_size("rows")
    sizes = [piece.size // 128 for piece in pieces]
    block = jnp.concatenate([piece.reshape(-1, 128) for piece in pieces], 0)
    total = pl.pallas_call(
        lambda *refs: sum_kernel(frames, rows, *refs),
        out_shape=jax.ShapeDtypeStruct(block.shape, jnp.float32),
        in_specs=[pl.BlockSpec(memory_space=pltpu.VMEM)],
        out_specs=pl.BlockSpec(memory_space=pltpu.VMEM),
        scratch_shapes=[
            pltpu.VMEM(block.shape, jnp.float32),
            pltpu.VMEM((rows,) + block.shape, jnp.float32),
            pltpu.VMEM((frames,) + block.shape, jnp.float32),
            pltpu.SemaphoreType.DMA((rows,)),
            pltpu.SemaphoreType.DMA((rows,)),
            pltpu.SemaphoreType.DMA((frames,)),
            pltpu.SemaphoreType.DMA((frames,)),
        ],
        compiler_params=pltpu.CompilerParams(collective_id=call, has_side_effects=True),
    )(block)
    results = []
    start = 0
    for piece, size in zip(pieces, sizes):
        results.append(total[start : start + size].reshape(piece.shape))
        start += size
    return results


def add_rows(target, source, rows, target_columns=None):
    step = 8
    while rows % (2 * step) == 0 and 2 * step * source.shape[-1] <= 32768:
        step *= 2

    @pl.loop(0, rows // step)
    def _(place):
        spot = pl.ds(pl.multiple_of(place * step, step), step)
        if target_columns is None:
            target[spot, :] = target[spot, :] + source[spot, :]
        else:
            target[spot, target_columns] = target[spot, target_columns] + source[spot, :]


def gradient_item(grad, out, bufs, send, recv, place):
    own, from_core, first_p, first_q, second_p, second_q, third, fourth, final = bufs
    a_count, b_count, rows, columns = own.shape
    half, quarter = columns // 2, columns // 4
    ia, ib, c, r = place
    f = (ia * b_count + ib) * 2 + c
    low, high = pl.ds(0, half), pl.ds(half, half)
    flip1 = r + 1 - 2 * lax.rem(r, 2)
    flip2 = lax.rem(r + 2, 4)
    pending = []
    used = [0]

    def remote(source, target, device):
        copy = pltpu.make_async_remote_copy(
            src_ref=source,
            dst_ref=target,
            send_sem=send.at[used[0]],
            recv_sem=recv.at[used[0]],
            device_id=device,
            device_id_type=MESH,
        )
        used[0] += 1
        copy.start()
        pending.append(copy)
        return copy

    def a_peer(step):
        other = lax.rem(ia + step, a_count)
        return other, ((other * b_count + ib) * 2 + c, r)

    def b_peer(step):
        other = lax.rem(ib + step, b_count)
        return other, ((ia * b_count + other) * 2 + c, r)

    core = (f + 1 - 2 * c, r)
    local = pltpu.make_async_copy(grad.at[:, :, c], own, recv.at[used[0]])
    used[0] += 1
    local.start()
    waits = [remote(grad.at[:, :, 1 - c], from_core, core)]
    yield
    local.wait()
    waits[0].wait_recv()
    for i in range(a_count):
        for j in range(b_count):
            add_rows(own.at[i, j], from_core.at[i, j], rows)
    waits = []
    for step in range(1, b_count):
        other, device = b_peer(step)
        waits.append(remote(own.at[:, other, :, low], first_p.at[step - 1], device))
    for step in range(1, a_count):
        other, device = a_peer(step)
        waits.append(remote(own.at[other, :, :, high], first_q.at[step - 1], device))
    yield
    for copy in waits:
        copy.wait_recv()
    for step in range(1, b_count):
        for i in range(a_count):
            add_rows(own.at[i, ib, :, low], first_p.at[step - 1, i], rows)
    for step in range(1, a_count):
        for j in range(b_count):
            add_rows(own.at[ia, j, :, high], first_q.at[step - 1, j], rows)
    waits = []
    for step in range(1, a_count):
        other, device = a_peer(step)
        waits.append(remote(own.at[other, ib, :, low], second_p.at[step - 1], device))
    for step in range(1, b_count):
        other, device = b_peer(step)
        waits.append(remote(own.at[ia, other, :, high], second_q.at[step - 1], device))
    yield
    for copy in waits:
        copy.wait_recv()
    mine = own.at[ia, ib]
    for step in range(1, a_count):
        add_rows(mine.at[:, low], second_p.at[step - 1], rows)
    for step in range(1, b_count):
        add_rows(mine.at[:, high], second_q.at[step - 1], rows)

    def part(index):
        return pl.ds(pl.multiple_of(index * quarter, quarter), quarter)

    waits = []
    for k in range(2):
        waits.append(remote(mine.at[:, part(lax.rem(flip1, 2) + 2 * k)], third.at[k], (f, flip1)))
    yield
    for copy in waits:
        copy.wait_recv()
    for k in range(2):
        add_rows(mine, third.at[k], rows, part(lax.rem(r, 2) + 2 * k))
    waits = [remote(mine.at[:, part(flip2)], fourth, (f, flip2))]
    yield
    waits[0].wait_recv()
    add_rows(mine, fourth, rows, part(r))
    piece = mine.at[:, part(r)]
    cut = rows // 2 if rows % 16 == 0 else rows
    first, second = pl.ds(0, cut), pl.ds(cut, rows - cut)
    local = pltpu.make_async_copy(piece, out.at[ia, ib, c], recv.at[used[0]])
    used[0] += 1
    local.start()
    waits = []
    for step in range(1, b_count):
        other, device = b_peer(step)
        waits.append(remote(piece.at[first], out.at[ia, ib, c, first], device))
    if cut < rows:
        for step in range(1, a_count):
            other, device = a_peer(step)
            waits.append(remote(piece.at[second], out.at[ia, ib, c, second], device))
    yield
    local.wait()
    for copy in waits:
        copy.wait_recv()
    waits = []
    for step in range(1, a_count):
        other, device = a_peer(step)
        waits.append(remote(out.at[ia, :, c, first], out.at[ia, :, c, first], device))
    if cut < rows:
        for step in range(1, b_count):
            other, device = b_peer(step)
            waits.append(remote(out.at[:, ib, c, second], out.at[:, ib, c, second], device))
    yield
    for copy in waits:
        copy.wait_recv()
    waits = [remote(out.at[:, :, c], out.at[:, :, c], core)]
    yield
    waits[0].wait_recv()
    for copy in pending:
        copy.wait_send()


def gradient_kernel(splits, counts, *refs):
    a_count, b_count = counts
    grads, refs = refs[: len(splits)], refs[len(splits) :]
    outs, refs = refs[: len(splits)], refs[len(splits) :]
    f = lax.axis_index("frames")
    r = lax.axis_index("rows")
    c = lax.rem(f, 2)
    ib = lax.rem(f // 2, b_count)
    ia = f // (2 * b_count)
    partners = [
        (f + 1 - 2 * c, r),
        (f, r + 1 - 2 * lax.rem(r, 2)),
        (f, lax.rem(r + 2, 4)),
    ]
    for step in range(1, b_count):
        partners.append(((ia * b_count + lax.rem(ib + step, b_count)) * 2 + c, r))
    for step in range(1, a_count):
        partners.append(((lax.rem(ia + step, a_count) * b_count + ib) * 2 + c, r))
    barrier = pltpu.get_barrier_semaphore()
    for partner in partners:
        pl.semaphore_signal(barrier, inc=1, device_id=partner, device_id_type=MESH)
    pl.semaphore_wait(barrier, len(partners))
    waiting = []
    for index, split in enumerate(splits):
        for k in range(split):
            bufs, refs = refs[:9], refs[9:]
            send, recv, refs = refs[0], refs[1], refs[2:]
            waiting.append(
                gradient_item(
                    grads[index].at[k], outs[index].at[k], bufs, send, recv, (ia, ib, c, r)
                )
            )
    active = []
    while waiting or active:
        running = []
        for item in active:
            if next(item, active) is None:
                running.append(item)
        if waiting:
            item = waiting.pop(0)
            next(item)
            running.append(item)
        active = running


def sum_gradients(grads, call):
    frames = lax.axis_size("frames")
    levels = int(math.log2(frames // 2))
    b_count = 2 ** (levels // 2)
    a_count = frames // 2 // b_count
    operands, results, scratch = [], [], []
    copies = 8 + 2 * (a_count - 1) * 2 + 2 * (b_count - 1) * 2
    for grad, split in grads:
        depth, columns = grad.shape
        rows = depth // (split * frames)
        operands.append(grad.reshape(split, a_count, b_count, 2, rows, columns))
        results.append(
            jax.ShapeDtypeStruct((split, a_count, b_count, 2, rows, columns // 4), jnp.float32)
        )
        for _ in range(split):
            for shape in (
                (a_count, b_count, rows, columns),
                (a_count, b_count, rows, columns),
                (b_count - 1, a_count, rows, columns // 2),
                (a_count - 1, b_count, rows, columns // 2),
                (a_count - 1, rows, columns // 2),
                (b_count - 1, rows, columns // 2),
                (2, rows, columns // 4),
                (rows, columns // 4),
                (8, 128),
            ):
                scratch.append(pltpu.VMEM(shape, jnp.float32))
            scratch += [pltpu.SemaphoreType.DMA((copies,)), pltpu.SemaphoreType.DMA((copies,))]
    splits = [split for _, split in grads]
    totals = pl.pallas_call(
        lambda *refs: gradient_kernel(splits, (a_count, b_count), *refs),
        out_shape=results,
        in_specs=[pl.BlockSpec(memory_space=pl.ANY)] * len(grads),
        out_specs=[pl.BlockSpec(memory_space=pl.ANY)] * len(grads),
        scratch_shapes=scratch,
        compiler_params=pltpu.CompilerParams(
            collective_id=call, has_side_effects=True, vmem_limit_bytes=60 * 2**20
        ),
    )(*operands)
    return [
        total.reshape(grad.shape[0], grad.shape[1] // 4)
        for total, (grad, _) in zip(totals, grads)
    ]


def global_count(field):
    return (
        field.shape[0]
        * field.shape[1]
        * field.shape[2]
        * lax.axis_size("frames")
        * lax.axis_size("rows")
    )


def norm_forward(field, call):
    totals, squares = global_sum(
        (jnp.sum(field, axis=(0, 1, 2)), jnp.sum(field * field, axis=(0, 1, 2))), call
    )
    number = global_count(field)
    center = totals / number
    spread = lax.rsqrt(squares / number - center * center + EPSILON)
    return ((field - center) * spread, spread)


def norm_backward(grads, normed, spread, gain, call):
    bias_grad, gain_grad = global_sum(
        (jnp.sum(grads, axis=(0, 1, 2)), jnp.sum(grads * normed, axis=(0, 1, 2))), call
    )
    number = global_count(grads)
    field_grad = gain * spread * (grads - bias_grad / number - normed * (gain_grad / number))
    return (field_grad, gain_grad, bias_grad)


def layer_one(
    input_feature_maps,
    opening_reducer,
    downsampling_filter,
    opening_expander,
    skip_projection,
    narrow_norm_gains,
    narrow_norm_biases,
    wide_norm_gains,
    wide_norm_biases,
):
    normed_a, spread_a = norm_forward(pointwise_mapping(input_feature_maps, opening_reducer), 0)
    before_a = normed_a * narrow_norm_gains[0] + narrow_norm_biases[0]
    hidden_a = logistic_squash(before_a)
    upper_rim = from_behind(hidden_a[:, -1:], "rows", 1)
    padded_a = jnp.concatenate([upper_rim, hidden_a], 1)
    normed_b, spread_b = norm_forward(conv_stride(padded_a, downsampling_filter), 1)
    before_b = normed_b * narrow_norm_gains[1] + narrow_norm_biases[1]
    hidden_b = logistic_squash(before_b)
    standardized_current, spread_c = norm_forward(pointwise_mapping(hidden_b, opening_expander), 2)
    sampled = input_feature_maps[:, ::2, ::2]
    standardized_prior, spread_p = norm_forward(pointwise_mapping(sampled, skip_projection), 3)
    accumulated_total = (
        standardized_current * wide_norm_gains[0]
        + wide_norm_biases[0]
        + (standardized_prior * wide_norm_gains[1] + wide_norm_biases[1])
    )
    return SimpleNamespace(
        normed_a=normed_a,
        spread_a=spread_a,
        before_a=before_a,
        padded_a=padded_a,
        normed_b=normed_b,
        spread_b=spread_b,
        before_b=before_b,
        hidden_b=hidden_b,
        normed_c=standardized_current,
        spread_c=spread_c,
        sampled=sampled,
        normed_p=standardized_prior,
        spread_p=spread_p,
        summed=accumulated_total,
        output=logistic_squash(accumulated_total),
    )


def layer_one_back(
    kept,
    out_grad,
    input_feature_maps,
    opening_reducer,
    downsampling_filter,
    opening_expander,
    skip_projection,
    narrow_norm_gains,
    wide_norm_gains,
):
    total_grad = out_grad * unit_slope(kept.summed)
    grad_c, amp_c, base_c = norm_backward(
        total_grad, kept.normed_c, kept.spread_c, wide_norm_gains[0], 7)
    grad_p, amp_p, base_p = norm_backward(
        total_grad, kept.normed_p, kept.spread_p, wide_norm_gains[1], 8)
    grad_widener = outer_sum(kept.hidden_b, grad_c)
    grad_shortcut = outer_sum(kept.sampled, grad_p)
    before_b_grad = project_back(grad_c, opening_expander) * unit_slope(kept.before_b)
    grad_b, scale_b, offset_b = norm_backward(
        before_b_grad, kept.normed_b, kept.spread_b, narrow_norm_gains[1], 9)
    strided, pull_stride = jax.vjp(conv_stride, kept.padded_a, downsampling_filter)
    padded_grad, grad_strider = pull_stride(grad_b)
    lower_rim = from_behind(padded_grad[:, 0:1], "rows", -1)
    hidden_grad = padded_grad[:, 1:] + jnp.concatenate(
        [jnp.zeros_like(padded_grad[:, 1:-1]), lower_rim], 1
    )
    before_a_grad = hidden_grad * unit_slope(kept.before_a)
    grad_a, scale_a, offset_a = norm_backward(
        before_a_grad, kept.normed_a, kept.spread_a, narrow_norm_gains[0], 10)
    grad_narrower = outer_sum(input_feature_maps, grad_a)
    sample_grad = project_back(grad_p, skip_projection)
    frame_count, row_count, column_count, channel_count = sample_grad.shape
    spread_out = jnp.pad(
        sample_grad[:, :, None, :, None, :], ((0, 0), (0, 0), (0, 1), (0, 0), (0, 1), (0, 0))
    )
    spread_out = spread_out.reshape(frame_count, 2 * row_count, 2 * column_count, channel_count)
    input_grad = project_back(grad_a, opening_reducer) + spread_out
    return SimpleNamespace(
        input=input_grad,
        narrower=grad_narrower,
        strider=grad_strider,
        widener=grad_widener,
        shortcut=grad_shortcut,
        scales=(scale_a, scale_b),
        offsets=(offset_a, offset_b),
        amps=(amp_c, amp_p),
        bases=(base_c, base_p),
    )


def layer_two(
    above_adjacent,
    closing_reducer,
    excite_reducer,
    excite_spatial_filter,
    excite_expander,
    time_taps,
    spatial_filters,
    closing_expander,
    narrow_norm_gains,
    narrow_norm_biases,
    wide_norm_gains,
    wide_norm_biases,
    earlier_boundary_filter,
    later_boundary_filter,
):
    normed_a, spread_a = norm_forward(pointwise_mapping(above_adjacent, closing_reducer), 4)
    before_a = normed_a * narrow_norm_gains[2] + narrow_norm_biases[2]
    hidden = logistic_squash(before_a)
    reduced = pointwise_mapping(hidden, excite_reducer)
    incoming = from_behind(reduced[0:1], "frames", -1)
    following = jnp.concatenate([reduced[1:], incoming], 0) * later_boundary_filter
    follow_pad = row_padded(following)
    motion = (conv_valid(follow_pad, excite_spatial_filter) - reduced) * later_boundary_filter
    area = motion.shape[1] * motion.shape[2] * lax.axis_size("rows")
    pooled = lax.psum(jnp.sum(motion, axis=(1, 2)), "rows") / area
    gating = jax.nn.sigmoid(jnp.dot(pooled, excite_expander, precision=HIGHEST))
    excited = hidden * (1.0 + gating[:, None, None, :])
    width = excited.shape[-1] // 4
    branches = [excited[..., :width]]
    source_pads = []
    mixed_pads = []
    for index in range(3):
        source = excited[..., (index + 1) * width : (index + 2) * width]
        if index > 0:
            source = source + branches[-1]
        source_pad = frame_padded(source)
        mixed = time_mix(
            source_pad,
            time_taps[:, index * width : (index + 1) * width],
            earlier_boundary_filter,
            later_boundary_filter,
        )
        mixed_pad = row_padded(mixed)
        branches.append(conv_valid(mixed_pad, spatial_filters[index]))
        source_pads.append(source_pad)
        mixed_pads.append(mixed_pad)
    normed_b, spread_b = norm_forward(jnp.concatenate(branches, -1), 5)
    before_b = normed_b * narrow_norm_gains[3] + narrow_norm_biases[3]
    logistic_outcomes = logistic_squash(before_b)
    standardized_current, spread_c = norm_forward(
        pointwise_mapping(logistic_outcomes, closing_expander), 6)
    accumulated_total = (
        standardized_current * wide_norm_gains[2] + wide_norm_biases[2] + above_adjacent
    )
    return SimpleNamespace(
        normed_a=normed_a,
        spread_a=spread_a,
        before_a=before_a,
        hidden=hidden,
        reduced=reduced,
        follow_pad=follow_pad,
        pooled=pooled,
        gating=gating,
        source_pads=source_pads,
        mixed_pads=mixed_pads,
        normed_b=normed_b,
        spread_b=spread_b,
        before_b=before_b,
        squashed=logistic_outcomes,
        normed_c=standardized_current,
        spread_c=spread_c,
        summed=accumulated_total,
        output=logistic_squash(accumulated_total),
    )


def layer_two_back(
    kept,
    out_grad,
    above_adjacent,
    closing_reducer,
    excite_reducer,
    excite_spatial_filter,
    excite_expander,
    time_taps,
    spatial_filters,
    closing_expander,
    narrow_norm_gains,
    wide_norm_gains,
    earlier_boundary_filter,
    later_boundary_filter,
):
    total_grad = out_grad * unit_slope(kept.summed)
    grad_c, amp_c, base_c = norm_backward(
        total_grad, kept.normed_c, kept.spread_c, wide_norm_gains[2], 11)
    grad_restorer = outer_sum(kept.squashed, grad_c)
    before_b_grad = project_back(grad_c, closing_expander) * unit_slope(kept.before_b)
    merged_grad, scale_b, offset_b = norm_backward(
        before_b_grad, kept.normed_b, kept.spread_b, narrow_norm_gains[3], 12)
    width = merged_grad.shape[-1] // 4
    group_grads = [merged_grad[..., :width], None, None, None]
    kernel_grads = [None, None, None]
    tap_grads = [None, None, None]
    carried = jnp.zeros_like(merged_grad[..., :width])
    for index in (2, 1, 0):
        branch_grad = merged_grad[..., (index + 1) * width : (index + 2) * width] + carried
        kernel_grads[index] = kernel_grad(
            kept.mixed_pads[index], spatial_filters[index], branch_grad
        )
        mixed_grad = conv_valid(row_padded(branch_grad), flipped(spatial_filters[index]))
        source_pad = kept.source_pads[index]
        tap_grads[index] = jnp.stack(
            [
                jnp.sum(mixed_grad * earlier_boundary_filter * source_pad[:-2], axis=(0, 1, 2)),
                jnp.sum(mixed_grad * source_pad[1:-1], axis=(0, 1, 2)),
                jnp.sum(mixed_grad * later_boundary_filter * source_pad[2:], axis=(0, 1, 2)),
            ]
        )
        group_taps = time_taps[:, index * width : (index + 1) * width]
        carried = time_mix(
            frame_padded(mixed_grad),
            group_taps[::-1],
            earlier_boundary_filter,
            later_boundary_filter,
        )
        group_grads[index + 1] = carried
    excited_grad = jnp.concatenate(group_grads, -1)
    gating = kept.gating
    hidden = kept.hidden
    hidden_grad = excited_grad * (1.0 + gating[:, None, None, :])
    gate_part = jnp.sum(excited_grad * hidden, axis=(1, 2)) * gating * (1.0 - gating)
    grad_exciter = jnp.dot(kept.pooled.T, gate_part, precision=HIGHEST)
    logit_grad = lax.psum(gate_part, "rows")
    reduced = kept.reduced
    area = reduced.shape[1] * reduced.shape[2] * lax.axis_size("rows")
    pooled_grad = jnp.dot(logit_grad, excite_expander.T, precision=HIGHEST) / area
    motion_grad = jnp.broadcast_to(
        pooled_grad[:, None, None, :] * later_boundary_filter, reduced.shape
    )
    grad_stencil = kernel_grad(kept.follow_pad, excite_spatial_filter, motion_grad)
    follow_grad = (
        conv_valid(row_padded(motion_grad), flipped(excite_spatial_filter)) * later_boundary_filter
    )
    outgoing = from_behind(follow_grad[-1:], "frames", 1)
    reduced_grad = jnp.concatenate([outgoing, follow_grad[:-1]], 0) - motion_grad
    grad_condenser = outer_sum(hidden, reduced_grad)
    hidden_grad = hidden_grad + project_back(reduced_grad, excite_reducer)
    before_a_grad = hidden_grad * unit_slope(kept.before_a)
    grad_a, scale_a, offset_a = norm_backward(
        before_a_grad, kept.normed_a, kept.spread_a, narrow_norm_gains[2], 13)
    grad_squeezer = outer_sum(above_adjacent, grad_a)
    upper_grad = total_grad + project_back(grad_a, closing_reducer)
    return SimpleNamespace(
        upper=upper_grad,
        squeezer=grad_squeezer,
        condenser=grad_condenser,
        stencil=grad_stencil,
        exciter=grad_exciter,
        temporal=jnp.concatenate(tap_grads, 1),
        kernels=jnp.stack(kernel_grads),
        restorer=grad_restorer,
        scales=(scale_a, scale_b),
        offsets=(offset_a, offset_b),
        amp=amp_c,
        base=base_c,
    )


def flat(matrix):
    return matrix.reshape(-1, matrix.shape[-1])


def by_column(matrix):
    pieces = matrix.reshape(matrix.shape[0], 4, -1).transpose(1, 0, 2)
    return pieces.reshape(4, -1, 128).transpose(1, 0, 2).reshape(-1, 512)


def unflat(piece, model):
    return piece.reshape(model.shape[:-1] + (piece.shape[-1],))


def shards(
    input_feature_maps,
    sequence_slot_lookup,
    sequence_span_lookup,
    opening_reducer,
    downsampling_filter,
    opening_expander,
    skip_projection,
    closing_reducer,
    excite_reducer,
    excite_spatial_filter,
    excite_expander,
    time_taps,
    spatial_filters,
    closing_expander,
    narrow_norm_gains,
    narrow_norm_biases,
    wide_norm_gains,
    wide_norm_biases,
    loss_slope_wrt_final,
):
    opening_reducer = opening_reducer.astype(jnp.float32)
    downsampling_filter = downsampling_filter.astype(jnp.float32)
    opening_expander = opening_expander.astype(jnp.float32)
    skip_projection = skip_projection.astype(jnp.float32)
    closing_reducer = closing_reducer.astype(jnp.float32)
    excite_reducer = excite_reducer.astype(jnp.float32)
    excite_spatial_filter = excite_spatial_filter.astype(jnp.float32)
    excite_expander = excite_expander.astype(jnp.float32)
    time_taps = time_taps.astype(jnp.float32)
    spatial_filters = spatial_filters.astype(jnp.float32)
    closing_expander = closing_expander.astype(jnp.float32)
    earlier_boundary_filter = (sequence_slot_lookup > 0).astype(jnp.float32)[:, None, None, None]
    later_boundary_filter = (sequence_slot_lookup < sequence_span_lookup - 1).astype(jnp.float32)[
        :, None, None, None
    ]
    first = layer_one(
        input_feature_maps,
        opening_reducer,
        downsampling_filter,
        opening_expander,
        skip_projection,
        narrow_norm_gains,
        narrow_norm_biases,
        wide_norm_gains,
        wide_norm_biases,
    )
    above_adjacent = first.output
    again, incoming_grad = above_adjacent, loss_slope_wrt_final
    second = layer_two(
        again,
        closing_reducer,
        excite_reducer,
        excite_spatial_filter,
        excite_expander,
        time_taps,
        spatial_filters,
        closing_expander,
        narrow_norm_gains,
        narrow_norm_biases,
        wide_norm_gains,
        wide_norm_biases,
        earlier_boundary_filter,
        later_boundary_filter,
    )
    second_backward = layer_two_back(
        second,
        incoming_grad,
        again,
        closing_reducer,
        excite_reducer,
        excite_spatial_filter,
        excite_expander,
        time_taps,
        spatial_filters,
        closing_expander,
        narrow_norm_gains,
        wide_norm_gains,
        earlier_boundary_filter,
        later_boundary_filter,
    )
    first_backward = layer_one_back(
        first,
        second_backward.upper,
        input_feature_maps,
        opening_reducer,
        downsampling_filter,
        opening_expander,
        skip_projection,
        narrow_norm_gains,
        wide_norm_gains,
    )
    kernels = second_backward.kernels.reshape(4, -1, 4, second_backward.kernels.shape[-1] // 4)
    packed = jnp.concatenate(
        [
            kernels.transpose(1, 2, 0, 3).reshape(kernels.shape[1], -1),
            by_column(second_backward.condenser),
            by_column(flat(second_backward.stencil)),
            by_column(second_backward.exciter),
            by_column(jnp.pad(second_backward.temporal.reshape(3, 4, -1), ((0, 0), (0, 0), (0, 32))).reshape(3, -1)),
        ],
        0,
    )
    packed = jnp.pad(packed, ((0, -packed.shape[0] % 128 if packed.shape[0] > 1024 else 1024 - packed.shape[0]), (0, 0)))
    totals = sum_gradients(
        (
            (first_backward.shortcut, 2),
            (flat(first_backward.strider), 3),
            (first_backward.widener, 1),
            (second_backward.restorer, 1),
            (second_backward.squeezer, 1),
            (first_backward.narrower, 1),
            (packed, 1),
        ),
        14,
    )
    tail = totals[6]
    start = kernels.shape[1]
    grad_kernels = tail[:start].reshape(start, 4, -1).transpose(1, 0, 2).reshape(spatial_filters.shape[:-1] + (-1,))
    grad_condenser = tail[start : start + 32].reshape(excite_reducer.shape[0], -1)
    grad_stencil = tail[start + 32 : start + 50].reshape(excite_spatial_filter.shape[:-1] + (-1,))
    grad_exciter = tail[start + 50 : start + 82]
    grad_temporal = tail[start + 82 : start + 85, :96]
    grad_scaling = jnp.stack(
        [
            first_backward.scales[0],
            first_backward.scales[1],
            second_backward.scales[0],
            second_backward.scales[1],
        ]
    )
    grad_biasing = jnp.stack(
        [
            first_backward.offsets[0],
            first_backward.offsets[1],
            second_backward.offsets[0],
            second_backward.offsets[1],
        ]
    )
    grad_amplitudes = jnp.stack(
        [first_backward.amps[0], first_backward.amps[1], second_backward.amp]
    )
    baseline_gradient = jnp.stack(
        [first_backward.bases[0], first_backward.bases[1], second_backward.base]
    )
    return (
        second.output,
        first_backward.input,
        totals[5],
        unflat(totals[1], downsampling_filter),
        totals[2],
        totals[0],
        totals[4],
        grad_condenser,
        grad_stencil,
        grad_exciter,
        grad_temporal,
        grad_kernels,
        totals[3],
        grad_scaling,
        grad_biasing,
        grad_amplitudes,
        baseline_gradient,
    )


def solution(mesh):
    return jax.shard_map(
        shards,
        mesh=mesh,
        in_specs=(
            P("frames", "rows", None, None),
            P("frames"),
            P("frames"),
            P(),
            P(),
            P(),
            P(),
            P(),
            P(),
            P(),
            P(),
            P(),
            P(),
            P(),
            P(),
            P(),
            P(),
            P(),
            P("frames", "rows", None, None),
        ),
        out_specs=(
            P("frames", "rows", None, None),
            P("frames", "rows", None, None),
            P(None, "rows"),
            P(None, None, None, "rows"),
            P(None, "rows"),
            P(None, "rows"),
            P(None, "rows"),
            P(None, "rows"),
            P(None, None, None, "rows"),
            P(None, "rows"),
            P(None, "rows"),
            P(None, None, None, None, "rows"),
            P(None, "rows"),
            P(),
            P(),
            P(),
            P(),
        ),
        check_vma=False,
    )
```

```python
import math
from types import SimpleNamespace

import jax
import jax.numpy as jnp
from jax import lax
from jax.experimental import pallas as pl
from jax.experimental.pallas import tpu as pltpu
from jax.sharding import PartitionSpec as P

MESH = pl.DeviceIdType.MESH
EPSILON = 1e-05


def split(value):
    high = value.astype(jnp.bfloat16)
    return high, (value - high.astype(jnp.float32)).astype(jnp.bfloat16)


def put(pair_ref, index, value):
    high, low = split(value)
    pair_ref[(0,) + index] = high
    pair_ref[(1,) + index] = low


def product(stacked, weights, turned=False):
    result = lax.dot_general(
        stacked,
        weights,
        (((1,), (1 if turned else 0,)), ((), ())),
        preferred_element_type=jnp.float32,
    )
    half = result.shape[0] // 2
    return result[:half] + result[half:]


def small_product(value, weights, turned=False):
    return product(jnp.concatenate(split(value), 0), weights, turned)


def small_outer(left, right):
    def one(a, b):
        return lax.dot_general(
            a, b, (((0,), (0,)), ((), ())), preferred_element_type=jnp.float32
        )

    (a, b), (c, d) = split(left), split(right)
    return one(a, c) + one(a, d) + one(b, c)


def slope(value):
    logistic = jax.nn.sigmoid(value)
    return logistic * (1.0 + value * (1.0 - logistic))


def silu(value):
    return value * jax.nn.sigmoid(value)


def folded(value):
    return jnp.sum(value.reshape(-1, 8, value.shape[-1]), axis=0)


def moved_down(value):
    place = lax.broadcasted_iota(jnp.int32, value.shape, 0)
    return jnp.where(lax.rem(place, 8) == 0, 0.0, pltpu.roll(value, 1, 0))


def moved_up(value):
    place = lax.broadcasted_iota(jnp.int32, value.shape, 0)
    return jnp.where(lax.rem(place, 8) == 7, 0.0, pltpu.roll(value, value.shape[0] - 1, 0))


def chunks(total, step):
    def bind(body):
        @pl.loop(0, total // step)
        def _(place):
            body(pl.ds(pl.multiple_of(place * step, step), step))

    return bind


def chain_kernel(names, dims, *refs):
    frames, rows, depth = dims
    m = SimpleNamespace(**dict(zip(names, refs)))
    f = lax.axis_index("frames")
    r = lax.axis_index("rows")
    after_f, before_f = lax.rem(f + 1, frames), lax.rem(f + frames - 1, frames)
    band = depth * 8
    half = 2 * band
    number_half = float(half * frames * rows)
    number_full = 4.0 * number_half
    above, below = r > 0, r < rows - 1
    above_one, below_one = jnp.where(above, 1.0, 0.0), jnp.where(below, 1.0, 0.0)
    wide = 2048

    loads = []

    def load(source, target):
        copy = pltpu.make_async_copy(source, target, m.load_sem.at[len(loads)])
        copy.start()
        loads.append(copy)
        return copy

    lanes = [slice(k * 128, k * 128 + 128) for k in range(8)]

    def load_row(row):
        return [
            load(m.x.at[:, row, :, lane], m.xs.at[k, :, row]) for k, lane in enumerate(lanes)
        ]

    x_loads = [load_row(row) for row in (3, 0, 1, 2)]
    wn_load = load(m.wn_h, m.wn)
    wsk_load = load(m.wsk_h, m.wsk)
    ks_load = load(m.ks_h, m.ks)
    we_load = load(m.we_h, m.we)
    wcr_load = load(m.wcr_h, m.wcr)
    wce_load = load(m.wce_h, m.wce)
    kern_load = load(m.kern_h, m.kern)
    slope_loads = [load(m.slope_h.at[:, row], m.slope.at[row]) for row in range(2)]

    barrier = pltpu.get_barrier_semaphore()
    partners = [(f, lax.rem(r + step, rows)) for step in range(1, rows)]
    partners += [(lax.rem(f + step, frames), r) for step in range(1, frames)]
    for other in (after_f, before_f):
        partners += [(other, lax.rem(r + step, rows)) for step in range(1, rows)]
    for partner in partners:
        pl.semaphore_signal(barrier, inc=1, device_id=partner, device_id_type=MESH)
    pl.semaphore_wait(barrier, len(partners))

    sent = []

    def send(source, target, send_sem, recv_sem, device):
        copy = pltpu.make_async_remote_copy(
            src_ref=source,
            dst_ref=target,
            send_sem=send_sem,
            recv_sem=recv_sem,
            device_id=device,
            device_id_type=MESH,
        )
        copy.start()
        return copy

    class Sum:
        count = 0

        def __init__(self, pieces):
            self.set = Sum.count % 2
            Sum.count += 1
            place = 0
            for piece in pieces:
                for k in range(piece.shape[1] // 128):
                    m.ar_in[self.set, place : place + 1, :] = piece[:, k * 128 : k * 128 + 128]
                    place += 1
            self.size = -(-place // 8) * 8
            self.copies = self.spread(
                m.ar_in, m.ar_rows, m.ar_rs, m.ar_rr, r, rows, lambda other: (f, other)
            )

        def spread(self, source, slots, send_sem, recv_sem, me, count, device):
            piece = source.at[self.set, pl.ds(0, self.size)]
            copies = []
            for step in range(1, count):
                copies.append(
                    send(
                        piece,
                        slots.at[self.set, step, pl.ds(0, self.size)],
                        send_sem.at[self.set, step],
                        recv_sem.at[self.set, step],
                        device(lax.rem(me + step, count)),
                    )
                )
            return copies

        def gather(self, source, slots, me, count):
            for copy in self.copies:
                copy.wait_recv()
            slots[self.set, 0, : self.size] = source[self.set, : self.size]
            total = slots[self.set, me, : self.size]
            for other in range(1, count):
                spot = lax.rem(me + count - other, count)
                total = total + slots[self.set, spot, : self.size]
            return total

        def middle(self):
            first = self.copies
            m.ar_part[self.set, : self.size] = self.gather(m.ar_in, m.ar_rows, r, rows)
            self.copies = self.spread(
                m.ar_part, m.ar_frames, m.ar_fs, m.ar_fr, f, frames, lambda other: (other, r)
            )
            for copy in first:
                copy.wait_send()

        def finish(self, *sizes):
            m.ar_out[: self.size] = self.gather(m.ar_part, m.ar_frames, f, frames)
            for copy in self.copies:
                copy.wait_send()
            results, place = [], 0
            for size in sizes:
                parts = []
                for k in range(size // 128):
                    parts.append(m.ar_out[place : place + 1, :])
                    place += 1
                results.append(jnp.concatenate(parts, axis=1))
            return results

        def all(self, *sizes):
            self.middle()
            return self.finish(*sizes)

    def settle(k, totals, squares, number, gain, bias):
        size = totals.shape[1]
        center = totals / number
        spread = lax.rsqrt(squares / number - center * center + EPSILON)
        scale = spread * gain
        m.vec[6 * k : 6 * k + 1, :size] = center
        m.vec[6 * k + 1 : 6 * k + 2, :size] = spread
        m.vec[6 * k + 2 : 6 * k + 3, :size] = scale
        m.vec[6 * k + 3 : 6 * k + 4, :size] = bias - center * scale

    def settle_back(k, bias_grad, gain_grad, number):
        size = bias_grad.shape[1]
        m.vec[6 * k + 4 : 6 * k + 5, :size] = bias_grad / number
        m.vec[6 * k + 5 : 6 * k + 6, :size] = gain_grad / number

    def vec(k, which, cols=slice(0, 512)):
        return m.vec[6 * k + which : 6 * k + which + 1, cols]

    def affine(k, value, cols=slice(0, 512)):
        return value * vec(k, 2, cols) + vec(k, 3, cols)

    def normed(k, value, cols=slice(0, 512)):
        return (value - vec(k, 0, cols)) * vec(k, 1, cols)

    def field_grad(k, grads, value, cols=slice(0, 512)):
        return vec(k, 2, cols) * (
            grads - vec(k, 4, cols) - normed(k, value, cols) * vec(k, 5, cols)
        )

    def clear():
        m.stat[...] = jnp.zeros_like(m.stat)

    def collect(k, value, cols=slice(0, 512)):
        m.stat[k, :, cols] = m.stat[k, :, cols] + folded(value)

    def collected(k, size=512):
        return jnp.sum(m.stat[k, :, :size], axis=0, keepdims=True)

    def column_tiles(body):
        @pl.loop(0, wide // 512)
        def _(place):
            body(pl.ds(pl.multiple_of(place * 512, 512), 512))

    clear()

    @pl.when(r == 0)
    def _():
        m.a[0] = jnp.zeros(m.a.shape[1:], jnp.float32)

    @pl.when(r == rows - 1)
    def _():
        m.b_halo[...] = jnp.zeros_like(m.b_halo)
        m.back_halo[...] = jnp.zeros_like(m.back_halo)

    for buffers in (m.source, m.grad_pad):
        for k in range(3):

            @pl.when(r == 0)
            def _():
                buffers[k, 0] = jnp.zeros(buffers.shape[2:], jnp.float32)

            @pl.when(r == rows - 1)
            def _():
                buffers[k, 3] = jnp.zeros(buffers.shape[2:], jnp.float32)

    def reduce_row(row):
        @pl.loop(0, depth // 2)
        def _(pair):
            for parity in range(2):
                spot = pl.ds(parity, 8, stride=2)
                place = pl.multiple_of(row * half + parity * band + pair * 16, 16)
                for k, lane in enumerate(lanes):
                    value = jnp.concatenate(
                        [m.xs[k, 2 * pair, row, spot, :], m.xs[k, 2 * pair + 1, row, spot, :]], 0
                    )
                    put(m.xb, (pl.ds(place, 16), lane), value)

        place = pl.ds(pl.multiple_of(row * half, half), half)
        result = product(jnp.concatenate([m.xb[0, place, :], m.xb[1, place, :]], 0), m.wn[...])
        m.a[1 + row] = result.reshape(2, band, 512)
        collect(0, result)
        collect(1, result * result)

    for copy in x_loads[0]:
        copy.wait()
    wn_load.wait()
    reduce_row(3)

    @pl.when(below)
    def _():
        send(m.a.at[4], m.a.at[0], m.halo_s.at[0], m.halo_r.at[0], (f, r + 1))

    for copies in x_loads[1:]:
        for copy in copies:
            copy.wait()

    @pl.loop(0, 3)
    def _(row):
        reduce_row(row)

    total = Sum([collected(0), collected(1)])
    clear()
    wsk_load.wait()

    def shortcut_tile(cols):
        lhs = jnp.concatenate(
            [m.xb[k, pl.ds(row * half, band), :] for k in range(2) for row in (0, 2)], 0
        )
        result = product(lhs, m.wsk[:, cols])
        m.s[:, cols] = result
        collect(2, result, cols)
        collect(3, result * result, cols)

    @pl.loop(0, 2)
    def _(place):
        shortcut_tile(pl.ds(pl.multiple_of(place * 512, 512), 512))

    total.middle()

    @pl.loop(2, 4)
    def _(place):
        shortcut_tile(pl.ds(pl.multiple_of(place * 512, 512), 512))

    totals, squares = total.finish(512, 512)
    settle(0, totals, squares, number_full, m.gain[0:1], m.bias[0:1])

    def activate(row, keep):
        @chunks(band, 32)
        def _(spot):
            for parity in range(2):
                value = silu(affine(0, m.a[row, parity, spot, :]))
                if keep is not None:
                    value = value * keep
                if parity == 0:
                    put(m.pc, (row, spot, slice(512, 1024)), value)
                else:
                    put(m.pc, (row, spot, slice(1024, 1536)), value)
                    put(m.pc, (row, spot, slice(0, 512)), moved_down(value))

    @pl.loop(1, 5)
    def _(row):
        activate(row, None)

    @pl.when(above)
    def _():
        pltpu.make_async_remote_copy(
            src_ref=m.a.at[4],
            dst_ref=m.a.at[0],
            send_sem=m.halo_s.at[0],
            recv_sem=m.halo_r.at[0],
            device_id=(f, lax.rem(r + 1, rows)),
            device_id_type=MESH,
        ).wait_recv()

    activate(0, above_one)
    ks_load.wait()

    def strided(dy):
        return product(
            jnp.concatenate([m.pc[k, dy + 2 * i] for k in range(2) for i in range(2)], 0), m.ks[dy]
        )

    m.b[...] = strided(0)
    m.b[...] = m.b[...] + strided(1)
    result = m.b[...] + strided(2)
    m.b[...] = result
    collect(0, result)
    collect(1, result * result)

    @pl.when(above)
    def _():
        send(
            m.b.at[pl.ds(0, band)], m.b_halo, m.halo_s.at[1], m.halo_r.at[1], (f, r - 1)
        )

    totals, squares, totals_p, squares_p = Sum(
        [collected(0), collected(1), collected(2, wide), collected(3, wide)]
    ).all(512, 512, wide, wide)
    clear()
    settle(1, totals, squares, number_half, m.gain[1:2], m.bias[1:2])
    settle(5, totals_p, squares_p, number_half, m.wide_gain[1:2], m.wide_bias[1:2])

    @chunks(half, 32)
    def _(spot):
        put(m.h2, (spot, slice(None)), silu(affine(1, m.b[spot, :])))

    we_load.wait()

    @column_tiles
    def _(cols):
        result = product(jnp.concatenate([m.h2[0], m.h2[1]], 0), m.we[:, cols])
        m.c[:, cols] = result
        collect(0, result, cols)
        collect(1, result * result, cols)

    totals, squares = Sum([collected(0, wide), collected(1, wide)]).all(wide, wide)
    clear()
    settle(4, totals, squares, number_half, m.wide_gain[0:1], m.wide_bias[0:1])

    def first_sum(spot, cols):
        return affine(4, m.c[spot, cols], cols) + affine(5, m.s[spot, cols], cols)

    @column_tiles
    def _(cols):
        @chunks(half, 32)
        def _(spot):
            value = silu(first_sum(spot, cols))
            m.up[spot, cols] = value
            put(m.uh, (spot, cols), value)

    wcr_load.wait()
    result = product(jnp.concatenate([m.uh[0], m.uh[1]], 0), m.wcr[...])
    m.d[...] = result
    collect(0, result)
    collect(1, result * result)
    totals, squares = Sum([collected(0), collected(1)]).all(512, 512)
    clear()
    settle(2, totals, squares, number_half, m.gain[2:3], m.bias[2:3])

    @chunks(half, 32)
    def _(spot):
        m.hid[spot, :] = silu(affine(2, m.d[spot, :]))

    m.edge[...] = jnp.zeros_like(m.edge)
    for row in range(2):
        block = m.hid[row * band : row * band + band, :]
        column = lax.rem(lax.broadcasted_iota(jnp.int32, block.shape, 0), 8)
        for k, value in enumerate(
            (block, jnp.where(column == 0, block, 0.0), jnp.where(column == 7, block, 0.0))
        ):
            m.edge[k, row, :depth] = jnp.sum(value.reshape(depth, 8, 512), axis=1)
    pad = m.edge.shape[2]
    reduced = small_product(m.edge[...].reshape(6 * pad, 512), m.wer[...])

    def part(kind, row):
        start = (kind * 2 + row) * pad
        return reduced[start : start + pad]

    taps = []
    for dy in range(3):
        for dx in range(3):
            by_row = []
            for row in range(2):
                value = part(0, row)
                if dx == 0:
                    value = value - part(2, row)
                if dx == 2:
                    value = value - part(1, row)
                by_row.append(value)
            if dy == 0:
                by_row[1] = by_row[1] * below_one
            if dy == 2:
                by_row[0] = by_row[0] * above_one
            taps.append(by_row[0] + by_row[1])
    taps.append(jnp.zeros((pad, 96), jnp.float32))
    m.tap_in[...] = jnp.concatenate(taps, 1)

    def rows_sum(source, slots, near, near_slots, toward, sems):
        copies = []
        for step in range(1, rows):
            copies.append(
                send(
                    source,
                    slots.at[step],
                    m.rows_s.at[sems, step],
                    m.rows_r.at[sems, step],
                    (f, lax.rem(r + step, rows)),
                )
            )
        for step in range(rows):
            copies.append(
                send(
                    source.at[near],
                    near_slots.at[step],
                    m.rows_s.at[sems, rows + step],
                    m.rows_r.at[sems, rows + step],
                    (toward, lax.rem(r + step, rows)),
                )
            )
        slots[0] = source[...]
        for copy in copies:
            copy.wait_recv()
        total = slots[r]
        other_total = near_slots[r]
        for other in range(1, rows):
            spot = lax.rem(r + rows - other, rows)
            total = total + slots[spot]
            other_total = other_total + near_slots[spot]
        for copy in copies:
            copy.wait_send()
        return total, other_total

    current, later = rows_sum(
        m.tap_in, m.tap_slots, pl.ds(0, 8), m.tap_near, before_f, 0
    )
    place = lax.broadcasted_iota(jnp.int32, current.shape, 0)
    follow = pltpu.roll(current, pad - 1, 0)
    follow = jnp.where(place == depth - 1, later[0:1], follow)
    after16 = m.after16[...]
    before16 = m.before16[...]
    follow = jnp.where(place < depth, follow, 0.0) * jnp.concatenate([after16] * 3, 1)
    m.follow[...] = follow
    area = float(16 * rows)
    pooled = (
        (small_product(follow[:, :288], m.kst[...]) - current[:, 128:160])
        * after16[:, :32]
        / area
    )
    m.pooled[...] = pooled
    m.gate[...] = jax.nn.sigmoid(small_product(pooled, m.wex[...]))
    for frame in range(depth):
        m.gate_all[frame * 8 : frame * 8 + 8, :] = jnp.broadcast_to(
            1.0 + m.gate[frame : frame + 1, :], (8, 512)
        )

    def halo(field, sems):
        own, first, last = pl.ds(8, band), pl.ds(8, 8), pl.ds(band, 8)
        low, high = pl.ds(0, 8), pl.ds(band + 8, 8)
        moves = [
            (field.at[pl.ds(1, 2), last], field.at[pl.ds(1, 2), low], (after_f, r), None, None),
            (field.at[pl.ds(1, 2), first], field.at[pl.ds(1, 2), high], (before_f, r), None, None),
            (field.at[2, own], field.at[0, own], (f, r + 1), below, above),
            (field.at[1, own], field.at[3, own], (f, r - 1), above, below),
            (field.at[2, last], field.at[0, low], (after_f, r + 1), below, above),
            (field.at[1, last], field.at[3, low], (after_f, r - 1), above, below),
            (field.at[2, first], field.at[0, high], (before_f, r + 1), below, above),
            (field.at[1, first], field.at[3, high], (before_f, r - 1), above, below),
        ]
        copies = []
        for k, (source, target, device, able, arriving) in enumerate(moves):
            copies.append(
                pltpu.make_async_remote_copy(
                    src_ref=source,
                    dst_ref=target,
                    send_sem=m.ring_s.at[sems, k],
                    recv_sem=m.ring_r.at[sems, k],
                    device_id=device,
                    device_id_type=MESH,
                )
            )
        for copy, move in zip(copies, moves):
            if move[3] is None:
                copy.start()
            else:
                pl.when(move[3])(copy.start)
        for copy, move in zip(copies, moves):
            if move[4] is None:
                copy.wait_recv()
            else:
                pl.when(move[4])(copy.wait_recv)
        for copy, move in zip(copies, moves):
            if move[3] is None:
                copy.wait_send()
            else:
                pl.when(move[3])(copy.wait_send)

    own = pl.ds(8, band)
    previous, following = pl.ds(0, band), pl.ds(16, band)
    before_band = m.before_band[...]
    after_band = m.after_band[...]

    def sides(value):
        return jnp.concatenate([moved_down(value), value, moved_up(value)], 1)

    m.merged[:, 0:128] = jnp.concatenate(
        [m.hid[i * band : i * band + band, 0:128] * m.gate_all[:, 0:128] for i in range(2)], 0
    )
    kern_load.wait()
    for k in range(3):
        cols = slice((k + 1) * 128, (k + 2) * 128)
        for i in range(2):
            rows_i = slice(i * band, i * band + band)
            value = m.hid[rows_i, cols] * m.gate_all[:, cols]
            if k > 0:
                value = value + m.merged[rows_i, k * 128 : (k + 1) * 128]
            m.source[k, 1 + i, own] = value
        halo(m.source.at[k], k)
        tap = [m.taps[i : i + 1, k * 128 : (k + 1) * 128] for i in range(3)]
        for i in range(4):
            mixed = (
                tap[0] * before_band * m.source[k, i, previous]
                + tap[1] * m.source[k, i, own]
                + tap[2] * after_band * m.source[k, i, following]
            )
            put(m.mixed, (k, i), sides(mixed))
        result = jnp.zeros((half, 128), jnp.float32)
        for dy in range(3):
            lhs = jnp.concatenate([m.mixed[p, k, i + dy] for p in range(2) for i in range(2)], 0)
            result = result + product(lhs, m.kern[k, dy])
        m.merged[:, cols] = result

    result = m.merged[...]
    collect(0, result)
    collect(1, result * result)
    totals, squares = Sum([collected(0), collected(1)]).all(512, 512)
    clear()
    settle(3, totals, squares, number_half, m.gain[3:4], m.bias[3:4])

    @chunks(half, 32)
    def _(spot):
        put(m.squashed, (spot, slice(None)), silu(affine(3, m.merged[spot, :])))

    wce_load.wait()

    @column_tiles
    def _(cols):
        result = product(jnp.concatenate([m.squashed[0], m.squashed[1]], 0), m.wce[:, cols])
        m.e[:, cols] = result
        collect(0, result, cols)
        collect(1, result * result, cols)

    totals, squares = Sum([collected(0, wide), collected(1, wide)]).all(wide, wide)
    clear()
    settle(6, totals, squares, number_half, m.wide_gain[2:3], m.wide_bias[2:3])

    for copy in slope_loads:
        copy.wait()

    @column_tiles
    def _(cols):
        for row in range(2):

            @pl.loop(0, depth // 4)
            def _(part_place):
                block = pl.ds(pl.multiple_of(part_place * 4, 4), 4)
                spot = pl.ds(pl.multiple_of(row * band + part_place * 32, 32), 32)
                raw = m.e[spot, cols]
                value = affine(6, raw, cols) + m.up[spot, cols]
                logistic = jax.nn.sigmoid(value)
                m.out[row, block, :, cols] = (value * logistic).reshape(4, 8, 512)
                grads = m.slope[row, block, :, cols].reshape(32, 512) * (
                    logistic * (1.0 + value * (1.0 - logistic))
                )
                m.d2[spot, cols] = grads
                collect(0, grads, cols)
                collect(1, grads * normed(6, raw, cols), cols)

    stores = []

    def store(source, target):
        copy = pltpu.make_async_copy(source, target, m.store_sem.at[len(stores)])
        copy.start()
        stores.append(copy)

    for row in range(2):
        store(m.out.at[row], m.layer_output.at[:, row])
    store(m.xb, m.xb_h)
    store(m.pc, m.pc_h)
    store(m.h2, m.h2_h)
    store(m.uh, m.uh_h)
    store(m.squashed, m.squashed_h)
    store(m.mixed, m.mixed_h)

    bias_grad, gain_grad = Sum([collected(0, wide), collected(1, wide)]).all(wide, wide)
    clear()
    settle_back(6, bias_grad, gain_grad, number_half)
    m.baselines[2:3] = bias_grad
    m.amplitudes[2:3] = gain_grad

    @column_tiles
    def _(cols):
        @chunks(half, 32)
        def _(spot):
            put(m.gc2, (spot, cols), field_grad(6, m.d2[spot, cols], m.e[spot, cols], cols))

    store(m.gc2, m.gc2_h)

    def back_through(pair, weights, raw, k):
        m.back[...] = product(jnp.concatenate([pair[0], pair[1]], 0), weights[...], True)

        @chunks(half, 32)
        def _(spot):
            value = raw[spot, :]
            grads = m.back[spot, :] * slope(affine(k, value))
            m.back[spot, :] = grads
            collect(0, grads)
            collect(1, grads * normed(k, value))

    back_through(m.gc2, m.wce, m.merged, 3)
    bias_grad, gain_grad = Sum([collected(0), collected(1)]).all(512, 512)
    clear()
    settle_back(3, bias_grad, gain_grad, number_half)
    m.biasing[3:4] = bias_grad
    m.scaling[3:4] = gain_grad
    merged_grad = field_grad(3, m.back[...], m.merged[...])
    m.eg[...] = merged_grad

    for k in (2, 1, 0):
        cols = slice((k + 1) * 128, (k + 2) * 128)
        grads = m.eg[:, cols]
        if k < 2:
            grads = grads + m.eg[:, (k + 2) * 128 : (k + 3) * 128]
        put(m.gk, (k,), grads)
        for i in range(2):
            m.grad_pad[k, 1 + i, own] = grads[i * band : i * band + band]
        halo(m.grad_pad.at[k], 3 + k)
        for i in range(4):
            put(m.grad_sides, (i,), sides(m.grad_pad[k, i]))
        result = jnp.zeros((2 * (band + 16), 128), jnp.float32)
        for dy in range(3):
            lhs = jnp.concatenate([m.grad_sides[p, i + dy] for p in range(2) for i in range(2)], 0)
            for dx in range(3):
                result = result + product(
                    lhs[:, dx * 128 : dx * 128 + 128],
                    m.kern[k, 2 - dy, (2 - dx) * 128 : (3 - dx) * 128, :],
                    True,
                )
        span = band + 16
        tap = [m.taps[i : i + 1, k * 128 : (k + 1) * 128] for i in range(3)]
        tap_grads = [0.0, 0.0, 0.0]
        for i in range(2):
            m.mixed_grad[i] = result[i * span : i * span + span]
            middle = m.mixed_grad[i, own]
            for j, value in enumerate(
                (
                    middle * before_band * m.source[k, 1 + i, previous],
                    middle * m.source[k, 1 + i, own],
                    middle * after_band * m.source[k, 1 + i, following],
                )
            ):
                tap_grads[j] = tap_grads[j] + jnp.sum(value, axis=0, keepdims=True)
            m.eg[i * band : i * band + band, cols] = (
                tap[2] * before_band * m.mixed_grad[i, previous]
                + tap[1] * middle
                + tap[0] * after_band * m.mixed_grad[i, following]
            )
        for j in range(3):
            m.temporal[j : j + 1, k * 128 : (k + 1) * 128] = tap_grads[j]

    store(m.gk, m.gk_h)

    gate = m.gate[...]
    m.gate_part[...] = jnp.zeros_like(m.gate_part)
    touched = m.eg[...] * m.hid[...]
    touched = jnp.sum(touched.reshape(2 * depth, 8, 512), axis=1)
    m.gate_part[:depth] = touched[:depth] + touched[depth:]
    m.gate_part[...] = m.gate_part[...] * gate * (1.0 - gate)
    m.exciter[...] = small_outer(m.pooled[...], m.gate_part[...])
    current, earlier = rows_sum(
        m.gate_part, m.gate_slots, pl.ds(pad - 8, 8), m.gate_near, after_f, 1
    )
    place = lax.broadcasted_iota(jnp.int32, current.shape, 0)
    last_row = depth - 1 - (pad - 8)
    shifted = jnp.where(place == 0, earlier[last_row : last_row + 1], pltpu.roll(current, 1, 0))
    pooled_grads = small_product(jnp.concatenate([current, shifted], 0), m.wex[...], True) / area
    motion = pooled_grads[:pad] * after16[:, :32]
    motion_before = pooled_grads[pad:] * before16[:, :32]
    m.stencil[...] = small_outer(m.follow[:, :288], motion) * (1.0 / rows)
    spread = small_product(motion_before, m.kst[...], True)

    def tap_value(dy, dx):
        start = (dy * 3 + dx) * 32
        return spread[:, start : start + 32]

    values = []
    by_row = []
    for row in range(2):
        columns = []
        for dx in range(3):
            if row == 0:
                value = tap_value(0, dx) + tap_value(1, dx)
                value = value + tap_value(2, dx) * above_one
            else:
                value = tap_value(1, dx) + tap_value(2, dx)
                value = value + tap_value(0, dx) * below_one
            columns.append(value)
        by_row.append(columns)
    for kind in range(3):
        for row in range(2):
            d0, d1, d2 = by_row[row]
            value = (d0 + d1 + d2, d0 + d1, d1 + d2)[kind]
            values.append(value - motion)
    reduced_grad = jnp.concatenate(values, 0)
    edges = jnp.concatenate([m.edge[0] - m.edge[1] - m.edge[2], m.edge[1], m.edge[2]], 0)
    m.condenser[...] = small_outer(edges.reshape(6 * pad, 512), reduced_grad)
    m.edge_back[...] = small_product(reduced_grad, m.wer[...], True).reshape(3, 2, pad, 512)

    for row in range(2):

        @pl.loop(0, depth)
        def _(frame):
            spot = pl.ds(pl.multiple_of(row * band + frame * 8, 8), 8)
            line = pl.ds(frame, 1)
            column = lax.broadcasted_iota(jnp.int32, (8, 512), 0)
            extra = jnp.where(
                column == 0,
                m.edge_back[1, row, line, :],
                jnp.where(column == 7, m.edge_back[2, row, line, :], m.edge_back[0, row, line, :]),
            )
            raw = m.d[spot, :]
            grads = m.eg[spot, :] * m.gate_all[pl.ds(pl.multiple_of(frame * 8, 8), 8), :] + extra
            grads = grads * slope(affine(2, raw))
            m.back[spot, :] = grads
            collect(0, grads)
            collect(1, grads * normed(2, raw))

    bias_grad, gain_grad = Sum([collected(0), collected(1)]).all(512, 512)
    clear()
    settle_back(2, bias_grad, gain_grad, number_half)
    m.biasing[2:3] = bias_grad
    m.scaling[2:3] = gain_grad

    @chunks(half, 32)
    def _(spot):
        put(m.ga2, (spot, slice(None)), field_grad(2, m.back[spot, :], m.d[spot, :]))

    store(m.ga2, m.ga2_h)

    @column_tiles
    def _(cols):
        m.e[:, cols] = product(jnp.concatenate([m.ga2[0], m.ga2[1]], 0), m.wcr[cols, :], True)

        @chunks(half, 32)
        def _(spot):
            grads = (m.d2[spot, cols] + m.e[spot, cols]) * slope(first_sum(spot, cols))
            m.d2[spot, cols] = grads
            collect(0, grads, cols)
            collect(1, grads * normed(4, m.c[spot, cols], cols), cols)
            collect(2, grads * normed(5, m.s[spot, cols], cols), cols)

    bias_grad, gain_c, gain_p = Sum(
        [collected(0, wide), collected(1, wide), collected(2, wide)]
    ).all(wide, wide, wide)
    clear()
    settle_back(4, bias_grad, gain_c, number_half)
    settle_back(5, bias_grad, gain_p, number_half)
    for k in range(2):
        m.baselines[k : k + 1] = bias_grad
    m.amplitudes[0:1] = gain_c
    m.amplitudes[1:2] = gain_p

    @column_tiles
    def _(cols):
        @chunks(half, 32)
        def _(spot):
            grads = m.d2[spot, cols]
            put(m.gc1, (spot, cols), field_grad(4, grads, m.c[spot, cols], cols))
            put(m.gp, (spot, cols), field_grad(5, grads, m.s[spot, cols], cols))

    store(m.gc1, m.gc1_h)
    store(m.gp, m.gp_h)
    back_through(m.gc1, m.we, m.b, 1)

    @pl.when(above)
    def _():
        send(
            m.back.at[pl.ds(0, band)], m.back_halo, m.halo_s.at[2], m.halo_r.at[2], (f, r - 1)
        )

    total = Sum([collected(0), collected(1)])
    clear()

    for cols in (slice(0, 512), slice(512, 1024)):
        if cols.start:
            total.middle()
        m.sample[:, cols] = product(
            jnp.concatenate([m.gp[0], m.gp[1]], 0), m.wsk[cols, :], True
        )

    bias_grad, gain_grad = total.finish(512, 512)
    settle_back(1, bias_grad, gain_grad, number_half)
    m.biasing[1:2] = bias_grad
    m.scaling[1:2] = gain_grad

    def strided_grad(row, spot, value):
        put(m.gb, (row, spot, slice(0, 512)), value)
        put(m.gb, (row, spot, slice(512, 1024)), moved_up(value))

    for row in range(2):

        @chunks(band, 32)
        def _(spot):
            place = pl.ds(pl.multiple_of(row * band + spot.start, 32), 32)
            strided_grad(row, spot, field_grad(1, m.back[place, :], m.b[place, :]))

    @pl.when(below)
    def _():
        for k, (source, target) in enumerate(((m.b, m.b_halo), (m.back, m.back_halo))):
            pltpu.make_async_remote_copy(
                src_ref=source.at[pl.ds(0, band)],
                dst_ref=target,
                send_sem=m.halo_s.at[1 + k],
                recv_sem=m.halo_r.at[1 + k],
                device_id=(f, lax.rem(r + 1, rows)),
                device_id_type=MESH,
            ).wait_recv()

    @chunks(band, 32)
    def _(spot):
        value = field_grad(1, m.back_halo[spot, :], m.b_halo[spot, :])
        strided_grad(2, spot, value * below_one)

    store(m.gb, m.gb_h)

    def gb_rows(first, variant):
        lanes = slice(variant * 512, variant * 512 + 512)
        return jnp.concatenate([m.gb[k, first + i, :, lanes] for k in range(2) for i in range(2)], 0)

    def tap_weights(dy, dx):
        return m.ks[dy, dx * 512 : dx * 512 + 512, :]

    @pl.when(above)
    def _():
        for k, source in enumerate((m.b, m.back)):
            pltpu.make_async_remote_copy(
                src_ref=source.at[pl.ds(0, band)],
                dst_ref=m.back_halo,
                send_sem=m.halo_s.at[1 + k],
                recv_sem=m.halo_r.at[1 + k],
                device_id=(f, lax.rem(r + 1, rows)),
                device_id_type=MESH,
            ).wait_send()

    plan = {
        (0, 0): [(0, 0, 1, 1)],
        (1, 0): [(0, 0, 1, 2), (0, 1, 1, 0)],
        (0, 1): [(0, 0, 2, 1), (1, 0, 0, 1)],
        (1, 1): [(0, 0, 2, 2), (1, 0, 0, 2), (0, 1, 2, 0), (1, 1, 0, 0)],
    }
    for (parity, odd), terms in plan.items():
        result = None
        for first, variant, dy, dx in terms:
            value = product(gb_rows(first, variant), tap_weights(dy, dx), True)
            result = value if result is None else result + value
        m.back[...] = result
        for i in range(2):
            row = 2 * i + odd

            @chunks(band, 32)
            def _(spot):
                place = pl.ds(pl.multiple_of(i * band + spot.start, 32), 32)
                raw = m.a[1 + row, parity, spot, :]
                grads = m.back[place, :] * slope(affine(0, raw))
                m.ha[row, parity, spot, :] = grads
                collect(0, grads)
                collect(1, grads * normed(0, raw))

    bias_grad, gain_grad = Sum([collected(0), collected(1)]).all(512, 512)
    settle_back(0, bias_grad, gain_grad, number_full)
    m.biasing[0:1] = bias_grad
    m.scaling[0:1] = gain_grad

    @pl.loop(0, 4)
    def _(row):
        for parity in range(2):

            @chunks(band, 32)
            def _(spot):
                value = field_grad(0, m.ha[row, parity, spot, :], m.a[1 + row, parity, spot, :])
                put(m.ga1, (row, parity, spot, slice(None)), value)

        lhs = jnp.concatenate([m.ga1[0, row].reshape(half, 512), m.ga1[1, row].reshape(half, 512)], 0)
        for part_cols in (slice(0, 512), slice(512, 1024)):
            result = product(lhs, m.wn[part_cols, :], True)
            even = jnp.where(lax.rem(row, 2) == 0, 1.0, 0.0)
            shortcut = m.sample[pl.ds(pl.multiple_of((row // 2) * band, band), band), part_cols]
            for parity in range(2):
                value = result[parity * band : parity * band + band]
                if parity == 0:
                    value = value + shortcut * even
                for frame in range(depth):
                    for k in range(4):
                        m.xs[
                            part_cols.start // 128 + k, frame, row, pl.ds(parity, 8, stride=2), :
                        ] = value[frame * 8 : frame * 8 + 8, k * 128 : k * 128 + 128]

    store(m.ga1, m.ga1_h)
    for row in range(4):
        for k, lane in enumerate(lanes):
            store(m.xs.at[k, :, row], m.pixels.at[:, row, :, lane])
    for copy in stores:
        copy.wait()

    @pl.when(below)
    def _():
        pltpu.make_async_remote_copy(
            src_ref=m.a.at[4],
            dst_ref=m.a.at[0],
            send_sem=m.halo_s.at[0],
            recv_sem=m.halo_r.at[0],
            device_id=(f, lax.rem(r + 1, rows)),
            device_id_type=MESH,
        ).wait_send()


def chain(
    x, before, after, wn, ks, we, wsk, wcr, wer, kst, wex, taps, kern, wce, gain, bias, wide_gain,
    wide_bias, slopes, call,
):
    frames, rows = lax.axis_size("frames"), lax.axis_size("rows")
    depth = x.shape[0]
    band, pad = depth * 8, -(-depth // 16) * 16
    half = 2 * band
    span = band + 16
    hbm, vmem = pl.BlockSpec(memory_space=pl.ANY), pl.BlockSpec(memory_space=pltpu.VMEM)

    def masks(mask):
        mask = mask.reshape(depth, 1)
        tall = jnp.broadcast_to(jnp.pad(mask, ((0, pad - depth), (0, 0))), (pad, 128))
        return tall, jnp.broadcast_to(mask[:, :, None], (depth, 8, 128)).reshape(band, 128)

    before16, before_band = masks(before)
    after16, after_band = masks(after)
    inputs = dict(
        x=(x, hbm), slope_h=(slopes, hbm), wn_h=(wn, hbm), wsk_h=(wsk, hbm), ks_h=(ks, hbm),
        we_h=(we, hbm), wcr_h=(wcr, hbm), wce_h=(wce, hbm), kern_h=(kern, hbm), wer=(wer, vmem),
        kst=(kst, vmem), wex=(wex, vmem), taps=(taps, vmem), gain=(gain, vmem), bias=(bias, vmem),
        wide_gain=(wide_gain, vmem), wide_bias=(wide_bias, vmem), before16=(before16, vmem),
        after16=(after16, vmem), before_band=(before_band, vmem), after_band=(after_band, vmem),
    )

    def wide_of(*shape):
        return jax.ShapeDtypeStruct(shape, jnp.float32)

    def slim_of(*shape):
        return jax.ShapeDtypeStruct(shape, jnp.bfloat16)

    kept = dict(
        xb=(2, 4 * half, 1024), pc=(2, 5, band, 1536), h2=(2, half, 512), uh=(2, half, 2048),
        squashed=(2, half, 512), mixed=(2, 3, 4, band, 384), gc2=(2, half, 2048),
        gk=(2, 3, half, 128), ga2=(2, half, 512), gc1=(2, half, 2048), gp=(2, half, 2048),
        gb=(2, 3, band, 1024), ga1=(2, 4, 2, band, 512),
    )
    outputs = dict(
        layer_output=(wide_of(depth, 2, 8, 2048), hbm), pixels=(wide_of(depth, 4, 16, 1024), hbm),
        scaling=(wide_of(4, 512), vmem), biasing=(wide_of(4, 512), vmem),
        amplitudes=(wide_of(3, 2048), vmem), baselines=(wide_of(3, 2048), vmem),
        condenser=(wide_of(512, 32), vmem), stencil=(wide_of(288, 32), vmem),
        exciter=(wide_of(32, 512), vmem), temporal=(wide_of(3, 384), vmem),
    )
    for name in kept:
        outputs[name + "_h"] = (slim_of(*kept[name]), hbm)

    def f32(*shape):
        return pltpu.VMEM(shape, jnp.float32)

    def b16(*shape):
        return pltpu.VMEM(shape, jnp.bfloat16)

    def sems(*shape):
        return pltpu.SemaphoreType.DMA(shape)

    scratch = dict(
        wn=b16(1024, 512), wsk=b16(1024, 2048), ks=b16(3, 1536, 512), we=b16(512, 2048),
        wcr=b16(2048, 512), wce=b16(512, 2048), kern=b16(3, 3, 384, 128),
        xs=f32(8, depth, 4, 16, 128), a=f32(5, 2, band, 512), b=f32(half, 512), c=f32(half, 2048),
        s=f32(half, 2048), up=f32(half, 2048), d=f32(half, 512), hid=f32(half, 512),
        merged=f32(half, 512), e=f32(half, 2048), out=f32(2, depth, 8, 2048),
        slope=f32(2, depth, 8, 2048), d2=f32(half, 2048), back=f32(half, 512), eg=f32(half, 512),
        sample=f32(half, 1024), ha=f32(4, 2, band, 512), b_halo=f32(band, 512),
        back_halo=f32(band, 512), source=f32(3, 4, span, 128), grad_pad=f32(3, 4, span, 128),
        mixed_grad=f32(2, span, 128), grad_sides=b16(2, 4, span, 384), gate_all=f32(band, 512),
        edge=f32(3, 2, pad, 512), edge_back=f32(3, 2, pad, 512), gate=f32(pad, 512),
        gate_part=f32(pad, 512), pooled=f32(pad, 32), follow=f32(pad, 384), tap_in=f32(pad, 384),
        tap_slots=f32(rows, pad, 384), tap_near=f32(rows, 8, 384), gate_slots=f32(rows, pad, 512),
        gate_near=f32(rows, 8, 512), stat=f32(4, 8, 2048), vec=f32(48, 2048), ar_in=f32(2, 48, 128),
        ar_part=f32(2, 48, 128), ar_out=f32(48, 128), ar_rows=f32(2, rows, 48, 128),
        ar_frames=f32(2, frames, 48, 128), ar_rs=sems(2, rows), ar_rr=sems(2, rows),
        ar_fs=sems(2, frames), ar_fr=sems(2, frames), rows_s=sems(2, 2 * rows),
        rows_r=sems(2, 2 * rows), ring_s=sems(6, 8), ring_r=sems(6, 8), halo_s=sems(3),
        halo_r=sems(3), load_sem=sems(48), store_sem=sems(56),
    )
    for name in kept:
        scratch[name] = b16(*kept[name])
    names = list(inputs) + list(outputs) + list(scratch)
    results = pl.pallas_call(
        lambda *refs: chain_kernel(names, (frames, rows, depth), *refs),
        out_shape=[shape for shape, _ in outputs.values()],
        in_specs=[spec for _, spec in inputs.values()],
        out_specs=[spec for _, spec in outputs.values()],
        scratch_shapes=list(scratch.values()),
        compiler_params=pltpu.CompilerParams(
            collective_id=call, has_side_effects=True, vmem_limit_bytes=63 * 2**20
        ),
    )(*[value for value, _ in inputs.values()])
    return SimpleNamespace(**dict(zip(outputs, results)))


def pair_outer(left, right):
    def one(a, b):
        return lax.dot_general(
            a, b, (((0,), (0,)), ((), ())), preferred_element_type=jnp.float32
        )

    return one(left[0], right[0]) + one(left[0], right[1]) + one(left[1], right[0])


def add_rows(target, source, rows, target_columns=None):
    step = 8
    while rows % (2 * step) == 0 and 2 * step * source.shape[-1] <= 32768:
        step *= 2

    @pl.loop(0, rows // step)
    def _(place):
        spot = pl.ds(pl.multiple_of(place * step, step), step)
        if target_columns is None:
            target[spot, :] = target[spot, :] + source[spot, :]
        else:
            target[spot, target_columns] = target[spot, target_columns] + source[spot, :]


def gradient_item(grad, out, bufs, send, recv, place):
    own, from_core, first_p, first_q, second_p, second_q, third, fourth, final = bufs
    a_count, b_count, rows, columns = own.shape
    half, quarter = columns // 2, columns // 4
    ia, ib, c, r = place
    f = (ia * b_count + ib) * 2 + c
    low, high = pl.ds(0, half), pl.ds(half, half)
    flip1 = r + 1 - 2 * lax.rem(r, 2)
    flip2 = lax.rem(r + 2, 4)
    pending = []
    used = [0]

    def remote(source, target, device):
        copy = pltpu.make_async_remote_copy(
            src_ref=source,
            dst_ref=target,
            send_sem=send.at[used[0]],
            recv_sem=recv.at[used[0]],
            device_id=device,
            device_id_type=MESH,
        )
        used[0] += 1
        copy.start()
        pending.append(copy)
        return copy

    def a_peer(step):
        other = lax.rem(ia + step, a_count)
        return other, ((other * b_count + ib) * 2 + c, r)

    def b_peer(step):
        other = lax.rem(ib + step, b_count)
        return other, ((ia * b_count + other) * 2 + c, r)

    core = (f + 1 - 2 * c, r)
    local = pltpu.make_async_copy(grad.at[:, :, c], own, recv.at[used[0]])
    used[0] += 1
    local.start()
    waits = [remote(grad.at[:, :, 1 - c], from_core, core)]
    yield
    local.wait()
    waits[0].wait_recv()
    for i in range(a_count):
        for j in range(b_count):
            add_rows(own.at[i, j], from_core.at[i, j], rows)
    waits = []
    for step in range(1, b_count):
        other, device = b_peer(step)
        waits.append(remote(own.at[:, other, :, low], first_p.at[step - 1], device))
    for step in range(1, a_count):
        other, device = a_peer(step)
        waits.append(remote(own.at[other, :, :, high], first_q.at[step - 1], device))
    yield
    for copy in waits:
        copy.wait_recv()
    for step in range(1, b_count):
        for i in range(a_count):
            add_rows(own.at[i, ib, :, low], first_p.at[step - 1, i], rows)
    for step in range(1, a_count):
        for j in range(b_count):
            add_rows(own.at[ia, j, :, high], first_q.at[step - 1, j], rows)
    waits = []
    for step in range(1, a_count):
        other, device = a_peer(step)
        waits.append(remote(own.at[other, ib, :, low], second_p.at[step - 1], device))
    for step in range(1, b_count):
        other, device = b_peer(step)
        waits.append(remote(own.at[ia, other, :, high], second_q.at[step - 1], device))
    yield
    for copy in waits:
        copy.wait_recv()
    mine = own.at[ia, ib]
    for step in range(1, a_count):
        add_rows(mine.at[:, low], second_p.at[step - 1], rows)
    for step in range(1, b_count):
        add_rows(mine.at[:, high], second_q.at[step - 1], rows)

    def part(index):
        return pl.ds(pl.multiple_of(index * quarter, quarter), quarter)

    waits = []
    for k in range(2):
        waits.append(remote(mine.at[:, part(lax.rem(flip1, 2) + 2 * k)], third.at[k], (f, flip1)))
    yield
    for copy in waits:
        copy.wait_recv()
    for k in range(2):
        add_rows(mine, third.at[k], rows, part(lax.rem(r, 2) + 2 * k))
    waits = [remote(mine.at[:, part(flip2)], fourth, (f, flip2))]
    yield
    waits[0].wait_recv()
    add_rows(mine, fourth, rows, part(r))
    piece = mine.at[:, part(r)]
    cut = rows // 2 if rows % 16 == 0 else rows
    first, second = pl.ds(0, cut), pl.ds(cut, rows - cut)
    local = pltpu.make_async_copy(piece, out.at[ia, ib, c], recv.at[used[0]])
    used[0] += 1
    local.start()
    waits = []
    for step in range(1, b_count):
        other, device = b_peer(step)
        waits.append(remote(piece.at[first], out.at[ia, ib, c, first], device))
    if cut < rows:
        for step in range(1, a_count):
            other, device = a_peer(step)
            waits.append(remote(piece.at[second], out.at[ia, ib, c, second], device))
    yield
    local.wait()
    for copy in waits:
        copy.wait_recv()
    waits = []
    for step in range(1, a_count):
        other, device = a_peer(step)
        waits.append(remote(out.at[ia, :, c, first], out.at[ia, :, c, first], device))
    if cut < rows:
        for step in range(1, b_count):
            other, device = b_peer(step)
            waits.append(remote(out.at[:, ib, c, second], out.at[:, ib, c, second], device))
    yield
    for copy in waits:
        copy.wait_recv()
    waits = [remote(out.at[:, :, c], out.at[:, :, c], core)]
    yield
    waits[0].wait_recv()
    for copy in pending:
        copy.wait_send()


def gradient_kernel(splits, counts, *refs):
    a_count, b_count = counts
    grads, refs = refs[: len(splits)], refs[len(splits) :]
    outs, refs = refs[: len(splits)], refs[len(splits) :]
    f = lax.axis_index("frames")
    r = lax.axis_index("rows")
    c = lax.rem(f, 2)
    ib = lax.rem(f // 2, b_count)
    ia = f // (2 * b_count)
    partners = [
        (f + 1 - 2 * c, r),
        (f, r + 1 - 2 * lax.rem(r, 2)),
        (f, lax.rem(r + 2, 4)),
    ]
    for step in range(1, b_count):
        partners.append(((ia * b_count + lax.rem(ib + step, b_count)) * 2 + c, r))
    for step in range(1, a_count):
        partners.append(((lax.rem(ia + step, a_count) * b_count + ib) * 2 + c, r))
    barrier = pltpu.get_barrier_semaphore()
    for partner in partners:
        pl.semaphore_signal(barrier, inc=1, device_id=partner, device_id_type=MESH)
    pl.semaphore_wait(barrier, len(partners))
    waiting = []
    for index, split in enumerate(splits):
        for k in range(split):
            bufs, refs = refs[:9], refs[9:]
            send, recv, refs = refs[0], refs[1], refs[2:]
            waiting.append(
                gradient_item(
                    grads[index].at[k], outs[index].at[k], bufs, send, recv, (ia, ib, c, r)
                )
            )
    active = []
    while waiting or active:
        running = []
        for item in active:
            if next(item, active) is None:
                running.append(item)
        if waiting:
            item = waiting.pop(0)
            next(item)
            running.append(item)
        active = running


def sum_gradients(grads, call):
    frames = lax.axis_size("frames")
    levels = int(math.log2(frames // 2))
    b_count = 2 ** (levels // 2)
    a_count = frames // 2 // b_count
    operands, results, scratch = [], [], []
    copies = 8 + 2 * (a_count - 1) * 2 + 2 * (b_count - 1) * 2
    for grad, split in grads:
        depth, columns = grad.shape
        rows = depth // (split * frames)
        operands.append(grad.reshape(split, a_count, b_count, 2, rows, columns))
        results.append(
            jax.ShapeDtypeStruct((split, a_count, b_count, 2, rows, columns // 4), jnp.float32)
        )
        for _ in range(split):
            for shape in (
                (a_count, b_count, rows, columns),
                (a_count, b_count, rows, columns),
                (b_count - 1, a_count, rows, columns // 2),
                (a_count - 1, b_count, rows, columns // 2),
                (a_count - 1, rows, columns // 2),
                (b_count - 1, rows, columns // 2),
                (2, rows, columns // 4),
                (rows, columns // 4),
                (8, 128),
            ):
                scratch.append(pltpu.VMEM(shape, jnp.float32))
            scratch += [pltpu.SemaphoreType.DMA((copies,)), pltpu.SemaphoreType.DMA((copies,))]
    splits = [split for _, split in grads]
    totals = pl.pallas_call(
        lambda *refs: gradient_kernel(splits, (a_count, b_count), *refs),
        out_shape=results,
        in_specs=[pl.BlockSpec(memory_space=pl.ANY)] * len(grads),
        out_specs=[pl.BlockSpec(memory_space=pl.ANY)] * len(grads),
        scratch_shapes=scratch,
        compiler_params=pltpu.CompilerParams(
            collective_id=call, has_side_effects=True, vmem_limit_bytes=60 * 2**20
        ),
    )(*operands)
    return [
        total.reshape(grad.shape[0], grad.shape[1] // 4)
        for total, (grad, _) in zip(totals, grads)
    ]


def flat(matrix):
    return matrix.reshape(-1, matrix.shape[-1])


def by_column(matrix):
    pieces = matrix.reshape(matrix.shape[0], 4, -1).transpose(1, 0, 2)
    return pieces.reshape(4, -1, 128).transpose(1, 0, 2).reshape(-1, 512)


def shards(
    input_feature_maps,
    sequence_slot_lookup,
    sequence_span_lookup,
    opening_reducer,
    downsampling_filter,
    opening_expander,
    skip_projection,
    closing_reducer,
    excite_reducer,
    excite_spatial_filter,
    excite_expander,
    time_taps,
    spatial_filters,
    closing_expander,
    narrow_norm_gains,
    narrow_norm_biases,
    wide_norm_gains,
    wide_norm_biases,
    loss_slope_wrt_final,
):
    before = (sequence_slot_lookup > 0).astype(jnp.float32)
    after = (sequence_slot_lookup < sequence_span_lookup - 1).astype(jnp.float32)
    k = chain(
        input_feature_maps,
        before,
        after,
        opening_reducer,
        downsampling_filter.reshape(3, 1536, 512),
        opening_expander,
        skip_projection,
        closing_reducer,
        excite_reducer,
        excite_spatial_filter.reshape(288, 32),
        excite_expander,
        time_taps.astype(jnp.float32),
        spatial_filters.reshape(3, 3, 384, 128),
        closing_expander,
        narrow_norm_gains,
        narrow_norm_biases,
        wide_norm_gains,
        wide_norm_biases,
        loss_slope_wrt_final,
        0,
    )
    half = k.h2_h.shape[1]
    band = half // 2
    strider = []
    gb = k.gb_h[:, :2, :, :512].reshape(2, half, 512)
    for dy in range(3):
        rows = k.pc_h[:, dy : dy + 3 : 2].reshape(2, half, 1536)
        strider.append(pair_outer(rows, gb))
    kernels = []
    for index in range(3):
        for dy in range(3):
            rows = k.mixed_h[:, index, dy : dy + 2].reshape(2, half, 384)
            kernels.append(pair_outer(rows, k.gk_h[:, index]))
    sampled = jnp.concatenate([k.xb_h[:, :band], k.xb_h[:, 2 * half : 2 * half + band]], 1)
    kernels = jnp.concatenate(kernels, 0).reshape(4, -1, 4, 32)
    temporal = jnp.pad(k.temporal.reshape(3, 4, -1), ((0, 0), (0, 0), (0, 32))).reshape(3, -1)
    packed = jnp.concatenate(
        [
            kernels.transpose(1, 2, 0, 3).reshape(kernels.shape[1], -1),
            by_column(k.condenser),
            by_column(k.stencil),
            by_column(k.exciter),
            by_column(temporal),
        ],
        0,
    )
    packed = jnp.pad(packed, ((0, 1024 - packed.shape[0]), (0, 0)))
    totals = sum_gradients(
        (
            (pair_outer(sampled, k.gp_h), 2),
            (jnp.concatenate(strider, 0), 3),
            (pair_outer(k.h2_h, k.gc1_h), 1),
            (pair_outer(k.squashed_h, k.gc2_h), 1),
            (pair_outer(k.uh_h, k.ga2_h), 1),
            (pair_outer(k.xb_h, k.ga1_h.reshape(2, -1, 512)), 1),
            (packed, 1),
        ),
        1,
    )
    tail = totals[6]
    start = kernels.shape[1]
    grad_kernels = tail[:start].reshape(start, 4, -1).transpose(1, 0, 2)
    return (
        k.layer_output,
        k.pixels,
        totals[5],
        totals[1].reshape(downsampling_filter.shape[:-1] + (-1,)),
        totals[2],
        totals[0],
        totals[4],
        tail[start : start + 32].reshape(excite_reducer.shape[0], -1),
        tail[start + 32 : start + 50].reshape(excite_spatial_filter.shape[:-1] + (-1,)),
        tail[start + 50 : start + 82],
        tail[start + 82 : start + 85, :96],
        grad_kernels.reshape(spatial_filters.shape[:-1] + (-1,)),
        totals[3],
        k.scaling,
        k.biasing,
        k.amplitudes,
        k.baselines,
    )


def solution(mesh):
    return jax.shard_map(
        shards,
        mesh=mesh,
        in_specs=(
            P("frames", "rows", None, None),
            P("frames"),
            P("frames"),
            P(),
            P(),
            P(),
            P(),
            P(),
            P(),
            P(),
            P(),
            P(),
            P(),
            P(),
            P(),
            P(),
            P(),
            P(),
            P("frames", "rows", None, None),
        ),
        out_specs=(
            P("frames", "rows", None, None),
            P("frames", "rows", None, None),
            P(None, "rows"),
            P(None, None, None, "rows"),
            P(None, "rows"),
            P(None, "rows"),
            P(None, "rows"),
            P(None, "rows"),
            P(None, None, None, "rows"),
            P(None, "rows"),
            P(None, "rows"),
            P(None, None, None, None, "rows"),
            P(None, "rows"),
            P(),
            P(),
            P(),
            P(),
        ),
        check_vma=False,
    )
```

```python
import math
from types import SimpleNamespace

import jax
import jax.numpy as jnp
from jax import lax
from jax.experimental import pallas as pl
from jax.experimental.pallas import tpu as pltpu
from jax.sharding import PartitionSpec as P

MESH = pl.DeviceIdType.MESH
EPSILON = 1e-05
VMEM_BYTES = 65400 * 2**10


def split(value):
    high = value.astype(jnp.bfloat16)
    return high, (value - high.astype(jnp.float32)).astype(jnp.bfloat16)


def put(pair_ref, index, value):
    high, low = split(value)
    pair_ref[(0,) + index] = high
    pair_ref[(1,) + index] = low


def product(stacked, weights, turned=False):
    result = lax.dot_general(
        stacked,
        weights,
        (((1,), (1 if turned else 0,)), ((), ())),
        preferred_element_type=jnp.float32,
    )
    half = result.shape[0] // 2
    return result[:half] + result[half:]


def small_product(value, weights, turned=False):
    return product(jnp.concatenate(split(value), 0), weights, turned)


def small_outer(left, right):
    def one(a, b):
        return lax.dot_general(
            a, b, (((0,), (0,)), ((), ())), preferred_element_type=jnp.float32
        )

    (a, b), (c, d) = split(left), split(right)
    return one(a, c) + one(a, d) + one(b, c)


def slope(value):
    logistic = jax.nn.sigmoid(value)
    return logistic * (1.0 + value * (1.0 - logistic))


def silu(value):
    return value * jax.nn.sigmoid(value)


def folded(value):
    return jnp.sum(value.reshape(-1, 8, value.shape[-1]), axis=0)


def moved_down(value):
    place = lax.broadcasted_iota(jnp.int32, value.shape, 0)
    return jnp.where(lax.rem(place, 8) == 0, 0.0, pltpu.roll(value, 1, 0))


def moved_up(value):
    place = lax.broadcasted_iota(jnp.int32, value.shape, 0)
    return jnp.where(lax.rem(place, 8) == 7, 0.0, pltpu.roll(value, value.shape[0] - 1, 0))


def chunks(total, step):
    def bind(body):
        @pl.loop(0, total // step)
        def _(place):
            body(pl.ds(pl.multiple_of(place * step, step), step))

    return bind


PUMPS = (1, 1, 1, 1, 1, 1, 1, 1, 1, 1, 1, 1)


def chain_kernel(names, dims, *refs):
    frames, rows, depth, a_count, b_count = dims
    m = SimpleNamespace(**dict(zip(names, refs)))
    f = lax.axis_index("frames")
    r = lax.axis_index("rows")
    after_f, before_f = lax.rem(f + 1, frames), lax.rem(f + frames - 1, frames)
    band = depth * 8
    half = 2 * band
    number_half = float(half * frames * rows)
    number_full = 4.0 * number_half
    above, below = r > 0, r < rows - 1
    above_one, below_one = jnp.where(above, 1.0, 0.0), jnp.where(below, 1.0, 0.0)
    wide = 2048

    loads = []

    def load(source, target):
        copy = pltpu.make_async_copy(source, target, m.load_sem.at[len(loads)])
        copy.start()
        loads.append(copy)
        return copy

    lanes = [slice(k * 128, k * 128 + 128) for k in range(8)]

    def load_row(row):
        return [
            load(m.x.at[:, row, :, lane], m.xs.at[k, :, row]) for k, lane in enumerate(lanes)
        ]

    x_loads = [load_row(row) for row in (3, 0, 1, 2)]
    wn_load = load(m.wn_h, m.wn)
    wsk_load = load(m.wsk_h, m.wsk)
    ks_load = load(m.ks_h, m.ks)
    we_load = load(m.we_h, m.we)
    wcr_load = load(m.wcr_h, m.wcr)
    wce_load = load(m.wce_h, m.wce)
    kern_load = load(m.kern_h, m.kern)
    slope_loads = [load(m.slope_h.at[:, row], m.slope.at[row]) for row in range(2)]

    barrier = pltpu.get_barrier_semaphore()
    partners = [(f, lax.rem(r + step, rows)) for step in range(1, rows)]
    partners += [(lax.rem(f + step, frames), r) for step in range(1, frames)]
    for other in (after_f, before_f):
        partners += [(other, lax.rem(r + step, rows)) for step in range(1, rows)]
    for partner in partners:
        pl.semaphore_signal(barrier, inc=1, device_id=partner, device_id_type=MESH)
    pl.semaphore_wait(barrier, len(partners))

    sent = []

    def send(source, target, send_sem, recv_sem, device):
        copy = pltpu.make_async_remote_copy(
            src_ref=source,
            dst_ref=target,
            send_sem=send_sem,
            recv_sem=recv_sem,
            device_id=device,
            device_id_type=MESH,
        )
        copy.start()
        return copy

    class Sum:
        count = 0

        def __init__(self, pieces):
            self.set = Sum.count % 2
            Sum.count += 1
            place = 0
            for piece in pieces:
                for k in range(piece.shape[1] // 128):
                    m.ar_in[self.set, place : place + 1, :] = piece[:, k * 128 : k * 128 + 128]
                    place += 1
            self.size = -(-place // 8) * 8
            self.copies = self.spread(
                m.ar_in, (m.ar_rows_a, m.ar_rows_b), m.ar_rs, m.ar_rr, r, rows, lambda other: (f, other)
            )

        def spread(self, source, slots, send_sem, recv_sem, me, count, device):
            piece = source.at[self.set, pl.ds(0, self.size)]
            copies = []
            for step in range(1, count):
                copies.append(
                    send(
                        piece,
                        slots[self.set].at[step, pl.ds(0, self.size)],
                        send_sem.at[self.set, step],
                        recv_sem.at[self.set, step],
                        device(lax.rem(me + step, count)),
                    )
                )
            return copies

        def gather(self, source, slots, me, count):
            for copy in self.copies:
                copy.wait_recv()
            slots = slots[self.set]
            slots[0, : self.size] = source[self.set, : self.size]
            total = slots[me, : self.size]
            for other in range(1, count):
                spot = lax.rem(me + count - other, count)
                total = total + slots[spot, : self.size]
            return total

        def middle(self):
            first = self.copies
            m.ar_part[self.set, : self.size] = self.gather(m.ar_in, (m.ar_rows_a, m.ar_rows_b), r, rows)
            self.copies = self.spread(
                m.ar_part, (m.ar_frames_a, m.ar_frames_b), m.ar_fs, m.ar_fr, f, frames, lambda other: (other, r)
            )
            for copy in first:
                copy.wait_send()

        def finish(self, *sizes):
            m.ar_out[: self.size] = self.gather(m.ar_part, (m.ar_frames_a, m.ar_frames_b), f, frames)
            for copy in self.copies:
                copy.wait_send()
            results, place = [], 0
            for size in sizes:
                parts = []
                for k in range(size // 128):
                    parts.append(m.ar_out[place : place + 1, :])
                    place += 1
                results.append(jnp.concatenate(parts, axis=1))
            return results

        def all(self, *sizes):
            self.middle()
            return self.finish(*sizes)

    def settle(k, totals, squares, number, gain, bias):
        size = totals.shape[1]
        center = totals / number
        spread = lax.rsqrt(squares / number - center * center + EPSILON)
        scale = spread * gain
        m.vec[6 * k : 6 * k + 1, :size] = center
        m.vec[6 * k + 1 : 6 * k + 2, :size] = spread
        m.vec[6 * k + 2 : 6 * k + 3, :size] = scale
        m.vec[6 * k + 3 : 6 * k + 4, :size] = bias - center * scale

    def settle_back(k, bias_grad, gain_grad, number):
        size = bias_grad.shape[1]
        m.vec[6 * k + 4 : 6 * k + 5, :size] = bias_grad / number
        m.vec[6 * k + 5 : 6 * k + 6, :size] = gain_grad / number

    def vec(k, which, cols=slice(0, 512)):
        return m.vec[6 * k + which : 6 * k + which + 1, cols]

    def affine(k, value, cols=slice(0, 512)):
        return value * vec(k, 2, cols) + vec(k, 3, cols)

    def normed(k, value, cols=slice(0, 512)):
        return (value - vec(k, 0, cols)) * vec(k, 1, cols)

    def field_grad(k, grads, value, cols=slice(0, 512)):
        return vec(k, 2, cols) * (
            grads - vec(k, 4, cols) - normed(k, value, cols) * vec(k, 5, cols)
        )

    def clear():
        m.stat[...] = jnp.zeros_like(m.stat)

    def collect(k, value, cols=slice(0, 512)):
        m.stat[k, :, cols] = m.stat[k, :, cols] + folded(value)

    def collected(k, size=512):
        return jnp.sum(m.stat[k, :, :size], axis=0, keepdims=True)

    def column_tiles(body):
        @pl.loop(0, wide // 512)
        def _(place):
            body(pl.ds(pl.multiple_of(place * 512, 512), 512))

    c = lax.rem(f, 2)
    ib = lax.rem(f // 2, b_count)
    ia = f // (2 * b_count)
    flip1 = r + 1 - 2 * lax.rem(r, 2)
    flip2 = lax.rem(r + 2, rows)
    core = (f + 1 - 2 * c, r)
    thin = 512 // frames

    def a_peer(step):
        other = lax.rem(ia + step, a_count)
        return other, ((other * b_count + ib) * 2 + c, r)

    def b_peer(step):
        other = lax.rem(ib + step, b_count)
        return other, ((ia * b_count + other) * 2 + c, r)

    def add_block(target, source):
        @pl.loop(0, thin // 8)
        def _(place):
            spot = pl.ds(pl.multiple_of(place * 8, 8), 8)
            target[spot, :] = target[spot, :] + source[spot, :]

    def column_part(index):
        return pl.ds(pl.multiple_of(index * 128, 128), 128)

    def unit_steps(fill, out, pair, kind):
        two, five = pair % 2, pair % 5
        own, away = m.g_own.at[kind, five], m.g_away.at[kind, two]
        near, third, fourth = m.g_near.at[kind, two], m.g_third.at[kind, two], m.g_fourth.at[kind, two]
        final = m.g_final.at[kind, two]
        first = (m.g_first_p, m.g_first_q)[kind].at[two]
        second = (m.g_second_p, m.g_second_q)[kind].at[two]
        one_count, one_peer = ((b_count, b_peer), (a_count, a_peer))[kind]
        two_count, two_peer = ((a_count, a_peer), (b_count, b_peer))[kind]
        send_sem, recv_sem = m.g_send.at[kind, pair % 10], m.g_recv.at[kind, pair % 10]
        used = [0]

        def go(source, target, device):
            spot = used[0]
            used[0] += 1
            return send(source, target, send_sem.at[spot], recv_sem.at[spot], device)

        def done(copies):
            for copy in copies:
                copy.wait_recv()
            for copy in copies:
                copy.wait_send()

        def pick(ref, one, other):
            return ref.at[other, one] if kind == 0 else ref.at[one, other]

        one_me, two_me = ((ib, ia), (ia, ib))[kind]
        fill(away, 1 - c)
        copies = [go(away, near, core)]
        fill(own, c)
        yield
        done(copies)
        for i in range(a_count):
            for j in range(b_count):
                add_block(own.at[i, j], near.at[i, j])
        copies = []
        for step in range(1, one_count):
            other, device = one_peer(step)
            source = own.at[:, other] if kind == 0 else own.at[other]
            copies.append(go(source, first.at[step - 1], device))
        yield
        done(copies)
        for step in range(1, one_count):
            for k in range(two_count):
                add_block(pick(own, one_me, k), first.at[step - 1, k])
        copies = []
        for step in range(1, two_count):
            other, device = two_peer(step)
            copies.append(go(pick(own, one_me, other), second.at[step - 1], device))
        yield
        done(copies)
        mine = own.at[ia, ib]
        for step in range(1, two_count):
            add_block(mine, second.at[step - 1])
        copies = []
        for k in range(2):
            copies.append(
                go(mine.at[:, column_part(lax.rem(flip1, 2) + 2 * k)], third.at[k], (f, flip1))
            )
        yield
        done(copies)
        for k in range(2):
            add_block(mine.at[:, column_part(lax.rem(r, 2) + 2 * k)], third.at[k])
        copies = [go(mine.at[:, column_part(flip2)], fourth, (f, flip2))]
        yield
        done(copies)
        final[...] = mine[:, column_part(r)] + fourth[...]
        local = pltpu.make_async_copy(final, out.at[c, ia, ib], recv_sem.at[used[0]])
        used[0] += 1
        local.start()
        copies = []
        for step in range(1, one_count):
            other, device = one_peer(step)
            copies.append(go(final, out.at[c, ia, ib], device))
        yield
        local.wait()
        done(copies)
        copies = []
        field = out.at[c, ia] if kind == 0 else out.at[c, :, ib]
        for step in range(1, two_count):
            other, device = two_peer(step)
            copies.append(go(field, field, device))
        yield
        done(copies)
        copies = [go(out.at[c], out.at[c], core)]
        yield
        done(copies)

    units, active, begun = [], [], [0]

    def advance():
        kept = []
        for pair in active:
            ended = False
            for unit in pair:
                if next(unit, active) is active:
                    ended = True
            if not ended:
                kept.append(pair)
        active[:] = kept
        if units:
            pair = []
            for kind in range(2):
                if units:
                    fill, out = units.pop(0)
                    pair.append(unit_steps(fill, out, begun[0], kind))
            begun[0] += 1
            for unit in pair:
                next(unit)
            active.append(pair)

    def pump(count):
        if count is None:
            while units or active:
                advance()
        else:
            for _ in range(count):
                advance()

    def begin_all_but(count):
        while len(units) > count:
            advance()

    def outer(left, right):
        def one(a, b):
            return lax.dot_general(
                a, b, (((0,), (0,)), ((), ())), preferred_element_type=jnp.float32
            )

        (high, low), (grad_high, grad_low) = left, right
        both = one(high, jnp.concatenate([grad_high, grad_low], 1))
        size = grad_high.shape[1]
        return both[:, :size] + both[:, size:] + one(low, grad_high)

    def blocks(value):
        return value.reshape(a_count, b_count, thin, value.shape[-1])

    def filler(left, right):
        def fill(target, which):
            start = pl.multiple_of(which * 256, 256)
            target[...] = blocks(
                outer([left(k, start) for k in range(2)], [right(k) for k in range(2)])
            )

        return fill

    def lanes_of(ref, quarter):
        def pick(k):
            return jnp.concatenate(
                [ref[k, :, z * 512 + quarter * 128 : z * 512 + quarter * 128 + 128] for z in range(4)],
                1,
            )

        return pick

    def whole(ref):
        return lambda k: ref[k]

    def rows_from(ref, base):
        return lambda k, start: ref[k, :, pl.ds(base + start, 256)]

    def out_lanes(ref, quarter):
        return ref.at[:, :, :, :, pl.ds(quarter * 128, 128)]

    def add_restorer():
        for quarter in range(4):
            units.append(
                (
                    filler(rows_from(m.squashed, 0), lanes_of(m.gc2, quarter)),
                    out_lanes(m.restorer, quarter),
                )
            )

    def add_widener():
        for quarter in range(4):
            units.append(
                (
                    filler(rows_from(m.h2, 0), lanes_of(m.uh, quarter)),
                    out_lanes(m.widener, quarter),
                )
            )

    def add_shortcut():
        def sampled(base):
            def pick(k, start):
                lane = pl.ds(base + start, 256)
                return jnp.concatenate(
                    [m.xb[k, pl.ds(row * half, band), lane] for row in (0, 2)], 0
                )

            return pick

        for quarter in range(4):
            for place in range(2):
                units.append(
                    (
                        filler(sampled(place * 512), lanes_of(m.gc2, quarter)),
                        out_lanes(m.shortcut.at[place], quarter),
                    )
                )

    def add_squeezer():
        for place in range(4):
            units.append(
                (filler(rows_from(m.uh, place * 512), whole(m.ga2)), m.squeezer.at[place])
            )

    def add_strider():
        def tapped(dy, base):
            def pick(k, start):
                lane = pl.ds(base + start, 256)
                return jnp.concatenate([m.pc[k, dy + 2 * i, :, lane] for i in range(2)], 0)

            return pick

        def grads(k):
            return jnp.concatenate([m.gb[k, i, :, 0:512] for i in range(2)], 0)

        for dy in range(3):
            for dx in range(3):
                units.append((filler(tapped(dy, dx * 512), grads), m.strider.at[dy * 3 + dx]))

    def add_narrower():
        def grads(k):
            return jnp.concatenate([m.uh[k, :, i * 512 : i * 512 + 512] for i in range(4)], 0)

        for place in range(2):
            units.append(
                (filler(rows_from(m.xb, place * 512), grads), m.narrower.at[place])
            )

    def one_hot(shape, places):
        row = lax.broadcasted_iota(jnp.int32, shape, 0)
        lane = lax.broadcasted_iota(jnp.int32, shape, 1)
        return jnp.where(row == places(lane), 1.0, 0.0).astype(jnp.bfloat16)

    def add_pack():
        def put_block(block, value):
            for lt in range(4):
                m.xs[lt * 2 + block // 4, pl.ds(block % 4 * 2, 2)] = value[
                    :, lt * 128 : lt * 128 + 128
                ].reshape(2, 4, 16, 128)

        spread = []
        for q in range(4):

            def places(lane):
                inside = lax.rem(lane, 128) - q * 32
                return jnp.where(
                    (inside >= 0) & (inside < 32), lax.div(lane, 128) * 32 + inside, -1
                )

            spread.append(one_hot((128, 512), places))

        def group_grads(k, q):
            return [
                lax.dot_general(
                    m.gk[p, k], spread[q], (((1,), (0,)), ((), ())), preferred_element_type=jnp.float32
                ).astype(jnp.bfloat16)
                for p in range(2)
            ]

        for block in range(7):
            value = None
            for q in range(4):
                tap = q * 7 + block
                if tap < 27:
                    k, dy, dx = tap // 9, tap % 9 // 3, tap % 3
                    lane = slice(dx * 128, dx * 128 + 128)
                    left = [
                        jnp.concatenate([m.mixed[p, k, i + dy, :, lane] for i in range(2)], 0)
                        for p in range(2)
                    ]
                    term = outer(left, group_grads(k, q))
                    value = term if value is None else value + term
            put_block(block, value)

        def fold(ref, size, count):
            total = None
            for j in range(count):

                def places(lane):
                    inside = lax.rem(lane, 128) - j * 8
                    return jnp.where((inside >= 0) & (inside < 8), lax.div(lane, 128) * 8 + inside, -1)

                term = small_product(ref[j * size : j * size + size, :], one_hot((32, 512), places))
                total = term if total is None else total + term
            return total

        def tap_places(lane):
            inside = lax.rem(lane, 128)
            return jnp.where(inside < 96, lax.div(lane, 128) * 96 + inside, -1)

        temporal = small_product(
            jnp.concatenate([m.temporal[...], jnp.zeros((5, 384), jnp.float32)], 0),
            one_hot((384, 512), tap_places),
        )
        put_block(
            7,
            jnp.concatenate(
                [
                    fold(m.condenser, 32, 16),
                    fold(m.stencil, 24, 12),
                    m.exciter[...],
                    temporal,
                    jnp.zeros((32, 512), jnp.float32),
                ],
                0,
            ),
        )

        for place in range(2):

            def fill(target, which, place=place):
                for lt in range(4):
                    value = m.xs[lt * 2 + place, pl.ds(which * 4, 4)]
                    target[:, :, :, lt * 128 : lt * 128 + 128] = blocks(value.reshape(256, 128))

            units.append((fill, m.pack.at[place]))


    clear()

    @pl.when(r == 0)
    def _():
        m.a[0] = jnp.zeros(m.a.shape[1:], jnp.float32)

    @pl.when(r == rows - 1)
    def _():
        m.b_halo[...] = jnp.zeros_like(m.b_halo)
        m.back_halo[...] = jnp.zeros_like(m.back_halo)

    for buffers in (m.source, m.grad_pad):
        for k in range(3):

            @pl.when(r == 0)
            def _():
                buffers[k, 0] = jnp.zeros(buffers.shape[2:], jnp.float32)

            @pl.when(r == rows - 1)
            def _():
                buffers[k, 3] = jnp.zeros(buffers.shape[2:], jnp.float32)

    def reduce_row(row):
        @pl.loop(0, depth // 2)
        def _(pair):
            for parity in range(2):
                spot = pl.ds(parity, 8, stride=2)
                place = pl.multiple_of(row * half + parity * band + pair * 16, 16)
                for k, lane in enumerate(lanes):
                    value = jnp.concatenate(
                        [m.xs[k, 2 * pair, row, spot, :], m.xs[k, 2 * pair + 1, row, spot, :]], 0
                    )
                    put(m.xb, (pl.ds(place, 16), lane), value)

        place = pl.ds(pl.multiple_of(row * half, half), half)
        result = product(jnp.concatenate([m.xb[0, place, :], m.xb[1, place, :]], 0), m.wn[...])
        m.a[1 + row] = result.reshape(2, band, 512)
        collect(0, result)
        collect(1, result * result)

    for copy in x_loads[0]:
        copy.wait()
    wn_load.wait()
    reduce_row(3)

    @pl.when(below)
    def _():
        send(m.a.at[4], m.a.at[0], m.halo_s.at[0], m.halo_r.at[0], (f, r + 1))

    for copies in x_loads[1:]:
        for copy in copies:
            copy.wait()

    @pl.loop(0, 3)
    def _(row):
        reduce_row(row)

    total = Sum([collected(0), collected(1)])
    clear()
    wsk_load.wait()

    def shortcut_tile(cols):
        lhs = jnp.concatenate(
            [m.xb[k, pl.ds(row * half, band), :] for k in range(2) for row in (0, 2)], 0
        )
        result = product(lhs, m.wsk[:, cols])
        m.s[:, cols] = result
        collect(2, result, cols)
        collect(3, result * result, cols)

    @pl.loop(0, 2)
    def _(place):
        shortcut_tile(pl.ds(pl.multiple_of(place * 512, 512), 512))

    total.middle()

    @pl.loop(2, 4)
    def _(place):
        shortcut_tile(pl.ds(pl.multiple_of(place * 512, 512), 512))

    totals, squares = total.finish(512, 512)
    settle(0, totals, squares, number_full, m.gain[0:1], m.bias[0:1])

    def activate(row, keep):
        @chunks(band, 32)
        def _(spot):
            for parity in range(2):
                value = silu(affine(0, m.a[row, parity, spot, :]))
                if keep is not None:
                    value = value * keep
                if parity == 0:
                    put(m.pc, (row, spot, slice(512, 1024)), value)
                else:
                    put(m.pc, (row, spot, slice(1024, 1536)), value)
                    put(m.pc, (row, spot, slice(0, 512)), moved_down(value))

    @pl.loop(1, 5)
    def _(row):
        activate(row, None)

    @pl.when(above)
    def _():
        pltpu.make_async_remote_copy(
            src_ref=m.a.at[4],
            dst_ref=m.a.at[0],
            send_sem=m.halo_s.at[0],
            recv_sem=m.halo_r.at[0],
            device_id=(f, lax.rem(r + 1, rows)),
            device_id_type=MESH,
        ).wait_recv()

    activate(0, above_one)
    ks_load.wait()

    def strided(dy):
        return product(
            jnp.concatenate([m.pc[k, dy + 2 * i] for k in range(2) for i in range(2)], 0), m.ks[dy]
        )

    m.b[...] = strided(0)
    m.b[...] = m.b[...] + strided(1)
    result = m.b[...] + strided(2)
    m.b[...] = result
    collect(0, result)
    collect(1, result * result)

    @pl.when(above)
    def _():
        send(
            m.b.at[pl.ds(0, band)], m.b_halo, m.halo_s.at[1], m.halo_r.at[1], (f, r - 1)
        )

    totals, squares, totals_p, squares_p = Sum(
        [collected(0), collected(1), collected(2, wide), collected(3, wide)]
    ).all(512, 512, wide, wide)
    clear()
    settle(1, totals, squares, number_half, m.gain[1:2], m.bias[1:2])
    settle(5, totals_p, squares_p, number_half, m.wide_gain[1:2], m.wide_bias[1:2])

    @chunks(half, 32)
    def _(spot):
        put(m.h2, (spot, slice(None)), silu(affine(1, m.b[spot, :])))

    we_load.wait()

    @column_tiles
    def _(cols):
        result = product(jnp.concatenate([m.h2[0], m.h2[1]], 0), m.we[:, cols])
        m.c[:, cols] = result
        collect(0, result, cols)
        collect(1, result * result, cols)

    totals, squares = Sum([collected(0, wide), collected(1, wide)]).all(wide, wide)
    clear()
    settle(4, totals, squares, number_half, m.wide_gain[0:1], m.wide_bias[0:1])

    def first_sum(spot, cols):
        return affine(4, m.c[spot, cols], cols) + affine(5, m.s[spot, cols], cols)

    @column_tiles
    def _(cols):
        @chunks(half, 32)
        def _(spot):
            value = silu(first_sum(spot, cols))
            put(m.uh, (spot, cols), value)

    wcr_load.wait()
    result = product(jnp.concatenate([m.uh[0], m.uh[1]], 0), m.wcr[...])
    m.d[...] = result
    collect(0, result)
    collect(1, result * result)
    totals, squares = Sum([collected(0), collected(1)]).all(512, 512)
    clear()
    settle(2, totals, squares, number_half, m.gain[2:3], m.bias[2:3])

    @chunks(half, 32)
    def _(spot):
        m.hid[spot, :] = silu(affine(2, m.d[spot, :]))

    m.edge[...] = jnp.zeros_like(m.edge)
    for row in range(2):
        block = m.hid[row * band : row * band + band, :]
        column = lax.rem(lax.broadcasted_iota(jnp.int32, block.shape, 0), 8)
        for k, value in enumerate(
            (block, jnp.where(column == 0, block, 0.0), jnp.where(column == 7, block, 0.0))
        ):
            m.edge[k, row, :depth] = jnp.sum(value.reshape(depth, 8, 512), axis=1)
    pad = m.edge.shape[2]
    reduced = small_product(m.edge[...].reshape(6 * pad, 512), m.wer[...])

    def part(kind, row):
        start = (kind * 2 + row) * pad
        return reduced[start : start + pad]

    taps = []
    for dy in range(3):
        for dx in range(3):
            by_row = []
            for row in range(2):
                value = part(0, row)
                if dx == 0:
                    value = value - part(2, row)
                if dx == 2:
                    value = value - part(1, row)
                by_row.append(value)
            if dy == 0:
                by_row[1] = by_row[1] * below_one
            if dy == 2:
                by_row[0] = by_row[0] * above_one
            taps.append(by_row[0] + by_row[1])
    taps.append(jnp.zeros((pad, 96), jnp.float32))
    m.tap_in[...] = jnp.concatenate(taps, 1)

    def rows_sum(source, slots, near, near_slots, toward, sems):
        copies = []
        for step in range(1, rows):
            copies.append(
                send(
                    source,
                    slots.at[step],
                    m.rows_s.at[sems, step],
                    m.rows_r.at[sems, step],
                    (f, lax.rem(r + step, rows)),
                )
            )
        for step in range(rows):
            copies.append(
                send(
                    source.at[near],
                    near_slots.at[step],
                    m.rows_s.at[sems, rows + step],
                    m.rows_r.at[sems, rows + step],
                    (toward, lax.rem(r + step, rows)),
                )
            )
        slots[0] = source[...]
        for copy in copies:
            copy.wait_recv()
        total = slots[r]
        other_total = near_slots[r]
        for other in range(1, rows):
            spot = lax.rem(r + rows - other, rows)
            total = total + slots[spot]
            other_total = other_total + near_slots[spot]
        for copy in copies:
            copy.wait_send()
        return total, other_total

    current, later = rows_sum(
        m.tap_in, m.tap_slots, pl.ds(0, 8), m.tap_near, before_f, 0
    )
    place = lax.broadcasted_iota(jnp.int32, current.shape, 0)
    follow = pltpu.roll(current, pad - 1, 0)
    follow = jnp.where(place == depth - 1, later[0:1], follow)
    after16 = m.after16[...]
    before16 = m.before16[...]
    follow = jnp.where(place < depth, follow, 0.0) * jnp.concatenate([after16] * 3, 1)
    m.follow[...] = follow
    area = float(16 * rows)
    pooled = (
        (small_product(follow[:, :288], m.kst[...]) - current[:, 128:160])
        * after16[:, :32]
        / area
    )
    m.pooled[...] = pooled
    m.gate[...] = jax.nn.sigmoid(small_product(pooled, m.wex[...]))
    for frame in range(depth):
        m.gate_all[frame * 8 : frame * 8 + 8, :] = jnp.broadcast_to(
            1.0 + m.gate[frame : frame + 1, :], (8, 512)
        )

    def halo(field, sems, pumps=0):
        own, first, last = pl.ds(8, band), pl.ds(8, 8), pl.ds(band, 8)
        low, high = pl.ds(0, 8), pl.ds(band + 8, 8)
        moves = [
            (field.at[pl.ds(1, 2), last], field.at[pl.ds(1, 2), low], (after_f, r), None, None),
            (field.at[pl.ds(1, 2), first], field.at[pl.ds(1, 2), high], (before_f, r), None, None),
            (field.at[2, own], field.at[0, own], (f, r + 1), below, above),
            (field.at[1, own], field.at[3, own], (f, r - 1), above, below),
            (field.at[2, last], field.at[0, low], (after_f, r + 1), below, above),
            (field.at[1, last], field.at[3, low], (after_f, r - 1), above, below),
            (field.at[2, first], field.at[0, high], (before_f, r + 1), below, above),
            (field.at[1, first], field.at[3, high], (before_f, r - 1), above, below),
        ]
        copies = []
        for k, (source, target, device, able, arriving) in enumerate(moves):
            copies.append(
                pltpu.make_async_remote_copy(
                    src_ref=source,
                    dst_ref=target,
                    send_sem=m.ring_s.at[sems, k],
                    recv_sem=m.ring_r.at[sems, k],
                    device_id=device,
                    device_id_type=MESH,
                )
            )
        for copy, move in zip(copies, moves):
            if move[3] is None:
                copy.start()
            else:
                pl.when(move[3])(copy.start)
        pump(pumps)
        for copy, move in zip(copies, moves):
            if move[4] is None:
                copy.wait_recv()
            else:
                pl.when(move[4])(copy.wait_recv)
        for copy, move in zip(copies, moves):
            if move[3] is None:
                copy.wait_send()
            else:
                pl.when(move[3])(copy.wait_send)

    own = pl.ds(8, band)
    previous, following = pl.ds(0, band), pl.ds(16, band)
    before_band = m.before_band[...]
    after_band = m.after_band[...]

    def sides(value):
        return jnp.concatenate([moved_down(value), value, moved_up(value)], 1)

    m.merged[:, 0:128] = jnp.concatenate(
        [m.hid[i * band : i * band + band, 0:128] * m.gate_all[:, 0:128] for i in range(2)], 0
    )
    kern_load.wait()
    for k in range(3):
        cols = slice((k + 1) * 128, (k + 2) * 128)
        for i in range(2):
            rows_i = slice(i * band, i * band + band)
            value = m.hid[rows_i, cols] * m.gate_all[:, cols]
            if k > 0:
                value = value + m.merged[rows_i, k * 128 : (k + 1) * 128]
            m.source[k, 1 + i, own] = value
        halo(m.source.at[k], k)
        tap = [m.taps[i : i + 1, k * 128 : (k + 1) * 128] for i in range(3)]
        for i in range(4):
            mixed = (
                tap[0] * before_band * m.source[k, i, previous]
                + tap[1] * m.source[k, i, own]
                + tap[2] * after_band * m.source[k, i, following]
            )
            put(m.mixed, (k, i), sides(mixed))
        result = jnp.zeros((half, 128), jnp.float32)
        for dy in range(3):
            lhs = jnp.concatenate([m.mixed[p, k, i + dy] for p in range(2) for i in range(2)], 0)
            result = result + product(lhs, m.kern[k, dy])
        m.merged[:, cols] = result

    result = m.merged[...]
    collect(0, result)
    collect(1, result * result)
    totals, squares = Sum([collected(0), collected(1)]).all(512, 512)
    clear()
    settle(3, totals, squares, number_half, m.gain[3:4], m.bias[3:4])

    @chunks(half, 32)
    def _(spot):
        put(m.squashed, (spot, slice(None)), silu(affine(3, m.merged[spot, :])))

    wce_load.wait()

    @column_tiles
    def _(cols):
        result = product(jnp.concatenate([m.squashed[0], m.squashed[1]], 0), m.wce[:, cols])
        m.e[:, cols] = result
        collect(0, result, cols)
        collect(1, result * result, cols)

    totals, squares = Sum([collected(0, wide), collected(1, wide)]).all(wide, wide)
    clear()
    settle(6, totals, squares, number_half, m.wide_gain[2:3], m.wide_bias[2:3])

    for copy in slope_loads:
        copy.wait()

    @column_tiles
    def _(cols):
        for row in range(2):

            @pl.loop(0, depth // 4)
            def _(part_place):
                block = pl.ds(pl.multiple_of(part_place * 4, 4), 4)
                spot = pl.ds(pl.multiple_of(row * band + part_place * 32, 32), 32)
                raw = m.e[spot, cols]
                value = (
                    affine(6, raw, cols)
                    + m.uh[0, spot, cols].astype(jnp.float32)
                    + m.uh[1, spot, cols].astype(jnp.float32)
                )
                logistic = jax.nn.sigmoid(value)
                grads = m.slope[row, block, :, cols].reshape(32, 512) * (
                    logistic * (1.0 + value * (1.0 - logistic))
                )
                m.slope[row, block, :, cols] = (value * logistic).reshape(4, 8, 512)
                m.d2[spot, cols] = grads
                collect(0, grads, cols)
                collect(1, grads * normed(6, raw, cols), cols)

    stores = []

    def store(source, target):
        copy = pltpu.make_async_copy(source, target, m.store_sem.at[len(stores)])
        copy.start()
        stores.append(copy)

    for row in range(2):
        store(m.slope.at[row], m.layer_output.at[:, row])

    bias_grad, gain_grad = Sum([collected(0, wide), collected(1, wide)]).all(wide, wide)
    clear()
    settle_back(6, bias_grad, gain_grad, number_half)
    m.baselines[2:3] = bias_grad
    m.amplitudes[2:3] = gain_grad

    @column_tiles
    def _(cols):
        @chunks(half, 32)
        def _(spot):
            put(m.gc2, (spot, cols), field_grad(6, m.d2[spot, cols], m.e[spot, cols], cols))


    def back_through(pair, weights, raw, k):
        m.back[...] = product(jnp.concatenate([pair[0], pair[1]], 0), weights[...], True)

        @chunks(half, 32)
        def _(spot):
            value = raw[spot, :]
            grads = m.back[spot, :] * slope(affine(k, value))
            m.back[spot, :] = grads
            collect(0, grads)
            collect(1, grads * normed(k, value))

    back_through(m.gc2, m.wce, m.merged, 3)
    add_restorer()
    total = Sum([collected(0), collected(1)])
    pump(PUMPS[0])
    bias_grad, gain_grad = total.all(512, 512)
    clear()
    settle_back(3, bias_grad, gain_grad, number_half)
    m.biasing[3:4] = bias_grad
    m.scaling[3:4] = gain_grad
    merged_grad = field_grad(3, m.back[...], m.merged[...])
    m.eg[...] = merged_grad

    for k in (2, 1, 0):
        cols = slice((k + 1) * 128, (k + 2) * 128)
        grads = m.eg[:, cols]
        if k < 2:
            grads = grads + m.eg[:, (k + 2) * 128 : (k + 3) * 128]
        put(m.gk, (k,), grads)
        for i in range(2):
            m.grad_pad[k, 1 + i, own] = grads[i * band : i * band + band]
        halo(m.grad_pad.at[k], 3 + k, PUMPS[1 + k])
        for i in range(4):
            put(m.grad_sides, (i,), sides(m.grad_pad[k, i]))
        result = jnp.zeros((2 * (band + 16), 128), jnp.float32)
        for dy in range(3):
            lhs = jnp.concatenate([m.grad_sides[p, i + dy] for p in range(2) for i in range(2)], 0)
            for dx in range(3):
                result = result + product(
                    lhs[:, dx * 128 : dx * 128 + 128],
                    m.kern[k, 2 - dy, (2 - dx) * 128 : (3 - dx) * 128, :],
                    True,
                )
        span = band + 16
        tap = [m.taps[i : i + 1, k * 128 : (k + 1) * 128] for i in range(3)]
        tap_grads = [0.0, 0.0, 0.0]
        for i in range(2):
            m.mixed_grad[i] = result[i * span : i * span + span]
            middle = m.mixed_grad[i, own]
            for j, value in enumerate(
                (
                    middle * before_band * m.source[k, 1 + i, previous],
                    middle * m.source[k, 1 + i, own],
                    middle * after_band * m.source[k, 1 + i, following],
                )
            ):
                tap_grads[j] = tap_grads[j] + jnp.sum(value, axis=0, keepdims=True)
            m.eg[i * band : i * band + band, cols] = (
                tap[2] * before_band * m.mixed_grad[i, previous]
                + tap[1] * middle
                + tap[0] * after_band * m.mixed_grad[i, following]
            )
        for j in range(3):
            m.temporal[j : j + 1, k * 128 : (k + 1) * 128] = tap_grads[j]


    gate = m.gate[...]
    m.gate_part[...] = jnp.zeros_like(m.gate_part)
    touched = m.eg[...] * m.hid[...]
    touched = jnp.sum(touched.reshape(2 * depth, 8, 512), axis=1)
    m.gate_part[:depth] = touched[:depth] + touched[depth:]
    m.gate_part[...] = m.gate_part[...] * gate * (1.0 - gate)
    m.exciter[...] = small_outer(m.pooled[...], m.gate_part[...])
    current, earlier = rows_sum(
        m.gate_part, m.gate_slots, pl.ds(pad - 8, 8), m.gate_near, after_f, 1
    )
    place = lax.broadcasted_iota(jnp.int32, current.shape, 0)
    last_row = depth - 1 - (pad - 8)
    shifted = jnp.where(place == 0, earlier[last_row : last_row + 1], pltpu.roll(current, 1, 0))
    pooled_grads = small_product(jnp.concatenate([current, shifted], 0), m.wex[...], True) / area
    motion = pooled_grads[:pad] * after16[:, :32]
    motion_before = pooled_grads[pad:] * before16[:, :32]
    m.stencil[...] = small_outer(m.follow[:, :288], motion) * (1.0 / rows)
    spread = small_product(motion_before, m.kst[...], True)

    def tap_value(dy, dx):
        start = (dy * 3 + dx) * 32
        return spread[:, start : start + 32]

    values = []
    by_row = []
    for row in range(2):
        columns = []
        for dx in range(3):
            if row == 0:
                value = tap_value(0, dx) + tap_value(1, dx)
                value = value + tap_value(2, dx) * above_one
            else:
                value = tap_value(1, dx) + tap_value(2, dx)
                value = value + tap_value(0, dx) * below_one
            columns.append(value)
        by_row.append(columns)
    for kind in range(3):
        for row in range(2):
            d0, d1, d2 = by_row[row]
            value = (d0 + d1 + d2, d0 + d1, d1 + d2)[kind]
            values.append(value - motion)
    reduced_grad = jnp.concatenate(values, 0)
    edges = jnp.concatenate([m.edge[0] - m.edge[1] - m.edge[2], m.edge[1], m.edge[2]], 0)
    m.condenser[...] = small_outer(edges.reshape(6 * pad, 512), reduced_grad)
    m.edge_back[...] = small_product(reduced_grad, m.wer[...], True).reshape(3, 2, pad, 512)

    for row in range(2):

        @pl.loop(0, depth)
        def _(frame):
            spot = pl.ds(pl.multiple_of(row * band + frame * 8, 8), 8)
            line = pl.ds(frame, 1)
            column = lax.broadcasted_iota(jnp.int32, (8, 512), 0)
            extra = jnp.where(
                column == 0,
                m.edge_back[1, row, line, :],
                jnp.where(column == 7, m.edge_back[2, row, line, :], m.edge_back[0, row, line, :]),
            )
            raw = m.d[spot, :]
            grads = m.eg[spot, :] * m.gate_all[pl.ds(pl.multiple_of(frame * 8, 8), 8), :] + extra
            grads = grads * slope(affine(2, raw))
            m.back[spot, :] = grads
            collect(0, grads)
            collect(1, grads * normed(2, raw))

    total = Sum([collected(0), collected(1)])
    add_pack()
    pump(PUMPS[4])
    bias_grad, gain_grad = total.all(512, 512)
    clear()
    settle_back(2, bias_grad, gain_grad, number_half)
    m.biasing[2:3] = bias_grad
    m.scaling[2:3] = gain_grad

    @chunks(half, 32)
    def _(spot):
        put(m.ga2, (spot, slice(None)), field_grad(2, m.back[spot, :], m.d[spot, :]))


    @column_tiles
    def _(cols):
        m.e[:, cols] = product(jnp.concatenate([m.ga2[0], m.ga2[1]], 0), m.wcr[cols, :], True)

        @chunks(half, 32)
        def _(spot):
            grads = (m.d2[spot, cols] + m.e[spot, cols]) * slope(first_sum(spot, cols))
            m.d2[spot, cols] = grads
            collect(0, grads, cols)
            collect(1, grads * normed(4, m.c[spot, cols], cols), cols)
            collect(2, grads * normed(5, m.s[spot, cols], cols), cols)

    add_squeezer()
    total = Sum([collected(0, wide), collected(1, wide), collected(2, wide)])
    pump(PUMPS[5])
    total.middle()
    pump(PUMPS[6])
    bias_grad, gain_c, gain_p = total.finish(wide, wide, wide)
    clear()
    settle_back(4, bias_grad, gain_c, number_half)
    settle_back(5, bias_grad, gain_p, number_half)
    for k in range(2):
        m.baselines[k : k + 1] = bias_grad
    m.amplitudes[0:1] = gain_c
    m.amplitudes[1:2] = gain_p

    begin_all_but(0)

    @column_tiles
    def _(cols):
        @chunks(half, 32)
        def _(spot):
            grads = m.d2[spot, cols]
            put(m.uh, (spot, cols), field_grad(4, grads, m.c[spot, cols], cols))
            put(m.gc2, (spot, cols), field_grad(5, grads, m.s[spot, cols], cols))

    back_through(m.uh, m.we, m.b, 1)

    @pl.when(above)
    def _():
        send(
            m.back.at[pl.ds(0, band)], m.back_halo, m.halo_s.at[2], m.halo_r.at[2], (f, r - 1)
        )

    total = Sum([collected(0), collected(1)])
    clear()
    add_widener()
    add_shortcut()
    pump(PUMPS[7])

    for cols in (slice(0, 512), slice(512, 1024)):
        if cols.start:
            total.middle()
            pump(PUMPS[8])
        m.d2[:, cols] = product(jnp.concatenate([m.gc2[0], m.gc2[1]], 0), m.wsk[cols, :], True)

    bias_grad, gain_grad = total.finish(512, 512)
    settle_back(1, bias_grad, gain_grad, number_half)
    m.biasing[1:2] = bias_grad
    m.scaling[1:2] = gain_grad

    def strided_grad(row, spot, value):
        put(m.gb, (row, spot, slice(0, 512)), value)
        put(m.gb, (row, spot, slice(512, 1024)), moved_up(value))

    for row in range(2):

        @chunks(band, 32)
        def _(spot):
            place = pl.ds(pl.multiple_of(row * band + spot.start, 32), 32)
            strided_grad(row, spot, field_grad(1, m.back[place, :], m.b[place, :]))

    @pl.when(below)
    def _():
        for k, (source, target) in enumerate(((m.b, m.b_halo), (m.back, m.back_halo))):
            pltpu.make_async_remote_copy(
                src_ref=source.at[pl.ds(0, band)],
                dst_ref=target,
                send_sem=m.halo_s.at[1 + k],
                recv_sem=m.halo_r.at[1 + k],
                device_id=(f, lax.rem(r + 1, rows)),
                device_id_type=MESH,
            ).wait_recv()

    @chunks(band, 32)
    def _(spot):
        value = field_grad(1, m.back_halo[spot, :], m.b_halo[spot, :])
        strided_grad(2, spot, value * below_one)


    add_strider()
    pump(PUMPS[9])

    def gb_rows(first, variant):
        lanes = slice(variant * 512, variant * 512 + 512)
        return jnp.concatenate([m.gb[k, first + i, :, lanes] for k in range(2) for i in range(2)], 0)

    def tap_weights(dy, dx):
        return m.ks[dy, dx * 512 : dx * 512 + 512, :]

    @pl.when(above)
    def _():
        for k, source in enumerate((m.b, m.back)):
            pltpu.make_async_remote_copy(
                src_ref=source.at[pl.ds(0, band)],
                dst_ref=m.back_halo,
                send_sem=m.halo_s.at[1 + k],
                recv_sem=m.halo_r.at[1 + k],
                device_id=(f, lax.rem(r + 1, rows)),
                device_id_type=MESH,
            ).wait_send()

    def ha_rows(parity, spot):
        return pl.ds(pl.multiple_of(parity * band + spot.start, 32), 32)

    plan = {
        (0, 0): [(0, 0, 1, 1)],
        (1, 0): [(0, 0, 1, 2), (0, 1, 1, 0)],
        (0, 1): [(0, 0, 2, 1), (1, 0, 0, 1)],
        (1, 1): [(0, 0, 2, 2), (1, 0, 0, 2), (0, 1, 2, 0), (1, 1, 0, 0)],
    }
    for (parity, odd), terms in plan.items():
        result = None
        for first, variant, dy, dx in terms:
            value = product(gb_rows(first, variant), tap_weights(dy, dx), True)
            result = value if result is None else result + value
        m.back[...] = result
        for i in range(2):
            row = 2 * i + odd

            @chunks(band, 32)
            def _(spot):
                place = pl.ds(pl.multiple_of(i * band + spot.start, 32), 32)
                raw = m.a[1 + row, parity, spot, :]
                grads = m.back[place, :] * slope(affine(0, raw))
                m.e[ha_rows(parity, spot), row * 512 : row * 512 + 512] = grads
                collect(0, grads)
                collect(1, grads * normed(0, raw))

    total = Sum([collected(0), collected(1)])
    pump(PUMPS[10])
    total.middle()
    pump(PUMPS[11])
    bias_grad, gain_grad = total.finish(512, 512)
    settle_back(0, bias_grad, gain_grad, number_full)
    begin_all_but(17)
    m.biasing[0:1] = bias_grad
    m.scaling[0:1] = gain_grad

    @pl.loop(0, 4)
    def _(row):
        for parity in range(2):

            @chunks(band, 32)
            def _(spot):
                lane = pl.ds(pl.multiple_of(row * 512, 512), 512)
                value = field_grad(
                    0, m.e[ha_rows(parity, spot), lane], m.a[1 + row, parity, spot, :]
                )
                put(m.uh, (ha_rows(parity, spot), lane), value)

        lane = pl.ds(pl.multiple_of(row * 512, 512), 512)
        lhs = jnp.concatenate([m.uh[0, :, lane], m.uh[1, :, lane]], 0)
        for part_cols in (slice(0, 512), slice(512, 1024)):
            result = product(lhs, m.wn[part_cols, :], True)
            even = jnp.where(lax.rem(row, 2) == 0, 1.0, 0.0)
            shortcut = m.d2[pl.ds(pl.multiple_of((row // 2) * band, band), band), part_cols]
            for parity in range(2):
                value = result[parity * band : parity * band + band]
                if parity == 0:
                    value = value + shortcut * even
                for frame in range(depth):
                    for k in range(4):
                        m.xs[
                            part_cols.start // 128 + k, frame, row, pl.ds(parity, 8, stride=2), :
                        ] = value[frame * 8 : frame * 8 + 8, k * 128 : k * 128 + 128]

    for row in range(4):
        for k, lane in enumerate(lanes):
            store(m.xs.at[k, :, row], m.pixels.at[:, row, :, lane])
    add_narrower()
    pump(None)
    for copy in stores:
        copy.wait()

    @pl.when(below)
    def _():
        pltpu.make_async_remote_copy(
            src_ref=m.a.at[4],
            dst_ref=m.a.at[0],
            send_sem=m.halo_s.at[0],
            recv_sem=m.halo_r.at[0],
            device_id=(f, lax.rem(r + 1, rows)),
            device_id_type=MESH,
        ).wait_send()


def chain(
    x, before, after, wn, ks, we, wsk, wcr, wer, kst, wex, taps, kern, wce, gain, bias, wide_gain,
    wide_bias, slopes, call,
):
    frames, rows = lax.axis_size("frames"), lax.axis_size("rows")
    depth = x.shape[0]
    band, pad = depth * 8, -(-depth // 16) * 16
    half = 2 * band
    span = band + 16
    levels = int(math.log2(frames // 2))
    b_count = 2 ** (levels // 2)
    a_count = frames // 2 // b_count
    thin = 512 // frames
    blocks = (2, a_count, b_count, thin)
    unit = (a_count, b_count, thin, 512)
    copies = 6 + 2 * (a_count + b_count - 2)
    hbm, vmem = pl.BlockSpec(memory_space=pl.ANY), pl.BlockSpec(memory_space=pltpu.VMEM)

    def masks(mask):
        mask = mask.reshape(depth, 1)
        tall = jnp.broadcast_to(jnp.pad(mask, ((0, pad - depth), (0, 0))), (pad, 128))
        return tall, jnp.broadcast_to(mask[:, :, None], (depth, 8, 128)).reshape(band, 128)

    before16, before_band = masks(before)
    after16, after_band = masks(after)
    inputs = dict(
        x=(x, hbm), slope_h=(slopes, hbm), wn_h=(wn, hbm), wsk_h=(wsk, hbm), ks_h=(ks, hbm),
        we_h=(we, hbm), wcr_h=(wcr, hbm), wce_h=(wce, hbm), kern_h=(kern, hbm), wer=(wer, vmem),
        kst=(kst, vmem), wex=(wex, vmem), taps=(taps, vmem), gain=(gain, vmem), bias=(bias, vmem),
        wide_gain=(wide_gain, vmem), wide_bias=(wide_bias, vmem), before16=(before16, vmem),
        after16=(after16, vmem), before_band=(before_band, vmem), after_band=(after_band, vmem),
    )

    def wide_of(*shape):
        return jax.ShapeDtypeStruct(shape, jnp.float32)

    kept = dict(
        xb=(2, 4 * half, 1024), pc=(2, 5, band, 1536), h2=(2, half, 512), uh=(2, half, 2048),
        squashed=(2, half, 512), mixed=(2, 3, 4, band, 384), gc2=(2, half, 2048),
        gk=(2, 3, half, 128), ga2=(2, half, 512),
        gb=(2, 3, band, 1024),
    )
    outputs = dict(
        layer_output=(wide_of(depth, 2, 8, 2048), hbm), pixels=(wide_of(depth, 4, 16, 1024), hbm),
        scaling=(wide_of(4, 512), vmem), biasing=(wide_of(4, 512), vmem),
        amplitudes=(wide_of(3, 2048), vmem), baselines=(wide_of(3, 2048), vmem),
        narrower=(wide_of(2, *blocks, 128), hbm), strider=(wide_of(9, *blocks, 128), hbm),
        widener=(wide_of(*blocks, 512), hbm), shortcut=(wide_of(2, *blocks, 512), hbm),
        squeezer=(wide_of(4, *blocks, 128), hbm), restorer=(wide_of(*blocks, 512), hbm),
        pack=(wide_of(2, *blocks, 128), hbm),
    )

    def f32(*shape):
        return pltpu.VMEM(shape, jnp.float32)

    def b16(*shape):
        return pltpu.VMEM(shape, jnp.bfloat16)

    def sems(*shape):
        return pltpu.SemaphoreType.DMA(shape)

    scratch = dict(
        wn=b16(1024, 512), wsk=b16(1024, 2048), ks=b16(3, 1536, 512), we=b16(512, 2048),
        wcr=b16(2048, 512), wce=b16(512, 2048), kern=b16(3, 3, 384, 128),
        xs=f32(8, depth, 4, 16, 128), a=f32(5, 2, band, 512), b=f32(half, 512), c=f32(half, 2048),
        s=f32(half, 2048), d=f32(half, 512), hid=f32(half, 512),
        merged=f32(half, 512), e=f32(half, 2048),
        slope=f32(2, depth, 8, 2048), d2=f32(half, 2048), back=f32(half, 512), eg=f32(half, 512),
        b_halo=f32(band, 512),
        back_halo=f32(band, 512), source=f32(3, 4, span, 128), grad_pad=f32(3, 4, span, 128),
        mixed_grad=f32(2, span, 128), grad_sides=b16(2, 4, span, 384), gate_all=f32(band, 512),
        edge=f32(3, 2, pad, 512), edge_back=f32(3, 2, pad, 512), gate=f32(pad, 512),
        gate_part=f32(pad, 512), pooled=f32(pad, 32), follow=f32(pad, 384), tap_in=f32(pad, 384),
        tap_slots=f32(rows, pad, 384), tap_near=f32(rows, 8, 384), gate_slots=f32(rows, pad, 512),
        gate_near=f32(rows, 8, 512), stat=f32(4, 8, 2048), vec=f32(48, 2048), ar_in=f32(2, 48, 128),
        ar_part=f32(2, 48, 128), ar_out=f32(48, 128), ar_rows_a=f32(rows, 32, 128), ar_rows_b=f32(rows, 48, 128),
        ar_frames_a=f32(frames, 32, 128), ar_frames_b=f32(frames, 48, 128), ar_rs=sems(2, rows), ar_rr=sems(2, rows),
        ar_fs=sems(2, frames), ar_fr=sems(2, frames), rows_s=sems(2, 2 * rows),
        rows_r=sems(2, 2 * rows), ring_s=sems(6, 8), ring_r=sems(6, 8), halo_s=sems(3),
        halo_r=sems(3), condenser=f32(512, 32), stencil=f32(288, 32), exciter=f32(32, 512),
        temporal=f32(3, 384), g_own=f32(2, 5, *unit), g_away=f32(2, 2, *unit),
        g_near=f32(2, 2, *unit), g_first_p=f32(2, b_count - 1, a_count, thin, 512),
        g_first_q=f32(2, a_count - 1, b_count, thin, 512), g_third=f32(2, 2, 2, thin, 128),
        g_fourth=f32(2, 2, thin, 128), g_final=f32(2, 2, thin, 128),
        g_second_p=f32(2, a_count - 1, thin, 512), g_second_q=f32(2, b_count - 1, thin, 512),
        g_send=sems(2, 10, copies), g_recv=sems(2, 10, copies), load_sem=sems(48), store_sem=sems(40),
    )
    for name in kept:
        scratch[name] = b16(*kept[name])
    names = list(inputs) + list(outputs) + list(scratch)
    results = pl.pallas_call(
        lambda *refs: chain_kernel(names, (frames, rows, depth, a_count, b_count), *refs),
        out_shape=[shape for shape, _ in outputs.values()],
        in_specs=[spec for _, spec in inputs.values()],
        out_specs=[spec for _, spec in outputs.values()],
        scratch_shapes=list(scratch.values()),
        compiler_params=pltpu.CompilerParams(
            collective_id=call, has_side_effects=True, vmem_limit_bytes=VMEM_BYTES
        ),
    )(*[value for value, _ in inputs.values()])
    return SimpleNamespace(**dict(zip(outputs, results)))


def shards(
    input_feature_maps,
    sequence_slot_lookup,
    sequence_span_lookup,
    opening_reducer,
    downsampling_filter,
    opening_expander,
    skip_projection,
    closing_reducer,
    excite_reducer,
    excite_spatial_filter,
    excite_expander,
    time_taps,
    spatial_filters,
    closing_expander,
    narrow_norm_gains,
    narrow_norm_biases,
    wide_norm_gains,
    wide_norm_biases,
    loss_slope_wrt_final,
):
    before = (sequence_slot_lookup > 0).astype(jnp.float32)
    after = (sequence_slot_lookup < sequence_span_lookup - 1).astype(jnp.float32)
    k = chain(
        input_feature_maps,
        before,
        after,
        opening_reducer,
        downsampling_filter.reshape(3, 1536, 512),
        opening_expander,
        skip_projection,
        closing_reducer,
        excite_reducer,
        excite_spatial_filter.reshape(288, 32),
        excite_expander,
        time_taps.astype(jnp.float32),
        spatial_filters.reshape(3, 3, 384, 128),
        closing_expander,
        narrow_norm_gains,
        narrow_norm_biases,
        wide_norm_gains,
        wide_norm_biases,
        loss_slope_wrt_final,
        0,
    )
    tail = k.pack.reshape(-1, 128)
    kernels = tail[:896].reshape(7, 128, 4, 32).transpose(2, 0, 1, 3).reshape(-1, 32)[:3456]
    condenser = tail[896:928].reshape(32, 16, 8).transpose(1, 0, 2)
    stencil = tail[928:952, :96].reshape(24, 12, 8).transpose(1, 0, 2)
    return (
        k.layer_output,
        k.pixels,
        k.narrower.reshape(opening_reducer.shape[0], -1),
        k.strider.reshape(downsampling_filter.shape[:-1] + (-1,)),
        k.widener.reshape(opening_expander.shape[0], -1),
        k.shortcut.reshape(skip_projection.shape[0], -1),
        k.squeezer.reshape(closing_reducer.shape[0], -1),
        condenser.reshape(excite_reducer.shape[0], -1),
        stencil.reshape(excite_spatial_filter.shape[:-1] + (-1,)),
        tail[952:984],
        tail[984:987, :96],
        kernels.reshape(spatial_filters.shape[:-1] + (-1,)),
        k.restorer.reshape(closing_expander.shape[0], -1),
        k.scaling,
        k.biasing,
        k.amplitudes,
        k.baselines,
    )


def solution(mesh):
    return jax.shard_map(
        shards,
        mesh=mesh,
        in_specs=(
            P("frames", "rows", None, None),
            P("frames"),
            P("frames"),
            P(),
            P(),
            P(),
            P(),
            P(),
            P(),
            P(),
            P(),
            P(),
            P(),
            P(),
            P(),
            P(),
            P(),
            P(),
            P("frames", "rows", None, None),
        ),
        out_specs=(
            P("frames", "rows", None, None),
            P("frames", "rows", None, None),
            P(None, "rows"),
            P(None, None, None, "rows"),
            P(None, "rows"),
            P(None, "rows"),
            P(None, "rows"),
            P(None, "rows"),
            P(None, None, None, "rows"),
            P(None, "rows"),
            P(None, "rows"),
            P(None, None, None, None, "rows"),
            P(None, "rows"),
            P(),
            P(),
            P(),
            P(),
        ),
        check_vma=False,
    )
```

```python
import itertools
import math
from types import SimpleNamespace

import jax
import jax.numpy as jnp
from jax import lax
from jax.experimental import pallas as pl
from jax.experimental.pallas import tpu as pltpu
from jax.sharding import PartitionSpec as P

MESH = pl.DeviceIdType.MESH
EPSILON = 1e-05
VMEM_BYTES = 65400 * 2**10


def split(value):
    high = value.astype(jnp.bfloat16)
    return high, (value - high.astype(jnp.float32)).astype(jnp.bfloat16)


def put(pair_ref, index, value):
    high, low = split(value)
    pair_ref[(0,) + index] = high
    pair_ref[(1,) + index] = low


def product(stacked, weights, turned=False):
    result = lax.dot_general(
        stacked,
        weights,
        (((1,), (1 if turned else 0,)), ((), ())),
        preferred_element_type=jnp.float32,
    )
    half = result.shape[0] // 2
    return result[:half] + result[half:]


def small_product(value, weights, turned=False):
    return product(jnp.concatenate(split(value), 0), weights, turned)


def small_outer(left, right):
    def one(a, b):
        return lax.dot_general(
            a, b, (((0,), (0,)), ((), ())), preferred_element_type=jnp.float32
        )

    (a, b), (c, d) = split(left), split(right)
    return one(a, c) + one(a, d) + one(b, c)


def slope(value):
    logistic = jax.nn.sigmoid(value)
    return logistic * (1.0 + value * (1.0 - logistic))


def silu(value):
    return value * jax.nn.sigmoid(value)


def folded(value):
    return jnp.sum(value.reshape(-1, 8, value.shape[-1]), axis=0)


def moved_down(value):
    place = lax.broadcasted_iota(jnp.int32, value.shape, 0)
    return jnp.where(lax.rem(place, 8) == 0, 0.0, pltpu.roll(value, 1, 0))


def moved_up(value):
    place = lax.broadcasted_iota(jnp.int32, value.shape, 0)
    return jnp.where(lax.rem(place, 8) == 7, 0.0, pltpu.roll(value, value.shape[0] - 1, 0))


def chunks(total, step):
    def bind(body):
        @pl.loop(0, total // step)
        def _(place):
            body(pl.ds(pl.multiple_of(place * step, step), step))

    return bind


PUMPS = (1, 1, 1, 1, 1, 1, 1, 1, 1, 1, 1, 1)


def chain_kernel(names, dims, *refs):
    frames, rows, depth, a_count, b_count = dims
    m = SimpleNamespace(**dict(zip(names, refs)))
    f = lax.axis_index("frames")
    r = lax.axis_index("rows")
    after_f, before_f = lax.rem(f + 1, frames), lax.rem(f + frames - 1, frames)
    band = depth * 8
    half = 2 * band
    number_half = float(half * frames * rows)
    number_full = 4.0 * number_half
    above, below = r > 0, r < rows - 1
    above_one, below_one = jnp.where(above, 1.0, 0.0), jnp.where(below, 1.0, 0.0)
    wide = 2048

    loads = []

    def load(source, target, sem=None):
        if sem is None:
            sem = m.load_sem.at[len(loads)]
            loads.append(sem)
        copy = pltpu.make_async_copy(source, target, sem)
        copy.start()
        return copy

    def wait_row(row):
        block = m.xs.at[:, :, row]
        pltpu.make_async_copy(block, block, m.row_sem.at[row]).wait()

    lanes = [slice(k * 128, k * 128 + 128) for k in range(8)]

    def load_row(row):
        [
            load(m.x.at[:, row, :, lane], m.xs.at[k, :, row], m.row_sem.at[row])
            for k, lane in enumerate(lanes)
        ]

    for row in (3, 0, 1, 2):
        load_row(row)
    small_loads = [
        load(getattr(m, name + "_h"), getattr(m, name))
        for name in (
            "wer", "kst", "wex", "taps_in", "gain", "bias", "wide_gain", "wide_bias"
        )
    ]
    wn_load = load(m.wn_h, m.wn)
    wsk_load = load(m.wsk_h, m.wsk)
    ks_load = load(m.ks_h, m.ks)
    we_load = load(m.we_h, m.we)
    wcr_load = load(m.wcr_h, m.wcr)
    wce_load = load(m.wce_h, m.wce)
    kern_load = load(m.kern_h, m.kern)
    slope_loads = [load(m.slope_h.at[:, row], m.slope.at[row]) for row in range(2)]

    barrier = pltpu.get_barrier_semaphore()
    partners = [(f, lax.rem(r + step, rows)) for step in range(1, rows)]
    partners += [(lax.rem(f + step, frames), r) for step in range(1, frames)]
    for other in (after_f, before_f):
        partners += [(other, lax.rem(r + step, rows)) for step in range(1, rows)]
    for partner in partners:
        pl.semaphore_signal(barrier, inc=1, device_id=partner, device_id_type=MESH)
    pl.semaphore_wait(barrier, len(partners))

    sent = []

    def send(source, target, send_sem, recv_sem, device):
        copy = pltpu.make_async_remote_copy(
            src_ref=source,
            dst_ref=target,
            send_sem=send_sem,
            recv_sem=recv_sem,
            device_id=device,
            device_id_type=MESH,
        )
        copy.start()
        return copy

    class Sum:
        count = 0

        def __init__(self, pieces):
            self.set = Sum.count % 2
            Sum.count += 1
            place = 0
            for piece in pieces:
                for k in range(piece.shape[1] // 128):
                    m.ar_in[self.set, place : place + 1, :] = piece[:, k * 128 : k * 128 + 128]
                    place += 1
            self.size = -(-place // 8) * 8
            self.copies = self.spread(
                m.ar_in, (m.ar_rows_a, m.ar_rows_b), m.ar_rs, m.ar_rr, r, rows, lambda other: (f, other)
            )

        def spread(self, source, slots, send_sem, recv_sem, me, count, device):
            piece = source.at[self.set, pl.ds(0, self.size)]
            copies = []
            for step in range(1, count):
                copies.append(
                    send(
                        piece,
                        slots[self.set].at[step, pl.ds(0, self.size)],
                        send_sem.at[self.set, step],
                        recv_sem.at[self.set, step],
                        device(lax.rem(me + step, count)),
                    )
                )
            return copies

        def gather(self, source, slots, me, count):
            for copy in self.copies:
                copy.wait_recv()
            slots = slots[self.set]
            slots[0, : self.size] = source[self.set, : self.size]
            total = slots[me, : self.size]
            for other in range(1, count):
                spot = lax.rem(me + count - other, count)
                total = total + slots[spot, : self.size]
            return total

        def middle(self):
            first = self.copies
            m.ar_part[self.set, : self.size] = self.gather(m.ar_in, (m.ar_rows_a, m.ar_rows_b), r, rows)
            self.copies = self.spread(
                m.ar_part, (m.ar_frames_a, m.ar_frames_b), m.ar_fs, m.ar_fr, f, frames, lambda other: (other, r)
            )
            for copy in first:
                copy.wait_send()

        def finish(self, *sizes):
            m.ar_out[: self.size] = self.gather(m.ar_part, (m.ar_frames_a, m.ar_frames_b), f, frames)
            for copy in self.copies:
                copy.wait_send()
            results, place = [], 0
            for size in sizes:
                parts = []
                for k in range(size // 128):
                    parts.append(m.ar_out[place : place + 1, :])
                    place += 1
                results.append(jnp.concatenate(parts, axis=1))
            return results

        def all(self, *sizes):
            self.middle()
            return self.finish(*sizes)

    def settle(k, totals, squares, number, gain, bias):
        size = totals.shape[1]
        center = totals / number
        spread = lax.rsqrt(squares / number - center * center + EPSILON)
        scale = spread * gain
        m.vec[6 * k : 6 * k + 1, :size] = center
        m.vec[6 * k + 1 : 6 * k + 2, :size] = spread
        m.vec[6 * k + 2 : 6 * k + 3, :size] = scale
        m.vec[6 * k + 3 : 6 * k + 4, :size] = bias - center * scale

    def settle_back(k, bias_grad, gain_grad, number):
        size = bias_grad.shape[1]
        m.vec[6 * k + 4 : 6 * k + 5, :size] = bias_grad / number
        m.vec[6 * k + 5 : 6 * k + 6, :size] = gain_grad / number

    def vec(k, which, cols=slice(0, 512)):
        return m.vec[6 * k + which : 6 * k + which + 1, cols]

    def affine(k, value, cols=slice(0, 512)):
        return value * vec(k, 2, cols) + vec(k, 3, cols)

    def normed(k, value, cols=slice(0, 512)):
        return (value - vec(k, 0, cols)) * vec(k, 1, cols)

    def field_grad(k, grads, value, cols=slice(0, 512)):
        return vec(k, 2, cols) * (
            grads - vec(k, 4, cols) - normed(k, value, cols) * vec(k, 5, cols)
        )

    def clear():
        m.stat[...] = jnp.zeros_like(m.stat)

    def collect(k, value, cols=slice(0, 512)):
        m.stat[k, :, cols] = m.stat[k, :, cols] + folded(value)

    def collected(k, size=512):
        return jnp.sum(m.stat[k, :, :size], axis=0, keepdims=True)

    def column_tiles(body):
        @pl.loop(0, wide // 512)
        def _(place):
            body(pl.ds(pl.multiple_of(place * 512, 512), 512))

    c = lax.rem(f, 2)
    ib = lax.rem(f // 2, b_count)
    ia = f // (2 * b_count)
    flip1 = r + 1 - 2 * lax.rem(r, 2)
    flip2 = lax.rem(r + 2, rows)
    core = (f + 1 - 2 * c, r)
    thin = 512 // frames

    def a_peer(step):
        other = lax.rem(ia + step, a_count)
        return other, ((other * b_count + ib) * 2 + c, r)

    def b_peer(step):
        other = lax.rem(ib + step, b_count)
        return other, ((ia * b_count + other) * 2 + c, r)

    def add_blocks(target, source, lead=()):
        for index in itertools.product(*[range(size) for size in lead]):
            into, other = target.at[index], source.at[index]

            @pl.loop(0, thin // 8)
            def _(place):
                spot = pl.ds(pl.multiple_of(place * 8, 8), 8)
                into[spot, :] = into[spot, :] + other[spot, :]

    def column_part(index):
        return pl.ds(pl.multiple_of(index * 128, 128), 128)

    def unit_steps(fill, out, turn, kind):
        two, three = turn % 2, turn % 3
        own, away, near = m.g_own.at[kind, two], m.g_away.at[kind], m.g_near.at[kind, two]
        send_sem, recv_sem = m.g_send.at[kind, three], m.g_recv.at[kind, three]
        used = [0]

        def go(source, target, device):
            spot = used[0]
            used[0] += 1
            return send(source, target, send_sem.at[spot], recv_sem.at[spot], device)

        def done(copies):
            for copy in copies:
                copy.wait_recv()
            for copy in copies:
                copy.wait_send()

        def over_axis(count, peer, pick, buffer, lead):
            copies = []
            for step in range(1, count):
                other, device = peer(step)
                copies.append(go(pick(other), buffer.at[step - 1], device))
            yield
            done(copies)
            for step in range(2, count):
                add_blocks(buffer.at[0], buffer.at[step - 1], lead)

        def over_a(pick, buffer, lead):
            yield from over_axis(a_count, a_peer, pick, buffer, lead)
            add_blocks(buffer.at[0], pick(ia), lead)

        def over_b(pick, buffer, lead):
            yield from over_axis(b_count, b_peer, pick, buffer, lead)
            add_blocks(buffer.at[0], pick(ib), lead)

        def over_rows(pick, buffer, last, lead):
            copies = [go(pick(lax.rem(flip1, 2) + 2 * k), buffer.at[k], (f, flip1)) for k in range(2)]
            yield
            done(copies)
            for k in range(2):
                add_blocks(buffer.at[k], pick(lax.rem(r, 2) + 2 * k), lead)
            copies = [go(buffer.at[1 - r // 2], last, (f, flip2))]
            yield
            done(copies)
            add_blocks(last, buffer.at[r // 2], lead)

        fill(away, 1 - c)
        copies = [go(away, near, core)]
        fill(own, c)
        yield
        done(copies)
        add_blocks(own, near, (a_count, b_count))
        if kind == 0:
            first, second = m.g_first_p.at[three], m.g_second_p.at[three]
            yield from over_b(lambda i: own.at[:, i], first, (a_count,))
            yield from over_a(lambda i: first.at[0, i], second, ())
        if kind == 1:
            first, second = m.g_first_q.at[three], m.g_second_q.at[three]
            yield from over_a(lambda i: own.at[i], first, (b_count,))
            yield from over_b(lambda i: first.at[0, i], second, ())
        if kind < 2:
            final = m.g_fourth.at[kind, three]
            yield from over_rows(
                lambda i: second.at[0, :, column_part(i)], m.g_third.at[kind, three], final, ()
            )
        else:
            both = m.g_both.at[three]
            yield from over_rows(
                lambda i: own.at[:, :, :, column_part(i)],
                m.g_rows.at[three],
                both,
                (a_count, b_count),
            )
            first, second = m.g_first_z.at[three], m.g_second_z.at[three]
            yield from over_a(lambda i: both.at[i], first, (b_count,))
            yield from over_b(lambda i: first.at[0, i], second, ())
            final = second.at[0]
        orders = ((b_count, b_peer), (a_count, a_peer))
        (one_count, one_peer), (two_count, two_peer) = orders[:: 1 if kind % 2 == 0 else -1]
        local = pltpu.make_async_copy(final, out.at[c, ia, ib], recv_sem.at[used[0]])
        used[0] += 1
        local.start()
        copies = []
        for step in range(1, one_count):
            _, device = one_peer(step)
            copies.append(go(final, out.at[c, ia, ib], device))
        yield
        local.wait()
        done(copies)
        copies = []
        field = out.at[c, ia] if kind % 2 == 0 else out.at[c, :, ib]
        for step in range(1, two_count):
            _, device = two_peer(step)
            copies.append(go(field, field, device))
        yield
        done(copies)
        copies = [go(out.at[c], out.at[c], core)]
        yield
        done(copies)

    units, active, begun = [], [], [0]

    def advance():
        kept = []
        for group in active:
            ended = False
            for unit in group:
                if next(unit, active) is active:
                    ended = True
            if not ended:
                kept.append(group)
        active[:] = kept
        if units:
            group = []
            for kind in range(3):
                if units:
                    fill, out = units.pop(0)
                    group.append(unit_steps(fill, out, begun[0], kind))
            begun[0] += 1
            for unit in group:
                next(unit)
            active.append(group)

    def pump(count):
        if count is None:
            while units or active:
                advance()
        else:
            for _ in range(count):
                advance()

    def begin_all_but(count):
        while len(units) > count:
            advance()

    def outer(left, right):
        def one(a, b):
            return lax.dot_general(
                a, b, (((0,), (0,)), ((), ())), preferred_element_type=jnp.float32
            )

        (high, low), (grad_high, grad_low) = left, right
        both = one(high, jnp.concatenate([grad_high, grad_low], 1))
        size = grad_high.shape[1]
        return both[:, :size] + both[:, size:] + one(low, grad_high)

    def blocks(value):
        return value.reshape(a_count, b_count, thin, value.shape[-1])

    def filler(left, right):
        def fill(target, which):
            start = pl.multiple_of(which * 256, 256)
            target[...] = blocks(
                outer([left(k, start) for k in range(2)], [right(k) for k in range(2)])
            )

        return fill

    def lanes_of(ref, quarter):
        def pick(k):
            return jnp.concatenate(
                [ref[k, :, z * 512 + quarter * 128 : z * 512 + quarter * 128 + 128] for z in range(4)],
                1,
            )

        return pick

    def whole(ref):
        return lambda k: ref[k]

    def rows_from(ref, base):
        return lambda k, start: ref[k, :, pl.ds(base + start, 256)]

    def out_lanes(ref, quarter):
        return ref.at[:, :, :, :, pl.ds(quarter * 128, 128)]

    def add_restorer():
        for quarter in range(4):
            units.append(
                (
                    filler(rows_from(m.squashed, 0), lanes_of(m.gc2, quarter)),
                    out_lanes(m.restorer, quarter),
                )
            )

    def add_widener():
        for quarter in range(4):
            units.append(
                (
                    filler(rows_from(m.h2, 0), lanes_of(m.uh, quarter)),
                    out_lanes(m.widener, quarter),
                )
            )

    def add_shortcut():
        def sampled(base):
            def pick(k, start):
                lane = pl.ds(base + start, 256)
                return jnp.concatenate(
                    [m.xb[k, pl.ds(row * half, band), lane] for row in (0, 2)], 0
                )

            return pick

        for quarter in range(4):
            for place in range(2):
                units.append(
                    (
                        filler(sampled(place * 512), lanes_of(m.gc2, quarter)),
                        out_lanes(m.shortcut.at[place], quarter),
                    )
                )

    def add_squeezer():
        for place in range(4):
            units.append(
                (filler(rows_from(m.uh, place * 512), whole(m.ga2)), m.squeezer.at[place])
            )

    def add_strider():
        def tapped(dy, base):
            def pick(k, start):
                lane = pl.ds(base + start, 256)
                return jnp.concatenate([m.pc[k, dy + 2 * i, :, lane] for i in range(2)], 0)

            return pick

        def grads(k):
            return jnp.concatenate([m.gb[k, i, :, 0:512] for i in range(2)], 0)

        for dy in range(3):
            for dx in range(3):
                units.append((filler(tapped(dy, dx * 512), grads), m.strider.at[dy * 3 + dx]))

    def add_narrower():
        def grads(k):
            return jnp.concatenate([m.uh[k, :, i * 512 : i * 512 + 512] for i in range(4)], 0)

        for place in range(2):
            units.append(
                (filler(rows_from(m.xb, place * 512), grads), m.narrower.at[place])
            )

    def one_hot(shape, places):
        row = lax.broadcasted_iota(jnp.int32, shape, 0)
        lane = lax.broadcasted_iota(jnp.int32, shape, 1)
        return jnp.where(row == places(lane), 1.0, 0.0).astype(jnp.bfloat16)

    def add_pack():
        def put_rows(start, z, value):
            spot = start % 64 // 16
            m.xs[z * 2 + start // 512, start % 512 // 64, spot : spot + 2] = value.reshape(2, 16, 128)

        for k in range(3):
            left = [m.gk[p, k] for p in range(2)]
            for dy in range(3):
                right = [
                    jnp.concatenate([m.mixed[p, k, i + dy] for i in range(2)], 0) for p in range(2)
                ]
                value = outer(left, right)
                for dx in range(3):
                    for z in range(4):
                        put_rows(
                            ((k * 3 + dy) * 3 + dx) * 32,
                            z,
                            value[z * 32 : z * 32 + 32, dx * 128 : dx * 128 + 128],
                        )

        def tap_places(lane):
            inside = lax.rem(lane, 128)
            return jnp.where(inside < 96, lax.div(lane, 128) * 96 + inside, -1)

        temporal = small_product(
            jnp.concatenate([m.temporal[...], jnp.zeros((5, 384), jnp.float32)], 0),
            one_hot((384, 512), tap_places),
        )
        for z in range(4):
            own_lanes = slice(z * 128, z * 128 + 128)
            eight = slice(z * 8, z * 8 + 8)
            put_rows(
                864,
                z,
                jnp.concatenate(
                    [m.condenser[eight, q * 128 : q * 128 + 128] for q in range(4)], 0
                ),
            )
            put_rows(
                896,
                z,
                jnp.concatenate(
                    [m.stencil[eight, q * 128 : q * 128 + 128] for q in range(3)]
                    + [temporal[:, own_lanes]],
                    0,
                ),
            )
            put_rows(928, z, m.exciter[:, own_lanes])

        for place in range(2):

            def fill(target, which, place=place):
                for lt in range(4):
                    value = m.xs[lt * 2 + place, pl.ds(which * 4, 4)]
                    target[:, :, :, lt * 128 : lt * 128 + 128] = blocks(value.reshape(256, 128))

            units.append((fill, m.pack.at[place]))


    for frame in range(depth):
        for mask, tall, flat_mask in (
            (m.place_of[frame] > 0, m.before_band, m.before16),
            (m.place_of[frame] < m.length_of[frame] - 1, m.after_band, m.after16),
        ):
            one = jnp.where(mask, 1.0, 0.0)
            tall[frame * 8 : frame * 8 + 8, :] = jnp.full((8, 128), one)
            flat_mask[frame : frame + 1, :] = jnp.full((1, 128), one)
    for flat_mask in (m.before16, m.after16):
        flat_mask[depth:, :] = jnp.zeros((flat_mask.shape[0] - depth, 128), jnp.float32)
    clear()

    @pl.when(r == 0)
    def _():
        m.a[0] = jnp.zeros(m.a.shape[1:], jnp.float32)

    @pl.when(r == rows - 1)
    def _():
        m.b_halo[...] = jnp.zeros_like(m.b_halo)
        m.back_halo[...] = jnp.zeros_like(m.back_halo)

    for buffers in (m.source, m.grad_pad):
        for k in range(buffers.shape[0]):

            @pl.when(r == 0)
            def _():
                buffers[k, 0] = jnp.zeros(buffers.shape[2:], jnp.float32)

            @pl.when(r == rows - 1)
            def _():
                buffers[k, 3] = jnp.zeros(buffers.shape[2:], jnp.float32)

    def reduce_row(row):
        @pl.loop(0, depth // 2)
        def _(pair):
            for parity in range(2):
                spot = pl.ds(parity, 8, stride=2)
                place = pl.multiple_of(row * half + parity * band + pair * 16, 16)
                for k, lane in enumerate(lanes):
                    value = jnp.concatenate(
                        [m.xs[k, 2 * pair, row, spot, :], m.xs[k, 2 * pair + 1, row, spot, :]], 0
                    )
                    put(m.xb, (pl.ds(place, 16), lane), value)

        place = pl.ds(pl.multiple_of(row * half, half), half)
        result = product(jnp.concatenate([m.xb[0, place, :], m.xb[1, place, :]], 0), m.wn[...])
        m.a[1 + row] = result.reshape(2, band, 512)
        collect(0, result)
        collect(1, result * result)

    wait_row(3)
    wn_load.wait()
    reduce_row(3)

    @pl.when(below)
    def _():
        send(m.a.at[4], m.a.at[0], m.halo_s.at[0], m.halo_r.at[0], (f, r + 1))

    for row in range(3):
        wait_row(row)

    @pl.loop(0, 3)
    def _(row):
        reduce_row(row)

    total = Sum([collected(0), collected(1)])
    clear()
    wsk_load.wait()

    def shortcut_tile(cols):
        lhs = jnp.concatenate(
            [m.xb[k, pl.ds(row * half, band), :] for k in range(2) for row in (0, 2)], 0
        )
        result = product(lhs, m.wsk[:, cols])
        m.s[:, cols] = result
        collect(2, result, cols)
        collect(3, result * result, cols)

    @pl.loop(0, 2)
    def _(place):
        shortcut_tile(pl.ds(pl.multiple_of(place * 512, 512), 512))

    total.middle()

    @pl.loop(2, 4)
    def _(place):
        shortcut_tile(pl.ds(pl.multiple_of(place * 512, 512), 512))

    totals, squares = total.finish(512, 512)
    for copy in small_loads:
        copy.wait()
    m.taps[...] = m.taps_in[...].astype(jnp.float32)
    settle(0, totals, squares, number_full, m.gain[0:1], m.bias[0:1])

    def activate(row, keep):
        @chunks(band, 32)
        def _(spot):
            for parity in range(2):
                value = silu(affine(0, m.a[row, parity, spot, :]))
                if keep is not None:
                    value = value * keep
                if parity == 0:
                    put(m.pc, (row, spot, slice(512, 1024)), value)
                else:
                    put(m.pc, (row, spot, slice(1024, 1536)), value)
                    put(m.pc, (row, spot, slice(0, 512)), moved_down(value))

    @pl.loop(1, 5)
    def _(row):
        activate(row, None)

    @pl.when(above)
    def _():
        pltpu.make_async_remote_copy(
            src_ref=m.a.at[4],
            dst_ref=m.a.at[0],
            send_sem=m.halo_s.at[0],
            recv_sem=m.halo_r.at[0],
            device_id=(f, lax.rem(r + 1, rows)),
            device_id_type=MESH,
        ).wait_recv()

    activate(0, above_one)
    ks_load.wait()

    def strided(dy):
        return product(
            jnp.concatenate([m.pc[k, dy + 2 * i] for k in range(2) for i in range(2)], 0), m.ks[dy]
        )

    m.b[...] = strided(0)
    m.b[...] = m.b[...] + strided(1)
    result = m.b[...] + strided(2)
    m.b[...] = result
    collect(0, result)
    collect(1, result * result)

    @pl.when(above)
    def _():
        send(
            m.b.at[pl.ds(0, band)], m.b_halo, m.halo_s.at[1], m.halo_r.at[1], (f, r - 1)
        )

    totals, squares, totals_p, squares_p = Sum(
        [collected(0), collected(1), collected(2, wide), collected(3, wide)]
    ).all(512, 512, wide, wide)
    clear()
    settle(1, totals, squares, number_half, m.gain[1:2], m.bias[1:2])
    settle(5, totals_p, squares_p, number_half, m.wide_gain[1:2], m.wide_bias[1:2])

    @chunks(half, 32)
    def _(spot):
        put(m.h2, (spot, slice(None)), silu(affine(1, m.b[spot, :])))

    we_load.wait()

    @column_tiles
    def _(cols):
        result = product(jnp.concatenate([m.h2[0], m.h2[1]], 0), m.we[:, cols])
        m.c[:, cols] = result
        collect(0, result, cols)
        collect(1, result * result, cols)

    totals, squares = Sum([collected(0, wide), collected(1, wide)]).all(wide, wide)
    clear()
    settle(4, totals, squares, number_half, m.wide_gain[0:1], m.wide_bias[0:1])

    def first_sum(spot, cols):
        return affine(4, m.c[spot, cols], cols) + affine(5, m.s[spot, cols], cols)

    @column_tiles
    def _(cols):
        @chunks(half, 32)
        def _(spot):
            value = silu(first_sum(spot, cols))
            put(m.uh, (spot, cols), value)

    wcr_load.wait()
    result = product(jnp.concatenate([m.uh[0], m.uh[1]], 0), m.wcr[...])
    m.d[...] = result
    collect(0, result)
    collect(1, result * result)
    totals, squares = Sum([collected(0), collected(1)]).all(512, 512)
    clear()
    settle(2, totals, squares, number_half, m.gain[2:3], m.bias[2:3])

    @chunks(half, 32)
    def _(spot):
        m.hid[spot, :] = silu(affine(2, m.d[spot, :]))

    m.edge[...] = jnp.zeros_like(m.edge)
    for row in range(2):
        block = m.hid[row * band : row * band + band, :]
        column = lax.rem(lax.broadcasted_iota(jnp.int32, block.shape, 0), 8)
        for k, value in enumerate(
            (block, jnp.where(column == 0, block, 0.0), jnp.where(column == 7, block, 0.0))
        ):
            m.edge[k, row, :depth] = jnp.sum(value.reshape(depth, 8, 512), axis=1)
    pad = m.edge.shape[2]
    reduced = small_product(m.edge[...].reshape(6 * pad, 512), m.wer[...], True)

    def part(kind, row):
        start = (kind * 2 + row) * pad
        return reduced[start : start + pad]

    taps = []
    for dy in range(3):
        for dx in range(3):
            by_row = []
            for row in range(2):
                value = part(0, row)
                if dx == 0:
                    value = value - part(2, row)
                if dx == 2:
                    value = value - part(1, row)
                by_row.append(value)
            if dy == 0:
                by_row[1] = by_row[1] * below_one
            if dy == 2:
                by_row[0] = by_row[0] * above_one
            taps.append(by_row[0] + by_row[1])
    taps.append(jnp.zeros((pad, 96), jnp.float32))
    m.tap_in[...] = jnp.concatenate(taps, 1)

    def rows_sum(source, slots, near, near_slots, toward, sems):
        copies = []
        for step in range(1, rows):
            copies.append(
                send(
                    source,
                    slots.at[step],
                    m.rows_s.at[sems, step],
                    m.rows_r.at[sems, step],
                    (f, lax.rem(r + step, rows)),
                )
            )
        for step in range(rows):
            copies.append(
                send(
                    source.at[near],
                    near_slots.at[step],
                    m.rows_s.at[sems, rows + step],
                    m.rows_r.at[sems, rows + step],
                    (toward, lax.rem(r + step, rows)),
                )
            )
        slots[0] = source[...]
        for copy in copies:
            copy.wait_recv()
        total = slots[r]
        other_total = near_slots[r]
        for other in range(1, rows):
            spot = lax.rem(r + rows - other, rows)
            total = total + slots[spot]
            other_total = other_total + near_slots[spot]
        for copy in copies:
            copy.wait_send()
        return total, other_total

    current, later = rows_sum(
        m.tap_in, m.tap_slots, pl.ds(0, 8), m.tap_near, before_f, 0
    )
    place = lax.broadcasted_iota(jnp.int32, current.shape, 0)
    follow = pltpu.roll(current, pad - 1, 0)
    follow = jnp.where(place == depth - 1, later[0:1], follow)
    after16 = m.after16[...]
    before16 = m.before16[...]
    follow = jnp.where(place < depth, follow, 0.0) * jnp.concatenate([after16] * 3, 1)
    m.follow[...] = follow
    area = float(16 * rows)
    pooled = (
        (small_product(follow[:, :288], m.kst[...]) - current[:, 128:160])
        * after16[:, :32]
        / area
    )
    m.pooled[...] = pooled
    m.gate[...] = jax.nn.sigmoid(small_product(pooled, m.wex[...]))
    for frame in range(depth):
        m.gate_all[frame * 8 : frame * 8 + 8, :] = jnp.broadcast_to(
            1.0 + m.gate[frame : frame + 1, :], (8, 512)
        )

    def halo(field, sems, pumps=0):
        own, first, last = pl.ds(8, band), pl.ds(8, 8), pl.ds(band, 8)
        low, high = pl.ds(0, 8), pl.ds(band + 8, 8)
        moves = [
            (field.at[pl.ds(1, 2), last], field.at[pl.ds(1, 2), low], (after_f, r), None, None),
            (field.at[pl.ds(1, 2), first], field.at[pl.ds(1, 2), high], (before_f, r), None, None),
            (field.at[2, own], field.at[0, own], (f, r + 1), below, above),
            (field.at[1, own], field.at[3, own], (f, r - 1), above, below),
            (field.at[2, last], field.at[0, low], (after_f, r + 1), below, above),
            (field.at[1, last], field.at[3, low], (after_f, r - 1), above, below),
            (field.at[2, first], field.at[0, high], (before_f, r + 1), below, above),
            (field.at[1, first], field.at[3, high], (before_f, r - 1), above, below),
        ]
        copies = []
        for k, (source, target, device, able, arriving) in enumerate(moves):
            copies.append(
                pltpu.make_async_remote_copy(
                    src_ref=source,
                    dst_ref=target,
                    send_sem=m.ring_s.at[sems % 2, k],
                    recv_sem=m.ring_r.at[sems % 2, k],
                    device_id=device,
                    device_id_type=MESH,
                )
            )
        for copy, move in zip(copies, moves):
            if move[3] is None:
                copy.start()
            else:
                pl.when(move[3])(copy.start)
        pump(pumps)
        for copy, move in zip(copies, moves):
            if move[4] is None:
                copy.wait_recv()
            else:
                pl.when(move[4])(copy.wait_recv)
        for copy, move in zip(copies, moves):
            if move[3] is None:
                copy.wait_send()
            else:
                pl.when(move[3])(copy.wait_send)

    own = pl.ds(8, band)
    previous, following = pl.ds(0, band), pl.ds(16, band)
    before_band = m.before_band[...]
    after_band = m.after_band[...]

    def sides(value):
        return jnp.concatenate([moved_down(value), value, moved_up(value)], 1)

    m.merged[:, 0:128] = jnp.concatenate(
        [m.hid[i * band : i * band + band, 0:128] * m.gate_all[:, 0:128] for i in range(2)], 0
    )
    kern_load.wait()
    for k in range(3):
        cols = slice((k + 1) * 128, (k + 2) * 128)
        for i in range(2):
            rows_i = slice(i * band, i * band + band)
            value = m.hid[rows_i, cols] * m.gate_all[:, cols]
            if k > 0:
                value = value + m.merged[rows_i, k * 128 : (k + 1) * 128]
            m.source[k, 1 + i, own] = value
        halo(m.source.at[k], k)
        tap = [m.taps[i : i + 1, k * 128 : (k + 1) * 128] for i in range(3)]
        for i in range(4):
            mixed = (
                tap[0] * before_band * m.source[k, i, previous]
                + tap[1] * m.source[k, i, own]
                + tap[2] * after_band * m.source[k, i, following]
            )
            put(m.mixed, (k, i), sides(mixed))
        result = jnp.zeros((half, 128), jnp.float32)
        for dy in range(3):
            lhs = jnp.concatenate([m.mixed[p, k, i + dy] for p in range(2) for i in range(2)], 0)
            result = result + product(lhs, m.kern[k, dy])
        m.merged[:, cols] = result

    result = m.merged[...]
    collect(0, result)
    collect(1, result * result)
    totals, squares = Sum([collected(0), collected(1)]).all(512, 512)
    clear()
    settle(3, totals, squares, number_half, m.gain[3:4], m.bias[3:4])

    @chunks(half, 32)
    def _(spot):
        put(m.squashed, (spot, slice(None)), silu(affine(3, m.merged[spot, :])))

    wce_load.wait()

    @column_tiles
    def _(cols):
        result = product(jnp.concatenate([m.squashed[0], m.squashed[1]], 0), m.wce[:, cols])
        m.e[:, cols] = result
        collect(0, result, cols)
        collect(1, result * result, cols)

    totals, squares = Sum([collected(0, wide), collected(1, wide)]).all(wide, wide)
    clear()
    settle(6, totals, squares, number_half, m.wide_gain[2:3], m.wide_bias[2:3])

    for copy in slope_loads:
        copy.wait()

    @column_tiles
    def _(cols):
        for row in range(2):

            @pl.loop(0, depth // 4)
            def _(part_place):
                block = pl.ds(pl.multiple_of(part_place * 4, 4), 4)
                spot = pl.ds(pl.multiple_of(row * band + part_place * 32, 32), 32)
                raw = m.e[spot, cols]
                value = (
                    affine(6, raw, cols)
                    + m.uh[0, spot, cols].astype(jnp.float32)
                    + m.uh[1, spot, cols].astype(jnp.float32)
                )
                logistic = jax.nn.sigmoid(value)
                grads = m.slope[row, block, :, cols].reshape(32, 512) * (
                    logistic * (1.0 + value * (1.0 - logistic))
                )
                m.slope[row, block, :, cols] = (value * logistic).reshape(4, 8, 512)
                m.d2[spot, cols] = grads
                collect(0, grads, cols)
                collect(1, grads * normed(6, raw, cols), cols)

    stores = []

    def store(source, target, sem=None):
        copy = pltpu.make_async_copy(source, target, m.store_sem.at[len(stores)] if sem is None else sem)
        copy.start()
        if sem is None:
            stores.append(copy)

    for row in range(2):
        store(m.slope.at[row], m.layer_output.at[:, row])

    bias_grad, gain_grad = Sum([collected(0, wide), collected(1, wide)]).all(wide, wide)
    clear()
    settle_back(6, bias_grad, gain_grad, number_half)
    m.baselines[2:3] = bias_grad
    m.amplitudes[2:3] = gain_grad

    @column_tiles
    def _(cols):
        @chunks(half, 32)
        def _(spot):
            put(m.gc2, (spot, cols), field_grad(6, m.d2[spot, cols], m.e[spot, cols], cols))


    def back_through(pair, weights, raw, k):
        m.back[...] = product(jnp.concatenate([pair[0], pair[1]], 0), weights[...], True)

        @chunks(half, 32)
        def _(spot):
            value = raw[spot, :]
            grads = m.back[spot, :] * slope(affine(k, value))
            m.back[spot, :] = grads
            collect(0, grads)
            collect(1, grads * normed(k, value))

    back_through(m.gc2, m.wce, m.merged, 3)
    add_restorer()
    total = Sum([collected(0), collected(1)])
    pump(PUMPS[0])
    bias_grad, gain_grad = total.all(512, 512)
    clear()
    settle_back(3, bias_grad, gain_grad, number_half)
    m.biasing[3:4] = bias_grad
    m.scaling[3:4] = gain_grad
    merged_grad = field_grad(3, m.back[...], m.merged[...])
    m.eg[...] = merged_grad

    for k in (2, 1, 0):
        cols = slice((k + 1) * 128, (k + 2) * 128)
        grads = m.eg[:, cols]
        if k < 2:
            grads = grads + m.eg[:, (k + 2) * 128 : (k + 3) * 128]
        put(m.gk, (k,), grads)
        for i in range(2):
            m.grad_pad[k % 2, 1 + i, own] = grads[i * band : i * band + band]
        halo(m.grad_pad.at[k % 2], 3 + k, PUMPS[1 + k])
        for i in range(4):
            put(m.grad_sides, (i,), sides(m.grad_pad[k % 2, i]))
        result = jnp.zeros((2 * (band + 16), 128), jnp.float32)
        for dy in range(3):
            lhs = jnp.concatenate([m.grad_sides[p, i + dy] for p in range(2) for i in range(2)], 0)
            for dx in range(3):
                result = result + product(
                    lhs[:, dx * 128 : dx * 128 + 128],
                    m.kern[k, 2 - dy, (2 - dx) * 128 : (3 - dx) * 128, :],
                    True,
                )
        span = band + 16
        tap = [m.taps[i : i + 1, k * 128 : (k + 1) * 128] for i in range(3)]
        tap_grads = [0.0, 0.0, 0.0]
        for i in range(2):
            m.mixed_grad[i] = result[i * span : i * span + span]
            middle = m.mixed_grad[i, own]
            for j, value in enumerate(
                (
                    middle * before_band * m.source[k, 1 + i, previous],
                    middle * m.source[k, 1 + i, own],
                    middle * after_band * m.source[k, 1 + i, following],
                )
            ):
                tap_grads[j] = tap_grads[j] + jnp.sum(value, axis=0, keepdims=True)
            m.eg[i * band : i * band + band, cols] = (
                tap[2] * before_band * m.mixed_grad[i, previous]
                + tap[1] * middle
                + tap[0] * after_band * m.mixed_grad[i, following]
            )
        for j in range(3):
            m.temporal[j : j + 1, k * 128 : (k + 1) * 128] = tap_grads[j]


    gate = m.gate[...]
    m.gate_part[...] = jnp.zeros_like(m.gate_part)
    touched = m.eg[...] * m.hid[...]
    touched = jnp.sum(touched.reshape(2 * depth, 8, 512), axis=1)
    m.gate_part[:depth] = touched[:depth] + touched[depth:]
    m.gate_part[...] = m.gate_part[...] * gate * (1.0 - gate)
    m.exciter[...] = small_outer(m.pooled[...], m.gate_part[...])
    current, earlier = rows_sum(
        m.gate_part, m.gate_slots, pl.ds(pad - 8, 8), m.gate_near, after_f, 1
    )
    place = lax.broadcasted_iota(jnp.int32, current.shape, 0)
    last_row = depth - 1 - (pad - 8)
    shifted = jnp.where(place == 0, earlier[last_row : last_row + 1], pltpu.roll(current, 1, 0))
    pooled_grads = small_product(jnp.concatenate([current, shifted], 0), m.wex[...], True) / area
    motion = pooled_grads[:pad] * after16[:, :32]
    motion_before = pooled_grads[pad:] * before16[:, :32]
    m.stencil[...] = small_outer(motion, m.follow[...]) * (1.0 / rows)
    spread = small_product(motion_before, m.kst[...], True)

    def tap_value(dy, dx):
        start = (dy * 3 + dx) * 32
        return spread[:, start : start + 32]

    values = []
    by_row = []
    for row in range(2):
        columns = []
        for dx in range(3):
            if row == 0:
                value = tap_value(0, dx) + tap_value(1, dx)
                value = value + tap_value(2, dx) * above_one
            else:
                value = tap_value(1, dx) + tap_value(2, dx)
                value = value + tap_value(0, dx) * below_one
            columns.append(value)
        by_row.append(columns)
    for kind in range(3):
        for row in range(2):
            d0, d1, d2 = by_row[row]
            value = (d0 + d1 + d2, d0 + d1, d1 + d2)[kind]
            values.append(value - motion)
    reduced_grad = jnp.concatenate(values, 0)
    edges = jnp.concatenate([m.edge[0] - m.edge[1] - m.edge[2], m.edge[1], m.edge[2]], 0)
    m.condenser[...] = small_outer(reduced_grad, edges.reshape(6 * pad, 512))
    m.e[: 6 * pad, :512] = small_product(reduced_grad, m.wer[...])

    for row in range(2):

        @pl.loop(0, depth)
        def _(frame):
            spot = pl.ds(pl.multiple_of(row * band + frame * 8, 8), 8)

            def edge_line(kind):
                return m.e[pl.ds((kind * 2 + row) * pad + frame, 1), 0:512]

            column = lax.broadcasted_iota(jnp.int32, (8, 512), 0)
            extra = jnp.where(
                column == 0,
                edge_line(1),
                jnp.where(column == 7, edge_line(2), edge_line(0)),
            )
            raw = m.d[spot, :]
            grads = m.eg[spot, :] * m.gate_all[pl.ds(pl.multiple_of(frame * 8, 8), 8), :] + extra
            grads = grads * slope(affine(2, raw))
            m.back[spot, :] = grads
            collect(0, grads)
            collect(1, grads * normed(2, raw))

    total = Sum([collected(0), collected(1)])
    add_pack()
    pump(PUMPS[4])
    bias_grad, gain_grad = total.all(512, 512)
    clear()
    settle_back(2, bias_grad, gain_grad, number_half)
    m.biasing[2:3] = bias_grad
    m.scaling[2:3] = gain_grad

    @chunks(half, 32)
    def _(spot):
        put(m.ga2, (spot, slice(None)), field_grad(2, m.back[spot, :], m.d[spot, :]))


    @column_tiles
    def _(cols):
        m.e[:, cols] = product(jnp.concatenate([m.ga2[0], m.ga2[1]], 0), m.wcr[cols, :], True)

        @chunks(half, 32)
        def _(spot):
            grads = (m.d2[spot, cols] + m.e[spot, cols]) * slope(first_sum(spot, cols))
            m.d2[spot, cols] = grads
            collect(0, grads, cols)
            collect(1, grads * normed(4, m.c[spot, cols], cols), cols)
            collect(2, grads * normed(5, m.s[spot, cols], cols), cols)

    add_squeezer()
    total = Sum([collected(0, wide), collected(1, wide), collected(2, wide)])
    pump(PUMPS[5])
    total.middle()
    pump(PUMPS[6])
    bias_grad, gain_c, gain_p = total.finish(wide, wide, wide)
    clear()
    settle_back(4, bias_grad, gain_c, number_half)
    settle_back(5, bias_grad, gain_p, number_half)
    for k in range(2):
        m.baselines[k : k + 1] = bias_grad
    m.amplitudes[0:1] = gain_c
    m.amplitudes[1:2] = gain_p

    begin_all_but(0)

    @column_tiles
    def _(cols):
        @chunks(half, 32)
        def _(spot):
            grads = m.d2[spot, cols]
            put(m.uh, (spot, cols), field_grad(4, grads, m.c[spot, cols], cols))
            put(m.gc2, (spot, cols), field_grad(5, grads, m.s[spot, cols], cols))

    back_through(m.uh, m.we, m.b, 1)

    @pl.when(above)
    def _():
        send(
            m.back.at[pl.ds(0, band)], m.back_halo, m.halo_s.at[2], m.halo_r.at[2], (f, r - 1)
        )

    total = Sum([collected(0), collected(1)])
    clear()
    add_widener()
    add_shortcut()
    pump(PUMPS[7])

    for cols in (slice(0, 512), slice(512, 1024)):
        if cols.start:
            total.middle()
            pump(PUMPS[8])
        m.d2[:, cols] = product(jnp.concatenate([m.gc2[0], m.gc2[1]], 0), m.wsk[cols, :], True)

    bias_grad, gain_grad = total.finish(512, 512)
    settle_back(1, bias_grad, gain_grad, number_half)
    m.biasing[1:2] = bias_grad
    m.scaling[1:2] = gain_grad

    def strided_grad(row, spot, value):
        put(m.gb, (row, spot, slice(0, 512)), value)
        put(m.gb, (row, spot, slice(512, 1024)), moved_up(value))

    for row in range(2):

        @chunks(band, 32)
        def _(spot):
            place = pl.ds(pl.multiple_of(row * band + spot.start, 32), 32)
            strided_grad(row, spot, field_grad(1, m.back[place, :], m.b[place, :]))

    @pl.when(below)
    def _():
        for k, (source, target) in enumerate(((m.b, m.b_halo), (m.back, m.back_halo))):
            pltpu.make_async_remote_copy(
                src_ref=source.at[pl.ds(0, band)],
                dst_ref=target,
                send_sem=m.halo_s.at[1 + k],
                recv_sem=m.halo_r.at[1 + k],
                device_id=(f, lax.rem(r + 1, rows)),
                device_id_type=MESH,
            ).wait_recv()

    @chunks(band, 32)
    def _(spot):
        value = field_grad(1, m.back_halo[spot, :], m.b_halo[spot, :])
        strided_grad(2, spot, value * below_one)


    add_strider()
    pump(PUMPS[9])

    def gb_rows(first, variant):
        lanes = slice(variant * 512, variant * 512 + 512)
        return jnp.concatenate([m.gb[k, first + i, :, lanes] for k in range(2) for i in range(2)], 0)

    def tap_weights(dy, dx):
        return m.ks[dy, dx * 512 : dx * 512 + 512, :]

    @pl.when(above)
    def _():
        for k, source in enumerate((m.b, m.back)):
            pltpu.make_async_remote_copy(
                src_ref=source.at[pl.ds(0, band)],
                dst_ref=m.back_halo,
                send_sem=m.halo_s.at[1 + k],
                recv_sem=m.halo_r.at[1 + k],
                device_id=(f, lax.rem(r + 1, rows)),
                device_id_type=MESH,
            ).wait_send()

    def ha_rows(parity, spot):
        return pl.ds(pl.multiple_of(parity * band + spot.start, 32), 32)

    plan = {
        (0, 0): [(0, 0, 1, 1)],
        (1, 0): [(0, 0, 1, 2), (0, 1, 1, 0)],
        (0, 1): [(0, 0, 2, 1), (1, 0, 0, 1)],
        (1, 1): [(0, 0, 2, 2), (1, 0, 0, 2), (0, 1, 2, 0), (1, 1, 0, 0)],
    }
    for (parity, odd), terms in plan.items():
        result = None
        for first, variant, dy, dx in terms:
            value = product(gb_rows(first, variant), tap_weights(dy, dx), True)
            result = value if result is None else result + value
        m.back[...] = result
        for i in range(2):
            row = 2 * i + odd

            @chunks(band, 32)
            def _(spot):
                place = pl.ds(pl.multiple_of(i * band + spot.start, 32), 32)
                raw = m.a[1 + row, parity, spot, :]
                grads = m.back[place, :] * slope(affine(0, raw))
                m.e[ha_rows(parity, spot), row * 512 : row * 512 + 512] = grads
                collect(0, grads)
                collect(1, grads * normed(0, raw))

    total = Sum([collected(0), collected(1)])
    pump(PUMPS[10])
    total.middle()
    pump(PUMPS[11])
    bias_grad, gain_grad = total.finish(512, 512)
    settle_back(0, bias_grad, gain_grad, number_full)
    begin_all_but(17)
    m.biasing[0:1] = bias_grad
    m.scaling[0:1] = gain_grad

    @pl.loop(0, 4)
    def _(row):
        for parity in range(2):

            @chunks(band, 32)
            def _(spot):
                lane = pl.ds(pl.multiple_of(row * 512, 512), 512)
                value = field_grad(
                    0, m.e[ha_rows(parity, spot), lane], m.a[1 + row, parity, spot, :]
                )
                put(m.uh, (ha_rows(parity, spot), lane), value)

        lane = pl.ds(pl.multiple_of(row * 512, 512), 512)
        lhs = jnp.concatenate([m.uh[0, :, lane], m.uh[1, :, lane]], 0)
        for part_cols in (slice(0, 512), slice(512, 1024)):
            result = product(lhs, m.wn[part_cols, :], True)
            even = jnp.where(lax.rem(row, 2) == 0, 1.0, 0.0)
            shortcut = m.d2[pl.ds(pl.multiple_of((row // 2) * band, band), band), part_cols]
            for parity in range(2):
                value = result[parity * band : parity * band + band]
                if parity == 0:
                    value = value + shortcut * even
                for frame in range(depth):
                    for k in range(4):
                        m.xs[
                            part_cols.start // 128 + k, frame, row, pl.ds(parity, 8, stride=2), :
                        ] = value[frame * 8 : frame * 8 + 8, k * 128 : k * 128 + 128]

    for row in range(4):
        for k, lane in enumerate(lanes):
            store(m.xs.at[k, :, row], m.pixels.at[:, row, :, lane], m.row_sem.at[row])
    for name in ("scaling", "biasing", "amplitudes", "baselines"):
        store(getattr(m, name), getattr(m, name + "_h"))
    add_narrower()
    pump(None)
    for copy in stores:
        copy.wait()
    for row in range(4):
        wait_row(row)

    @pl.when(below)
    def _():
        pltpu.make_async_remote_copy(
            src_ref=m.a.at[4],
            dst_ref=m.a.at[0],
            send_sem=m.halo_s.at[0],
            recv_sem=m.halo_r.at[0],
            device_id=(f, lax.rem(r + 1, rows)),
            device_id_type=MESH,
        ).wait_send()


def chain(
    x, place_of, length_of, wn, ks, we, wsk, wcr, wer, kst, wex, taps, kern, wce, gain, bias, wide_gain,
    wide_bias, slopes, call,
):
    frames, rows = lax.axis_size("frames"), lax.axis_size("rows")
    depth = x.shape[0]
    band, pad = depth * 8, -(-depth // 16) * 16
    half = 2 * band
    span = band + 16
    levels = int(math.log2(frames // 2))
    b_count = 2 ** (levels // 2)
    a_count = frames // 2 // b_count
    thin = 512 // frames
    blocks = (2, a_count, b_count, thin)
    unit = (a_count, b_count, thin, 512)
    copies = 6 + 2 * (a_count + b_count - 2)
    hbm, smem = pl.BlockSpec(memory_space=pl.ANY), pl.BlockSpec(memory_space=pltpu.SMEM)

    inputs = dict(
        x=(x, hbm), slope_h=(slopes, hbm), wn_h=(wn, hbm), wsk_h=(wsk, hbm), ks_h=(ks, hbm),
        we_h=(we, hbm), wcr_h=(wcr, hbm), wce_h=(wce, hbm), kern_h=(kern, hbm), wer_h=(wer, hbm),
        kst_h=(kst, hbm), wex_h=(wex, hbm), taps_in_h=(taps, hbm), gain_h=(gain, hbm),
        bias_h=(bias, hbm), wide_gain_h=(wide_gain, hbm), wide_bias_h=(wide_bias, hbm),
        place_of=(place_of, smem), length_of=(length_of, smem),
    )

    def wide_of(*shape):
        return jax.ShapeDtypeStruct(shape, jnp.float32)

    kept = dict(
        xb=(2, 4 * half, 1024), pc=(2, 5, band, 1536), h2=(2, half, 512), uh=(2, half, 2048),
        squashed=(2, half, 512), mixed=(2, 3, 4, band, 384), gc2=(2, half, 2048),
        gk=(2, 3, half, 128), ga2=(2, half, 512),
        gb=(2, 3, band, 1024),
    )
    outputs = dict(
        layer_output=(wide_of(depth, 2, 8, 2048), hbm), pixels=(wide_of(depth, 4, 16, 1024), hbm),
        scaling_h=(wide_of(4, 512), hbm), biasing_h=(wide_of(4, 512), hbm),
        amplitudes_h=(wide_of(3, 2048), hbm), baselines_h=(wide_of(3, 2048), hbm),
        narrower=(wide_of(2, *blocks, 128), hbm), strider=(wide_of(9, *blocks, 128), hbm),
        widener=(wide_of(*blocks, 512), hbm), shortcut=(wide_of(2, *blocks, 512), hbm),
        squeezer=(wide_of(4, *blocks, 128), hbm), restorer=(wide_of(*blocks, 512), hbm),
        pack=(wide_of(2, *blocks, 128), hbm),
    )

    def f32(*shape):
        return pltpu.VMEM(shape, jnp.float32)

    def b16(*shape):
        return pltpu.VMEM(shape, jnp.bfloat16)

    def sems(*shape):
        return pltpu.SemaphoreType.DMA(shape)

    scratch = dict(
        wn=b16(1024, 512), wsk=b16(1024, 2048), ks=b16(3, 1536, 512), we=b16(512, 2048),
        wcr=b16(2048, 512), wce=b16(512, 2048), kern=b16(3, 3, 384, 128),
        xs=f32(8, depth, 4, 16, 128), a=f32(5, 2, band, 512), b=f32(half, 512), c=f32(half, 2048),
        s=f32(half, 2048), d=f32(half, 512), hid=f32(half, 512),
        merged=f32(half, 512), e=f32(half, 2048),
        slope=f32(2, depth, 8, 2048), d2=f32(half, 2048), back=f32(half, 512), eg=f32(half, 512),
        b_halo=f32(band, 512),
        back_halo=f32(band, 512), source=f32(3, 4, span, 128), grad_pad=f32(2, 4, span, 128),
        mixed_grad=f32(2, span, 128), grad_sides=b16(2, 4, span, 384), gate_all=f32(band, 512),
        edge=f32(3, 2, pad, 512), gate=f32(pad, 512),
        gate_part=f32(pad, 512), pooled=f32(pad, 32), follow=f32(pad, 384), tap_in=f32(pad, 384),
        tap_slots=f32(rows, pad, 384), tap_near=f32(rows, 8, 384), gate_slots=f32(rows, pad, 512),
        gate_near=f32(rows, 8, 512), stat=f32(4, 8, 2048), vec=f32(48, 2048), ar_in=f32(2, 48, 128),
        ar_part=f32(2, 48, 128), ar_out=f32(48, 128), ar_rows_a=f32(rows, 32, 128), ar_rows_b=f32(rows, 48, 128),
        ar_frames_a=f32(frames, 32, 128), ar_frames_b=f32(frames, 48, 128), ar_rs=sems(2, rows), ar_rr=sems(2, rows),
        ar_fs=sems(2, frames), ar_fr=sems(2, frames), rows_s=sems(2, 2 * rows),
        rows_r=sems(2, 2 * rows), ring_s=sems(2, 8), ring_r=sems(2, 8), halo_s=sems(3),
        halo_r=sems(3), condenser=f32(32, 512), stencil=f32(32, 384), exciter=f32(32, 512),
        temporal=f32(3, 384), wer=b16(32, 512), kst=b16(288, 32), wex=b16(32, 512),
        taps_in=b16(3, 384), taps=f32(3, 384), gain=f32(4, 512), bias=f32(4, 512),
        wide_gain=f32(3, 2048), wide_bias=f32(3, 2048), before16=f32(pad, 128),
        after16=f32(pad, 128), before_band=f32(band, 128), after_band=f32(band, 128),
        scaling=f32(4, 512), biasing=f32(4, 512), amplitudes=f32(3, 2048), baselines=f32(3, 2048),
        g_own=f32(3, 2, *unit), g_away=f32(3, *unit), g_near=f32(3, 2, *unit),
        g_first_p=f32(3, b_count - 1, a_count, thin, 512),
        g_first_q=f32(3, a_count - 1, b_count, thin, 512),
        g_second_p=f32(3, a_count - 1, thin, 512), g_second_q=f32(3, b_count - 1, thin, 512),
        g_third=f32(2, 3, 2, thin, 128), g_fourth=f32(2, 3, thin, 128),
        g_rows=f32(3, 2, a_count, b_count, thin, 128), g_both=f32(3, a_count, b_count, thin, 128),
        g_first_z=f32(3, a_count - 1, b_count, thin, 128),
        g_second_z=f32(3, b_count - 1, thin, 128),
        g_send=sems(3, 3, copies), g_recv=sems(3, 3, copies),
        load_sem=sems(20), store_sem=sems(8), row_sem=sems(4),
    )
    for name in kept:
        scratch[name] = b16(*kept[name])
    names = list(inputs) + list(outputs) + list(scratch)
    results = pl.pallas_call(
        lambda *refs: chain_kernel(names, (frames, rows, depth, a_count, b_count), *refs),
        out_shape=[shape for shape, _ in outputs.values()],
        in_specs=[spec for _, spec in inputs.values()],
        out_specs=[spec for _, spec in outputs.values()],
        scratch_shapes=list(scratch.values()),
        compiler_params=pltpu.CompilerParams(
            collective_id=call, has_side_effects=True, vmem_limit_bytes=VMEM_BYTES
        ),
    )(*[value for value, _ in inputs.values()])
    return SimpleNamespace(**dict(zip(outputs, results)))


def finish_kernel(count, *refs):
    pack, refs = refs[0], refs[1:]
    sources, refs = refs[:count], refs[count:]
    targets, refs = refs[:count], refs[count:]
    condenser, stencil, exciter, temporal, kernels, tail = refs[:6]
    held, in_sems, out_sems = refs[6:-2], refs[-2], refs[-1]
    first = [
        pltpu.make_async_copy(source, block, in_sems.at[k])
        for k, (source, block) in enumerate(zip(sources, held))
    ]
    first.append(pltpu.make_async_copy(pack, tail, in_sems.at[count]))
    for copy in first:
        copy.start()
    second = []

    def put_out(source, target):
        copy = pltpu.make_async_copy(source, target, out_sems.at[len(second)])
        copy.start()
        second.append(copy)

    for copy, block, target in zip(first, held, targets):
        copy.wait()
        put_out(block, target)
    first[-1].wait()
    for tap in range(27):
        kernels[tap] = tail[tap * 32 : tap * 32 + 32, :]
    for q in range(4):
        condenser[:, q * 128 : q * 128 + 128] = tail[864 + q * 8 : 872 + q * 8, :]
    exciter[...] = tail[928:960, :]
    for tap in range(9):
        start, lane = 896 + tap // 4 * 8, tap % 4 * 32
        stencil[tap] = tail[start : start + 8, lane : lane + 32]
    temporal[...] = tail[920:923, :96]
    for copy in second:
        copy.wait()


def finish(pack, arrays):
    hbm, vmem = pl.BlockSpec(memory_space=pl.ANY), pl.BlockSpec(memory_space=pltpu.VMEM)
    shapes = [array.shape for array in arrays]
    shapes += [(8, 512), (9, 8, 32), (32, 128), (3, 96), (27, 32, 128)]
    count = len(arrays)
    return pl.pallas_call(
        lambda *refs: finish_kernel(count, *refs),
        out_shape=[jax.ShapeDtypeStruct(shape, jnp.float32) for shape in shapes],
        in_specs=[hbm] * (count + 1),
        out_specs=[hbm] * count + [vmem] * 5,
        scratch_shapes=[
            pltpu.VMEM(shape, jnp.float32) for shape in [pack.shape, *shapes[:count]]
        ]
        + [pltpu.SemaphoreType.DMA((count + 1,)), pltpu.SemaphoreType.DMA((count,))],
        compiler_params=pltpu.CompilerParams(vmem_limit_bytes=VMEM_BYTES),
    )(pack, *arrays)


def shards(
    input_feature_maps,
    sequence_slot_lookup,
    sequence_span_lookup,
    opening_reducer,
    downsampling_filter,
    opening_expander,
    skip_projection,
    closing_reducer,
    excite_reducer,
    excite_spatial_filter,
    excite_expander,
    time_taps,
    spatial_filters,
    closing_expander,
    narrow_norm_gains,
    narrow_norm_biases,
    wide_norm_gains,
    wide_norm_biases,
    loss_slope_wrt_final,
):
    k = chain(
        input_feature_maps,
        sequence_slot_lookup,
        sequence_span_lookup,
        opening_reducer,
        downsampling_filter.reshape(3, 1536, 512),
        opening_expander,
        skip_projection,
        closing_reducer,
        excite_reducer.T,
        excite_spatial_filter.reshape(288, 32),
        excite_expander,
        time_taps,
        spatial_filters.reshape(3, 3, 384, 128),
        closing_expander,
        narrow_norm_gains,
        narrow_norm_biases,
        wide_norm_gains,
        wide_norm_biases,
        loss_slope_wrt_final,
        0,
    )
    results = finish(
        k.pack.reshape(-1, 128),
        (
            k.layer_output,
            k.pixels,
            k.narrower.reshape(opening_reducer.shape[0], -1),
            k.strider.reshape(downsampling_filter.shape[:-1] + (-1,)),
            k.widener.reshape(opening_expander.shape[0], -1),
            k.shortcut.reshape(skip_projection.shape[0], -1),
            k.squeezer.reshape(closing_reducer.shape[0], -1),
            k.restorer.reshape(closing_expander.shape[0], -1),
            k.scaling_h,
            k.biasing_h,
            k.amplitudes_h,
            k.baselines_h,
        ),
    )
    condenser, stencil, exciter, temporal, kernels = results[12:]
    return (
        *results[:7],
        condenser.T,
        stencil.transpose(0, 2, 1).reshape(excite_spatial_filter.shape[:-1] + (-1,)),
        exciter,
        temporal,
        kernels.transpose(0, 2, 1).reshape(spatial_filters.shape[:-1] + (-1,)),
        *results[7:12],
    )


def solution(mesh):
    return jax.shard_map(
        shards,
        mesh=mesh,
        in_specs=(
            P("frames", "rows", None, None),
            P("frames"),
            P("frames"),
            P(),
            P(),
            P(),
            P(),
            P(),
            P(),
            P(),
            P(),
            P(),
            P(),
            P(),
            P(),
            P(),
            P(),
            P(),
            P("frames", "rows", None, None),
        ),
        out_specs=(
            P("frames", "rows", None, None),
            P("frames", "rows", None, None),
            P(None, "rows"),
            P(None, None, None, "rows"),
            P(None, "rows"),
            P(None, "rows"),
            P(None, "rows"),
            P(None, "rows"),
            P(None, None, None, "rows"),
            P(None, "rows"),
            P(None, "rows"),
            P(None, None, None, None, "rows"),
            P(None, "rows"),
            P(),
            P(),
            P(),
            P(),
        ),
        check_vma=False,
    )
```

```python
import itertools
import math
from types import SimpleNamespace

import jax
import jax.numpy as jnp
from jax import lax
from jax.experimental import pallas as pl
from jax.experimental.pallas import tpu as pltpu
from jax.sharding import PartitionSpec as P

MESH = pl.DeviceIdType.MESH
EPSILON = 1e-05
VMEM_BYTES = 65400 * 2**10


def split(value):
    high = value.astype(jnp.bfloat16)
    return high, (value - high.astype(jnp.float32)).astype(jnp.bfloat16)


def put(pair_ref, index, value):
    high, low = split(value)
    pair_ref[(0,) + index] = high
    pair_ref[(1,) + index] = low


def product(stacked, weights, turned=False):
    result = lax.dot_general(
        stacked,
        weights,
        (((1,), (1 if turned else 0,)), ((), ())),
        preferred_element_type=jnp.float32,
    )
    half = result.shape[0] // 2
    return result[:half] + result[half:]


def small_product(value, weights, turned=False):
    return product(jnp.concatenate(split(value), 0), weights, turned)


def small_outer(left, right):
    def one(a, b):
        return lax.dot_general(
            a, b, (((0,), (0,)), ((), ())), preferred_element_type=jnp.float32
        )

    (a, b), (c, d) = split(left), split(right)
    return one(a, c) + one(a, d) + one(b, c)


def slope(value):
    logistic = jax.nn.sigmoid(value)
    return logistic * (1.0 + value * (1.0 - logistic))


def silu(value):
    return value * jax.nn.sigmoid(value)


def folded(value):
    return jnp.sum(value.reshape(-1, 8, value.shape[-1]), axis=0)


def moved_down(value):
    place = lax.broadcasted_iota(jnp.int32, value.shape, 0)
    return jnp.where(lax.rem(place, 8) == 0, 0.0, pltpu.roll(value, 1, 0))


def moved_up(value):
    place = lax.broadcasted_iota(jnp.int32, value.shape, 0)
    return jnp.where(lax.rem(place, 8) == 7, 0.0, pltpu.roll(value, value.shape[0] - 1, 0))


def chunks(total, step):
    def bind(body):
        @pl.loop(0, total // step)
        def _(place):
            body(pl.ds(pl.multiple_of(place * step, step), step))

    return bind


PUMPS = (1, 1, 1, 1, 1, 1, 1, 1, 1, 1, 1, 1)


def chain_kernel(names, dims, *refs):
    frames, rows, depth, a_count, b_count = dims
    m = SimpleNamespace(**dict(zip(names, refs)))
    f = lax.axis_index("frames")
    r = lax.axis_index("rows")
    after_f, before_f = lax.rem(f + 1, frames), lax.rem(f + frames - 1, frames)
    band = depth * 8
    half = 2 * band
    number_half = float(half * frames * rows)
    number_full = 4.0 * number_half
    above, below = r > 0, r < rows - 1
    above_one, below_one = jnp.where(above, 1.0, 0.0), jnp.where(below, 1.0, 0.0)
    wide = 2048

    loads = []

    def load(source, target, sem=None):
        if sem is None:
            sem = m.load_sem.at[len(loads)]
            loads.append(sem)
        copy = pltpu.make_async_copy(source, target, sem)
        copy.start()
        return copy

    def wait_row(row):
        block = m.xs.at[:, :, row]
        pltpu.make_async_copy(block, block, m.row_sem.at[row]).wait()

    lanes = [slice(k * 128, k * 128 + 128) for k in range(8)]

    def load_row(row):
        [
            load(m.x.at[:, row, :, lane], m.xs.at[k, :, row], m.row_sem.at[row])
            for k, lane in enumerate(lanes)
        ]

    for row in (3, 0, 1, 2):
        load_row(row)
    small_loads = [
        load(getattr(m, name + "_h"), getattr(m, name))
        for name in (
            "wer", "kst", "wex", "taps_in", "gain", "bias", "wide_gain", "wide_bias"
        )
    ]
    wn_load = load(m.wn_h, m.wn)
    wsk_load = load(m.wsk_h, m.wsk)
    ks_load = load(m.ks_h, m.ks)
    we_load = load(m.we_h, m.we)
    wcr_load = load(m.wcr_h, m.wcr)
    wce_load = load(m.wce_h, m.wce)
    kern_load = load(m.kern_h, m.kern)
    slope_loads = [load(m.slope_h.at[:, row], m.slope.at[row]) for row in range(2)]

    barrier = pltpu.get_barrier_semaphore()
    partners = [(f, lax.rem(r + step, rows)) for step in range(1, rows)]
    partners += [(lax.rem(f + step, frames), r) for step in range(1, frames)]
    for other in (after_f, before_f):
        partners += [(other, lax.rem(r + step, rows)) for step in range(1, rows)]
    if frames == 8:
        for chip_step in range(1, frames // 2):
            other = lax.rem(f + 2 * chip_step, frames)
            partners += [(other, lax.rem(r + step, rows)) for step in range(1, rows)]
    for partner in partners:
        pl.semaphore_signal(barrier, inc=1, device_id=partner, device_id_type=MESH)
    pl.semaphore_wait(barrier, len(partners))

    sent = []

    def send(source, target, send_sem, recv_sem, device):
        copy = pltpu.make_async_remote_copy(
            src_ref=source,
            dst_ref=target,
            send_sem=send_sem,
            recv_sem=recv_sem,
            device_id=device,
            device_id_type=MESH,
        )
        copy.start()
        return copy

    class Sum:
        count = 0

        def __init__(self, pieces):
            self.set = Sum.count % 2
            Sum.count += 1
            place = 0
            for piece in pieces:
                for k in range(piece.shape[1] // 128):
                    m.ar_in[self.set, place : place + 1, :] = piece[:, k * 128 : k * 128 + 128]
                    place += 1
            self.size = -(-place // 8) * 8
            half_f, core_f = f // 2, lax.rem(f, 2)
            self.first = (
                (m.ar_rows_a, m.ar_rows_b), m.ar_rs, m.ar_rr, r, rows, lambda other: (f, other)
            )
            self.second = (
                (m.ar_frames_a, m.ar_frames_b), m.ar_fs, m.ar_fr, f, frames, lambda other: (other, r)
            )
            if frames == 8 and self.size == 8:
                self.first = (
                    *self.first[:3], core_f, 2, lambda other: (f - core_f + other, r)
                )
                self.second = (
                    (m.ar_small.at[0], m.ar_small.at[1]), m.ar_fs, m.ar_fr,
                    half_f * rows + r, frames // 2 * rows,
                    lambda other: (other // rows * 2 + core_f, lax.rem(other, rows)),
                )
            self.copies = self.spread(m.ar_in, *self.first)

        def spread(self, source, slots, send_sem, recv_sem, me, count, device):
            piece = source.at[self.set, pl.ds(0, self.size)]
            copies = []
            for step in range(1, count):
                copies.append(
                    send(
                        piece,
                        slots[self.set].at[step, pl.ds(0, self.size)],
                        send_sem.at[self.set, step],
                        recv_sem.at[self.set, step],
                        device(lax.rem(me + step, count)),
                    )
                )
            return copies

        def gather(self, source, slots, send_sem, recv_sem, me, count, device):
            for copy in self.copies:
                copy.wait_recv()
            slots = slots[self.set]
            slots[0, : self.size] = source[self.set, : self.size]
            total = slots[me, : self.size]
            for other in range(1, count):
                spot = lax.rem(me + count - other, count)
                total = total + slots[spot, : self.size]
            return total

        def middle(self):
            first = self.copies
            m.ar_part[self.set, : self.size] = self.gather(m.ar_in, *self.first)
            self.copies = self.spread(m.ar_part, *self.second)
            for copy in first:
                copy.wait_send()

        def finish(self, *sizes):
            m.ar_out[: self.size] = self.gather(m.ar_part, *self.second)
            for copy in self.copies:
                copy.wait_send()
            results, place = [], 0
            for size in sizes:
                parts = []
                for k in range(size // 128):
                    parts.append(m.ar_out[place : place + 1, :])
                    place += 1
                results.append(jnp.concatenate(parts, axis=1))
            return results

        def all(self, *sizes):
            self.middle()
            return self.finish(*sizes)

    def settle(k, totals, squares, number, gain, bias):
        size = totals.shape[1]
        center = totals / number
        spread = lax.rsqrt(squares / number - center * center + EPSILON)
        scale = spread * gain
        m.vec[6 * k : 6 * k + 1, :size] = center
        m.vec[6 * k + 1 : 6 * k + 2, :size] = spread
        m.vec[6 * k + 2 : 6 * k + 3, :size] = scale
        m.vec[6 * k + 3 : 6 * k + 4, :size] = bias - center * scale

    def settle_back(k, bias_grad, gain_grad, number):
        size = bias_grad.shape[1]
        m.vec[6 * k + 4 : 6 * k + 5, :size] = bias_grad / number
        m.vec[6 * k + 5 : 6 * k + 6, :size] = gain_grad / number

    def vec(k, which, cols=slice(0, 512)):
        return m.vec[6 * k + which : 6 * k + which + 1, cols]

    def affine(k, value, cols=slice(0, 512)):
        return value * vec(k, 2, cols) + vec(k, 3, cols)

    def normed(k, value, cols=slice(0, 512)):
        return (value - vec(k, 0, cols)) * vec(k, 1, cols)

    def field_grad(k, grads, value, cols=slice(0, 512)):
        return vec(k, 2, cols) * (
            grads - vec(k, 4, cols) - normed(k, value, cols) * vec(k, 5, cols)
        )

    def clear():
        m.stat[...] = jnp.zeros_like(m.stat)

    def collect(k, value, cols=slice(0, 512)):
        m.stat[k, :, cols] = m.stat[k, :, cols] + folded(value)

    def collected(k, size=512):
        return jnp.sum(m.stat[k, :, :size], axis=0, keepdims=True)

    def column_tiles(body):
        @pl.loop(0, wide // 512)
        def _(place):
            body(pl.ds(pl.multiple_of(place * 512, 512), 512))

    c = lax.rem(f, 2)
    ib = lax.rem(f // 2, b_count)
    ia = f // (2 * b_count)
    flip1 = r + 1 - 2 * lax.rem(r, 2)
    flip2 = lax.rem(r + 2, rows)
    core = (f + 1 - 2 * c, r)
    thin = 512 // frames

    def a_peer(step):
        other = lax.rem(ia + step, a_count)
        return other, ((other * b_count + ib) * 2 + c, r)

    def b_peer(step):
        other = lax.rem(ib + step, b_count)
        return other, ((ia * b_count + other) * 2 + c, r)

    def add_blocks(target, source, lead=()):
        for index in itertools.product(*[range(size) for size in lead]):
            into, other = target.at[index], source.at[index]

            size = min(thin, 32 if into.shape[-1] > 128 else 64)

            @pl.loop(0, thin // size)
            def _(place):
                spot = pl.ds(pl.multiple_of(place * size, size), size)
                into[spot, :] = into[spot, :] + other[spot, :]

    def column_part(index):
        return pl.ds(pl.multiple_of(index * 128, 128), 128)

    ring = m.g_rows.shape[0]

    def unit_steps(fill, out, turn, kind):
        two, three, deep = turn % 2, turn % 3, turn % ring
        own, away, near = m.g_own.at[kind, two], m.g_away.at[kind], m.g_near.at[kind, two]
        bank = [m.g_send.at[kind, deep], m.g_recv.at[kind, deep]]
        used = [0]

        def go(source, target, device):
            spot = used[0]
            used[0] += 1
            return send(source, target, bank[0].at[spot], bank[1].at[spot], device)

        def done(copies):
            for copy in copies:
                copy.wait_recv()
            for copy in copies:
                copy.wait_send()

        def over_axis(count, peer, pick, buffer, lead):
            copies = []
            for step in range(1, count):
                other, device = peer(step)
                copies.append(go(pick(other), buffer.at[step - 1], device))
            yield
            done(copies)
            for step in range(2, count):
                add_blocks(buffer.at[0], buffer.at[step - 1], lead)

        def over_a(pick, buffer, lead):
            yield from over_axis(a_count, a_peer, pick, buffer, lead)
            add_blocks(buffer.at[0], pick(ia), lead)

        def over_b(pick, buffer, lead):
            yield from over_axis(b_count, b_peer, pick, buffer, lead)
            add_blocks(buffer.at[0], pick(ib), lead)

        def over_rows(pick, buffer, last, lead):
            copies = [go(pick(lax.rem(flip1, 2) + 2 * k), buffer.at[k], (f, flip1)) for k in range(2)]
            yield
            done(copies)
            for k in range(2):
                add_blocks(buffer.at[k], pick(lax.rem(r, 2) + 2 * k), lead)
            copies = [go(buffer.at[1 - r // 2], last, (f, flip2))]
            yield
            done(copies)
            add_blocks(last, buffer.at[r // 2], lead)

        fill(away, 1 - c)
        copies = [go(away, near, core)]
        fill(own, c)
        yield
        done(copies)
        add_blocks(own, near, (a_count, b_count))
        if kind == 0:
            first, second = m.g_first_p.at[deep], m.g_second_p.at[three]
            yield from over_b(lambda i: own.at[:, i], first, (a_count,))
            yield from over_a(lambda i: first.at[0, i], second, ())
        if kind == 1:
            first, second = m.g_first_q.at[deep], m.g_second_q.at[three]
            yield from over_a(lambda i: own.at[i], first, (b_count,))
            yield from over_b(lambda i: first.at[0, i], second, ())
        if kind < 2:
            final = m.g_fourth.at[kind, three]
            yield from over_rows(
                lambda i: second.at[0, :, column_part(i)], m.g_third.at[kind, three], final, ()
            )
        else:
            both = m.g_both.at[three]
            yield from over_rows(
                lambda i: own.at[:, :, :, column_part(i)],
                m.g_rows.at[deep],
                both,
                (a_count, b_count),
            )
            first, second = m.g_first_z.at[three], m.g_second_z.at[three]
            yield from over_a(lambda i: both.at[i], first, (b_count,))
            yield from over_b(lambda i: first.at[0, i], second, ())
            final = second.at[0]
        orders = ((b_count, b_peer), (a_count, a_peer))
        (one_count, one_peer), (two_count, two_peer) = orders[:: 1 if kind % 2 == 0 else -1]
        local = pltpu.make_async_copy(final, out.at[c, ia, ib], bank[1].at[used[0]])
        used[0] += 1
        local.start()
        copies = []
        for step in range(1, one_count):
            _, device = one_peer(step)
            copies.append(go(final, out.at[c, ia, ib], device))
        yield
        local.wait()
        done(copies)
        copies = []
        field = out.at[c, ia] if kind % 2 == 0 else out.at[c, :, ib]
        for step in range(1, two_count):
            _, device = two_peer(step)
            copies.append(go(field, field, device))
        yield
        done(copies)
        copies = [go(out.at[c], out.at[c], core)]
        yield
        done(copies)

    units, active, begun = [], [], [0]

    def advance():
        kept = []
        for age, group in active:
            group = [unit for unit in group if next(unit, active) is not active]
            if group:
                kept.append((age + 1, group))
        active[:] = kept
        if units:
            group = []
            for kind in range(3):
                if units:
                    fill, out = units.pop(0)
                    group.append(unit_steps(fill, out, begun[0], kind))
            begun[0] += 1
            for unit in group:
                next(unit)
            active.append((1, group))

    def pump(count):
        if count is None:
            while units or active:
                advance()
        else:
            for _ in range(count):
                advance()

    def begin_all_but(count):
        while len(units) > count:
            advance()

    def outer(left, right):
        def one(a, b):
            return lax.dot_general(
                a, b, (((0,), (0,)), ((), ())), preferred_element_type=jnp.float32
            )

        (high, low), (grad_high, grad_low) = left, right
        both = one(high, jnp.concatenate([grad_high, grad_low], 1))
        size = grad_high.shape[1]
        return both[:, :size] + both[:, size:] + one(low, grad_high)

    def blocks(value):
        return value.reshape(a_count, b_count, thin, value.shape[-1])

    def filler(left, right):
        def fill(target, which):
            start = pl.multiple_of(which * 256, 256)
            target[...] = blocks(
                outer([left(k, start) for k in range(2)], [right(k) for k in range(2)])
            )

        return fill

    def lanes_of(ref, quarter):
        def pick(k):
            return jnp.concatenate(
                [ref[k, :, z * 512 + quarter * 128 : z * 512 + quarter * 128 + 128] for z in range(4)],
                1,
            )

        return pick

    def whole(ref):
        return lambda k: ref[k]

    def rows_from(ref, base):
        return lambda k, start: ref[k, :, pl.ds(base + start, 256)]

    def out_lanes(ref, quarter):
        return ref.at[:, :, :, :, pl.ds(quarter * 128, 128)]

    def add_restorer():
        for quarter in range(4):
            units.append(
                (
                    filler(rows_from(m.squashed, 0), lanes_of(m.gc2, quarter)),
                    out_lanes(m.restorer, quarter),
                )
            )

    def add_widener():
        for quarter in range(4):
            units.append(
                (
                    filler(rows_from(m.h2, 0), lanes_of(m.uh, quarter)),
                    out_lanes(m.widener, quarter),
                )
            )

    def add_shortcut():
        def sampled(base):
            def pick(k, start):
                lane = pl.ds(base + start, 256)
                return jnp.concatenate(
                    [m.xb[k, pl.ds(row * half, band), lane] for row in (0, 2)], 0
                )

            return pick

        for quarter in range(4):
            for place in range(2):
                units.append(
                    (
                        filler(sampled(place * 512), lanes_of(m.gc2, quarter)),
                        out_lanes(m.shortcut.at[place], quarter),
                    )
                )

    def add_squeezer():
        for place in range(4):
            units.append(
                (filler(rows_from(m.uh, place * 512), whole(m.ga2)), m.squeezer.at[place])
            )

    def add_strider():
        def tapped(dy, base):
            def pick(k, start):
                lane = pl.ds(base + start, 256)
                return jnp.concatenate([m.pc[k, dy + 2 * i, :, lane] for i in range(2)], 0)

            return pick

        def grads(k):
            return jnp.concatenate([m.gb[k, i, :, 0:512] for i in range(2)], 0)

        for dy in range(3):
            for dx in range(3):
                units.append((filler(tapped(dy, dx * 512), grads), m.strider.at[dy * 3 + dx]))

    def add_narrower():
        def grads(k):
            return jnp.concatenate([m.uh[k, :, i * 512 : i * 512 + 512] for i in range(4)], 0)

        for place in range(2):
            units.append(
                (filler(rows_from(m.xb, place * 512), grads), m.narrower.at[place])
            )

    def one_hot(shape, places):
        row = lax.broadcasted_iota(jnp.int32, shape, 0)
        lane = lax.broadcasted_iota(jnp.int32, shape, 1)
        return jnp.where(row == places(lane), 1.0, 0.0).astype(jnp.bfloat16)

    def add_pack():
        def put_rows(start, z, value):
            spot = start % 64 // 16
            m.xs[z * 2 + start // 512, start % 512 // 64, spot : spot + 2] = value.reshape(2, 16, 128)

        for k in range(3):
            left = [m.gk[p, k] for p in range(2)]
            for dy in range(3):
                right = [
                    jnp.concatenate([m.mixed[p, k, i + dy] for i in range(2)], 0) for p in range(2)
                ]
                value = outer(left, right)
                for dx in range(3):
                    for z in range(4):
                        put_rows(
                            ((k * 3 + dy) * 3 + dx) * 32,
                            z,
                            value[z * 32 : z * 32 + 32, dx * 128 : dx * 128 + 128],
                        )

        def tap_places(lane):
            inside = lax.rem(lane, 128)
            return jnp.where(inside < 96, lax.div(lane, 128) * 96 + inside, -1)

        temporal = small_product(
            jnp.concatenate([m.temporal[...], jnp.zeros((5, 384), jnp.float32)], 0),
            one_hot((384, 512), tap_places),
        )
        for z in range(4):
            own_lanes = slice(z * 128, z * 128 + 128)
            eight = slice(z * 8, z * 8 + 8)
            put_rows(
                864,
                z,
                jnp.concatenate(
                    [m.condenser[eight, q * 128 : q * 128 + 128] for q in range(4)], 0
                ),
            )
            put_rows(
                896,
                z,
                jnp.concatenate(
                    [m.stencil[eight, q * 128 : q * 128 + 128] for q in range(3)]
                    + [temporal[:, own_lanes]],
                    0,
                ),
            )
            put_rows(928, z, m.exciter[:, own_lanes])

        for place in range(2):

            def fill(target, which, place=place):
                for lt in range(4):
                    value = m.xs[lt * 2 + place, pl.ds(which * 4, 4)]
                    target[:, :, :, lt * 128 : lt * 128 + 128] = blocks(value.reshape(256, 128))

            units.append((fill, m.pack.at[place]))


    for frame in range(depth):
        for mask, tall, flat_mask in (
            (m.place_of[frame] > 0, m.before_band, m.before16),
            (m.place_of[frame] < m.length_of[frame] - 1, m.after_band, m.after16),
        ):
            one = jnp.where(mask, 1.0, 0.0)
            tall[frame * 8 : frame * 8 + 8, :] = jnp.full((8, 128), one)
            flat_mask[frame : frame + 1, :] = jnp.full((1, 128), one)
    for flat_mask in (m.before16, m.after16):
        flat_mask[depth:, :] = jnp.zeros((flat_mask.shape[0] - depth, 128), jnp.float32)
    clear()

    @pl.when(r == 0)
    def _():
        m.a[0] = jnp.zeros(m.a.shape[1:], jnp.float32)

    @pl.when(r == rows - 1)
    def _():
        m.b_halo[...] = jnp.zeros_like(m.b_halo)
        m.back_halo[...] = jnp.zeros_like(m.back_halo)

    for buffers in (m.source, m.grad_pad):
        for k in range(buffers.shape[0]):

            @pl.when(r == 0)
            def _():
                buffers[k, 0] = jnp.zeros(buffers.shape[2:], jnp.float32)

            @pl.when(r == rows - 1)
            def _():
                buffers[k, 3] = jnp.zeros(buffers.shape[2:], jnp.float32)

    def reduce_row(row):
        @pl.loop(0, depth // 2)
        def _(pair):
            for parity in range(2):
                spot = pl.ds(parity, 8, stride=2)
                place = pl.multiple_of(row * half + parity * band + pair * 16, 16)
                for k, lane in enumerate(lanes):
                    value = jnp.concatenate(
                        [m.xs[k, 2 * pair, row, spot, :], m.xs[k, 2 * pair + 1, row, spot, :]], 0
                    )
                    put(m.xb, (pl.ds(place, 16), lane), value)

        place = pl.ds(pl.multiple_of(row * half, half), half)
        result = product(jnp.concatenate([m.xb[0, place, :], m.xb[1, place, :]], 0), m.wn[...])
        m.a[1 + row] = result.reshape(2, band, 512)
        collect(0, result)
        collect(1, result * result)

    wait_row(3)
    wn_load.wait()
    reduce_row(3)

    @pl.when(below)
    def _():
        send(m.a.at[4], m.a.at[0], m.halo_s.at[0], m.halo_r.at[0], (f, r + 1))

    for row in range(3):
        wait_row(row)

    @pl.loop(0, 3)
    def _(row):
        reduce_row(row)

    total = Sum([collected(0), collected(1)])
    clear()
    wsk_load.wait()

    def shortcut_tile(cols):
        lhs = jnp.concatenate(
            [m.xb[k, pl.ds(row * half, band), :] for k in range(2) for row in (0, 2)], 0
        )
        result = product(lhs, m.wsk[:, cols])
        m.s[:, cols] = result
        collect(2, result, cols)
        collect(3, result * result, cols)

    @pl.loop(0, 2)
    def _(place):
        shortcut_tile(pl.ds(pl.multiple_of(place * 512, 512), 512))

    total.middle()

    @pl.loop(2, 4)
    def _(place):
        shortcut_tile(pl.ds(pl.multiple_of(place * 512, 512), 512))

    totals, squares = total.finish(512, 512)
    for copy in small_loads:
        copy.wait()
    m.taps[...] = m.taps_in[...].astype(jnp.float32)
    settle(0, totals, squares, number_full, m.gain[0:1], m.bias[0:1])

    def activate(row, keep):
        @chunks(band, 32)
        def _(spot):
            for parity in range(2):
                value = silu(affine(0, m.a[row, parity, spot, :]))
                if keep is not None:
                    value = value * keep
                if parity == 0:
                    put(m.pc, (row, spot, slice(512, 1024)), value)
                else:
                    put(m.pc, (row, spot, slice(1024, 1536)), value)
                    put(m.pc, (row, spot, slice(0, 512)), moved_down(value))

    @pl.loop(1, 5)
    def _(row):
        activate(row, None)

    @pl.when(above)
    def _():
        pltpu.make_async_remote_copy(
            src_ref=m.a.at[4],
            dst_ref=m.a.at[0],
            send_sem=m.halo_s.at[0],
            recv_sem=m.halo_r.at[0],
            device_id=(f, lax.rem(r + 1, rows)),
            device_id_type=MESH,
        ).wait_recv()

    activate(0, above_one)
    ks_load.wait()

    def strided(dy):
        return product(
            jnp.concatenate([m.pc[k, dy + 2 * i] for k in range(2) for i in range(2)], 0), m.ks[dy]
        )

    m.b[...] = strided(0)
    m.b[...] = m.b[...] + strided(1)
    result = m.b[...] + strided(2)
    m.b[...] = result
    collect(0, result)
    collect(1, result * result)

    @pl.when(above)
    def _():
        send(
            m.b.at[pl.ds(0, band)], m.b_halo, m.halo_s.at[1], m.halo_r.at[1], (f, r - 1)
        )

    totals, squares, totals_p, squares_p = Sum(
        [collected(0), collected(1), collected(2, wide), collected(3, wide)]
    ).all(512, 512, wide, wide)
    clear()
    settle(1, totals, squares, number_half, m.gain[1:2], m.bias[1:2])
    settle(5, totals_p, squares_p, number_half, m.wide_gain[1:2], m.wide_bias[1:2])

    @chunks(half, 32)
    def _(spot):
        put(m.h2, (spot, slice(None)), silu(affine(1, m.b[spot, :])))

    we_load.wait()

    @column_tiles
    def _(cols):
        result = product(jnp.concatenate([m.h2[0], m.h2[1]], 0), m.we[:, cols])
        m.c[:, cols] = result
        collect(0, result, cols)
        collect(1, result * result, cols)

    totals, squares = Sum([collected(0, wide), collected(1, wide)]).all(wide, wide)
    clear()
    settle(4, totals, squares, number_half, m.wide_gain[0:1], m.wide_bias[0:1])

    def first_sum(spot, cols):
        return affine(4, m.c[spot, cols], cols) + affine(5, m.s[spot, cols], cols)

    @column_tiles
    def _(cols):
        @chunks(half, 32)
        def _(spot):
            value = silu(first_sum(spot, cols))
            put(m.uh, (spot, cols), value)

    wcr_load.wait()
    result = product(jnp.concatenate([m.uh[0], m.uh[1]], 0), m.wcr[...])
    m.d[...] = result
    collect(0, result)
    collect(1, result * result)
    totals, squares = Sum([collected(0), collected(1)]).all(512, 512)
    clear()
    settle(2, totals, squares, number_half, m.gain[2:3], m.bias[2:3])

    @chunks(half, 32)
    def _(spot):
        m.hid[spot, :] = silu(affine(2, m.d[spot, :]))

    m.edge[...] = jnp.zeros_like(m.edge)
    for row in range(2):
        block = m.hid[row * band : row * band + band, :]
        column = lax.rem(lax.broadcasted_iota(jnp.int32, block.shape, 0), 8)
        for k, value in enumerate(
            (block, jnp.where(column == 0, block, 0.0), jnp.where(column == 7, block, 0.0))
        ):
            m.edge[k, row, :depth] = jnp.sum(value.reshape(depth, 8, 512), axis=1)
    pad = m.edge.shape[2]
    reduced = small_product(m.edge[...].reshape(6 * pad, 512), m.wer[...], True)

    def part(kind, row):
        start = (kind * 2 + row) * pad
        return reduced[start : start + pad]

    taps = []
    for dy in range(3):
        for dx in range(3):
            by_row = []
            for row in range(2):
                value = part(0, row)
                if dx == 0:
                    value = value - part(2, row)
                if dx == 2:
                    value = value - part(1, row)
                by_row.append(value)
            if dy == 0:
                by_row[1] = by_row[1] * below_one
            if dy == 2:
                by_row[0] = by_row[0] * above_one
            taps.append(by_row[0] + by_row[1])
    taps.append(jnp.zeros((pad, 96), jnp.float32))
    m.tap_in[...] = jnp.concatenate(taps, 1)

    def rows_sum(source, slots, near, near_slots, toward, sems):
        copies = []
        for step in range(1, rows):
            copies.append(
                send(
                    source,
                    slots.at[step],
                    m.rows_s.at[sems, step],
                    m.rows_r.at[sems, step],
                    (f, lax.rem(r + step, rows)),
                )
            )
        for step in range(rows):
            copies.append(
                send(
                    source.at[near],
                    near_slots.at[step],
                    m.rows_s.at[sems, rows + step],
                    m.rows_r.at[sems, rows + step],
                    (toward, lax.rem(r + step, rows)),
                )
            )
        slots[0] = source[...]
        for copy in copies:
            copy.wait_recv()
        total = slots[r]
        other_total = near_slots[r]
        for other in range(1, rows):
            spot = lax.rem(r + rows - other, rows)
            total = total + slots[spot]
            other_total = other_total + near_slots[spot]
        for copy in copies:
            copy.wait_send()
        return total, other_total

    current, later = rows_sum(
        m.tap_in, m.tap_slots, pl.ds(0, 8), m.tap_near, before_f, 0
    )
    place = lax.broadcasted_iota(jnp.int32, current.shape, 0)
    follow = pltpu.roll(current, pad - 1, 0)
    follow = jnp.where(place == depth - 1, later[0:1], follow)
    after16 = m.after16[...]
    before16 = m.before16[...]
    follow = jnp.where(place < depth, follow, 0.0) * jnp.concatenate([after16] * 3, 1)
    m.follow[...] = follow
    area = float(16 * rows)
    pooled = (
        (small_product(follow[:, :288], m.kst[...]) - current[:, 128:160])
        * after16[:, :32]
        / area
    )
    m.pooled[...] = pooled
    m.gate[...] = jax.nn.sigmoid(small_product(pooled, m.wex[...]))
    for frame in range(depth):
        m.gate_all[frame * 8 : frame * 8 + 8, :] = jnp.broadcast_to(
            1.0 + m.gate[frame : frame + 1, :], (8, 512)
        )

    def halo(field, sems, pumps=0):
        own, first, last = pl.ds(8, band), pl.ds(8, 8), pl.ds(band, 8)
        low, high = pl.ds(0, 8), pl.ds(band + 8, 8)
        moves = [
            (field.at[pl.ds(1, 2), last], field.at[pl.ds(1, 2), low], (after_f, r), None, None),
            (field.at[pl.ds(1, 2), first], field.at[pl.ds(1, 2), high], (before_f, r), None, None),
            (field.at[2, own], field.at[0, own], (f, r + 1), below, above),
            (field.at[1, own], field.at[3, own], (f, r - 1), above, below),
            (field.at[2, last], field.at[0, low], (after_f, r + 1), below, above),
            (field.at[1, last], field.at[3, low], (after_f, r - 1), above, below),
            (field.at[2, first], field.at[0, high], (before_f, r + 1), below, above),
            (field.at[1, first], field.at[3, high], (before_f, r - 1), above, below),
        ]
        copies = []
        for k, (source, target, device, able, arriving) in enumerate(moves):
            copies.append(
                pltpu.make_async_remote_copy(
                    src_ref=source,
                    dst_ref=target,
                    send_sem=m.ring_s.at[sems % 2, k],
                    recv_sem=m.ring_r.at[sems % 2, k],
                    device_id=device,
                    device_id_type=MESH,
                )
            )
        for copy, move in zip(copies, moves):
            if move[3] is None:
                copy.start()
            else:
                pl.when(move[3])(copy.start)
        pump(pumps)
        for copy, move in zip(copies, moves):
            if move[4] is None:
                copy.wait_recv()
            else:
                pl.when(move[4])(copy.wait_recv)
        for copy, move in zip(copies, moves):
            if move[3] is None:
                copy.wait_send()
            else:
                pl.when(move[3])(copy.wait_send)

    own = pl.ds(8, band)
    previous, following = pl.ds(0, band), pl.ds(16, band)
    before_band = m.before_band[...]
    after_band = m.after_band[...]

    def sides(value):
        return jnp.concatenate([moved_down(value), value, moved_up(value)], 1)

    m.merged[:, 0:128] = jnp.concatenate(
        [m.hid[i * band : i * band + band, 0:128] * m.gate_all[:, 0:128] for i in range(2)], 0
    )
    kern_load.wait()
    for k in range(3):
        cols = slice((k + 1) * 128, (k + 2) * 128)
        for i in range(2):
            rows_i = slice(i * band, i * band + band)
            value = m.hid[rows_i, cols] * m.gate_all[:, cols]
            if k > 0:
                value = value + m.merged[rows_i, k * 128 : (k + 1) * 128]
            m.source[k, 1 + i, own] = value
        halo(m.source.at[k], k)
        tap = [m.taps[i : i + 1, k * 128 : (k + 1) * 128] for i in range(3)]
        for i in range(4):
            mixed = (
                tap[0] * before_band * m.source[k, i, previous]
                + tap[1] * m.source[k, i, own]
                + tap[2] * after_band * m.source[k, i, following]
            )
            put(m.mixed, (k, i), sides(mixed))
        result = jnp.zeros((half, 128), jnp.float32)
        for dy in range(3):
            lhs = jnp.concatenate([m.mixed[p, k, i + dy] for p in range(2) for i in range(2)], 0)
            result = result + product(lhs, m.kern[k, dy])
        m.merged[:, cols] = result

    result = m.merged[...]
    collect(0, result)
    collect(1, result * result)
    totals, squares = Sum([collected(0), collected(1)]).all(512, 512)
    clear()
    settle(3, totals, squares, number_half, m.gain[3:4], m.bias[3:4])

    @chunks(half, 32)
    def _(spot):
        put(m.squashed, (spot, slice(None)), silu(affine(3, m.merged[spot, :])))

    wce_load.wait()

    @column_tiles
    def _(cols):
        result = product(jnp.concatenate([m.squashed[0], m.squashed[1]], 0), m.wce[:, cols])
        m.e[:, cols] = result
        collect(0, result, cols)
        collect(1, result * result, cols)

    totals, squares = Sum([collected(0, wide), collected(1, wide)]).all(wide, wide)
    clear()
    settle(6, totals, squares, number_half, m.wide_gain[2:3], m.wide_bias[2:3])

    for copy in slope_loads:
        copy.wait()

    @column_tiles
    def _(cols):
        for row in range(2):

            @pl.loop(0, depth // 4)
            def _(part_place):
                block = pl.ds(pl.multiple_of(part_place * 4, 4), 4)
                spot = pl.ds(pl.multiple_of(row * band + part_place * 32, 32), 32)
                raw = m.e[spot, cols]
                value = (
                    affine(6, raw, cols)
                    + m.uh[0, spot, cols].astype(jnp.float32)
                    + m.uh[1, spot, cols].astype(jnp.float32)
                )
                logistic = jax.nn.sigmoid(value)
                grads = m.slope[row, block, :, cols].reshape(32, 512) * (
                    logistic * (1.0 + value * (1.0 - logistic))
                )
                m.slope[row, block, :, cols] = (value * logistic).reshape(4, 8, 512)
                m.d2[spot, cols] = grads
                collect(0, grads, cols)
                collect(1, grads * normed(6, raw, cols), cols)

    stores = []

    def store(source, target, sem=None):
        copy = pltpu.make_async_copy(source, target, m.store_sem.at[len(stores)] if sem is None else sem)
        copy.start()
        if sem is None:
            stores.append(copy)

    for row in range(2):
        store(m.slope.at[row], m.layer_output.at[:, row])

    bias_grad, gain_grad = Sum([collected(0, wide), collected(1, wide)]).all(wide, wide)
    clear()
    settle_back(6, bias_grad, gain_grad, number_half)
    m.baselines[2:3] = bias_grad
    m.amplitudes[2:3] = gain_grad

    @column_tiles
    def _(cols):
        @chunks(half, 32)
        def _(spot):
            put(m.gc2, (spot, cols), field_grad(6, m.d2[spot, cols], m.e[spot, cols], cols))


    def back_through(pair, weights, raw, k):
        m.back[...] = product(jnp.concatenate([pair[0], pair[1]], 0), weights[...], True)

        @chunks(half, 32)
        def _(spot):
            value = raw[spot, :]
            grads = m.back[spot, :] * slope(affine(k, value))
            m.back[spot, :] = grads
            collect(0, grads)
            collect(1, grads * normed(k, value))

    back_through(m.gc2, m.wce, m.merged, 3)
    add_restorer()
    total = Sum([collected(0), collected(1)])
    pump(PUMPS[0])
    bias_grad, gain_grad = total.all(512, 512)
    clear()
    settle_back(3, bias_grad, gain_grad, number_half)
    m.biasing[3:4] = bias_grad
    m.scaling[3:4] = gain_grad
    merged_grad = field_grad(3, m.back[...], m.merged[...])
    m.eg[...] = merged_grad

    for k in (2, 1, 0):
        cols = slice((k + 1) * 128, (k + 2) * 128)
        grads = m.eg[:, cols]
        if k < 2:
            grads = grads + m.eg[:, (k + 2) * 128 : (k + 3) * 128]
        put(m.gk, (k,), grads)
        for i in range(2):
            m.grad_pad[k % 2, 1 + i, own] = grads[i * band : i * band + band]
        halo(m.grad_pad.at[k % 2], 3 + k, PUMPS[1 + k])
        for i in range(4):
            put(m.grad_sides, (i,), sides(m.grad_pad[k % 2, i]))
        result = jnp.zeros((2 * (band + 16), 128), jnp.float32)
        for dy in range(3):
            lhs = jnp.concatenate([m.grad_sides[p, i + dy] for p in range(2) for i in range(2)], 0)
            for dx in range(3):
                result = result + product(
                    lhs[:, dx * 128 : dx * 128 + 128],
                    m.kern[k, 2 - dy, (2 - dx) * 128 : (3 - dx) * 128, :],
                    True,
                )
        span = band + 16
        tap = [m.taps[i : i + 1, k * 128 : (k + 1) * 128] for i in range(3)]
        tap_grads = [0.0, 0.0, 0.0]
        for i in range(2):
            m.mixed_grad[i] = result[i * span : i * span + span]
            middle = m.mixed_grad[i, own]
            for j, value in enumerate(
                (
                    middle * before_band * m.source[k, 1 + i, previous],
                    middle * m.source[k, 1 + i, own],
                    middle * after_band * m.source[k, 1 + i, following],
                )
            ):
                tap_grads[j] = tap_grads[j] + jnp.sum(value, axis=0, keepdims=True)
            m.eg[i * band : i * band + band, cols] = (
                tap[2] * before_band * m.mixed_grad[i, previous]
                + tap[1] * middle
                + tap[0] * after_band * m.mixed_grad[i, following]
            )
        for j in range(3):
            m.temporal[j : j + 1, k * 128 : (k + 1) * 128] = tap_grads[j]


    gate = m.gate[...]
    m.gate_part[...] = jnp.zeros_like(m.gate_part)
    touched = m.eg[...] * m.hid[...]
    touched = jnp.sum(touched.reshape(2 * depth, 8, 512), axis=1)
    m.gate_part[:depth] = touched[:depth] + touched[depth:]
    m.gate_part[...] = m.gate_part[...] * gate * (1.0 - gate)
    current, earlier = rows_sum(
        m.gate_part, m.gate_slots, pl.ds(pad - 8, 8), m.gate_near, after_f, 1
    )
    place = lax.broadcasted_iota(jnp.int32, current.shape, 0)
    last_row = depth - 1 - (pad - 8)
    shifted = jnp.where(place == 0, earlier[last_row : last_row + 1], pltpu.roll(current, 1, 0))
    pooled_grads = small_product(jnp.concatenate([current, shifted], 0), m.wex[...], True) / area
    motion = pooled_grads[:pad] * after16[:, :32]
    motion_before = pooled_grads[pad:] * before16[:, :32]
    spread = small_product(motion_before, m.kst[...], True)

    def tap_value(dy, dx):
        start = (dy * 3 + dx) * 32
        return spread[:, start : start + 32]

    values = []
    by_row = []
    for row in range(2):
        columns = []
        for dx in range(3):
            if row == 0:
                value = tap_value(0, dx) + tap_value(1, dx)
                value = value + tap_value(2, dx) * above_one
            else:
                value = tap_value(1, dx) + tap_value(2, dx)
                value = value + tap_value(0, dx) * below_one
            columns.append(value)
        by_row.append(columns)
    for kind in range(3):
        for row in range(2):
            d0, d1, d2 = by_row[row]
            value = (d0 + d1 + d2, d0 + d1, d1 + d2)[kind]
            values.append(value - motion)
    reduced_grad = jnp.concatenate(values, 0)
    m.e[: 6 * pad, :512] = small_product(reduced_grad, m.wer[...])

    for row in range(2):

        @pl.loop(0, depth)
        def _(frame):
            spot = pl.ds(pl.multiple_of(row * band + frame * 8, 8), 8)

            def edge_line(kind):
                return m.e[pl.ds((kind * 2 + row) * pad + frame, 1), 0:512]

            column = lax.broadcasted_iota(jnp.int32, (8, 512), 0)
            extra = jnp.where(
                column == 0,
                edge_line(1),
                jnp.where(column == 7, edge_line(2), edge_line(0)),
            )
            raw = m.d[spot, :]
            grads = m.eg[spot, :] * m.gate_all[pl.ds(pl.multiple_of(frame * 8, 8), 8), :] + extra
            grads = grads * slope(affine(2, raw))
            m.back[spot, :] = grads
            collect(0, grads)
            collect(1, grads * normed(2, raw))

    total = Sum([collected(0), collected(1)])
    m.exciter[...] = small_outer(m.pooled[...], m.gate_part[...])
    m.stencil[...] = small_outer(motion, m.follow[...]) * (1.0 / rows)
    edges = jnp.concatenate([m.edge[0] - m.edge[1] - m.edge[2], m.edge[1], m.edge[2]], 0)
    m.condenser[...] = small_outer(reduced_grad, edges.reshape(6 * pad, 512))
    add_pack()
    pump(PUMPS[4])
    bias_grad, gain_grad = total.all(512, 512)
    clear()
    settle_back(2, bias_grad, gain_grad, number_half)
    m.biasing[2:3] = bias_grad
    m.scaling[2:3] = gain_grad

    @chunks(half, 32)
    def _(spot):
        put(m.ga2, (spot, slice(None)), field_grad(2, m.back[spot, :], m.d[spot, :]))


    @column_tiles
    def _(cols):
        m.e[:, cols] = product(jnp.concatenate([m.ga2[0], m.ga2[1]], 0), m.wcr[cols, :], True)

        @chunks(half, 32)
        def _(spot):
            grads = (m.d2[spot, cols] + m.e[spot, cols]) * slope(first_sum(spot, cols))
            m.d2[spot, cols] = grads
            collect(0, grads, cols)
            collect(1, grads * normed(4, m.c[spot, cols], cols), cols)
            collect(2, grads * normed(5, m.s[spot, cols], cols), cols)

    add_squeezer()
    total = Sum([collected(0, wide), collected(1, wide), collected(2, wide)])
    pump(PUMPS[5])
    total.middle()
    pump(PUMPS[6])
    bias_grad, gain_c, gain_p = total.finish(wide, wide, wide)
    clear()
    settle_back(4, bias_grad, gain_c, number_half)
    settle_back(5, bias_grad, gain_p, number_half)
    for k in range(2):
        m.baselines[k : k + 1] = bias_grad
    m.amplitudes[0:1] = gain_c
    m.amplitudes[1:2] = gain_p

    begin_all_but(0)

    @column_tiles
    def _(cols):
        @chunks(half, 32)
        def _(spot):
            grads = m.d2[spot, cols]
            put(m.uh, (spot, cols), field_grad(4, grads, m.c[spot, cols], cols))
            put(m.gc2, (spot, cols), field_grad(5, grads, m.s[spot, cols], cols))

    back_through(m.uh, m.we, m.b, 1)

    @pl.when(above)
    def _():
        send(
            m.back.at[pl.ds(0, band)], m.back_halo, m.halo_s.at[2], m.halo_r.at[2], (f, r - 1)
        )

    total = Sum([collected(0), collected(1)])
    clear()
    add_widener()
    add_shortcut()
    pump(PUMPS[7])

    for cols in (slice(0, 512), slice(512, 1024)):
        if cols.start:
            total.middle()
            pump(PUMPS[8])
        m.d2[:, cols] = product(jnp.concatenate([m.gc2[0], m.gc2[1]], 0), m.wsk[cols, :], True)

    bias_grad, gain_grad = total.finish(512, 512)
    settle_back(1, bias_grad, gain_grad, number_half)
    m.biasing[1:2] = bias_grad
    m.scaling[1:2] = gain_grad

    def strided_grad(row, spot, value):
        put(m.gb, (row, spot, slice(0, 512)), value)
        put(m.gb, (row, spot, slice(512, 1024)), moved_up(value))

    for row in range(2):

        @chunks(band, 32)
        def _(spot):
            place = pl.ds(pl.multiple_of(row * band + spot.start, 32), 32)
            strided_grad(row, spot, field_grad(1, m.back[place, :], m.b[place, :]))

    @pl.when(below)
    def _():
        for k, (source, target) in enumerate(((m.b, m.b_halo), (m.back, m.back_halo))):
            pltpu.make_async_remote_copy(
                src_ref=source.at[pl.ds(0, band)],
                dst_ref=target,
                send_sem=m.halo_s.at[1 + k],
                recv_sem=m.halo_r.at[1 + k],
                device_id=(f, lax.rem(r + 1, rows)),
                device_id_type=MESH,
            ).wait_recv()

    @chunks(band, 32)
    def _(spot):
        value = field_grad(1, m.back_halo[spot, :], m.b_halo[spot, :])
        strided_grad(2, spot, value * below_one)


    add_strider()
    pump(PUMPS[9])

    def gb_rows(first, variant):
        lanes = slice(variant * 512, variant * 512 + 512)
        return jnp.concatenate([m.gb[k, first + i, :, lanes] for k in range(2) for i in range(2)], 0)

    def tap_weights(dy, dx):
        return m.ks[dy, dx * 512 : dx * 512 + 512, :]

    @pl.when(above)
    def _():
        for k, source in enumerate((m.b, m.back)):
            pltpu.make_async_remote_copy(
                src_ref=source.at[pl.ds(0, band)],
                dst_ref=m.back_halo,
                send_sem=m.halo_s.at[1 + k],
                recv_sem=m.halo_r.at[1 + k],
                device_id=(f, lax.rem(r + 1, rows)),
                device_id_type=MESH,
            ).wait_send()

    def ha_rows(parity, spot):
        return pl.ds(pl.multiple_of(parity * band + spot.start, 32), 32)

    plan = {
        (0, 0): [(0, 0, 1, 1)],
        (1, 0): [(0, 0, 1, 2), (0, 1, 1, 0)],
        (0, 1): [(0, 0, 2, 1), (1, 0, 0, 1)],
        (1, 1): [(0, 0, 2, 2), (1, 0, 0, 2), (0, 1, 2, 0), (1, 1, 0, 0)],
    }
    for (parity, odd), terms in plan.items():
        result = None
        for first, variant, dy, dx in terms:
            value = product(gb_rows(first, variant), tap_weights(dy, dx), True)
            result = value if result is None else result + value
        m.back[...] = result
        for i in range(2):
            row = 2 * i + odd

            @chunks(band, 32)
            def _(spot):
                place = pl.ds(pl.multiple_of(i * band + spot.start, 32), 32)
                raw = m.a[1 + row, parity, spot, :]
                grads = m.back[place, :] * slope(affine(0, raw))
                m.e[ha_rows(parity, spot), row * 512 : row * 512 + 512] = grads
                collect(0, grads)
                collect(1, grads * normed(0, raw))

    total = Sum([collected(0), collected(1)])
    pump(PUMPS[10])
    total.middle()
    pump(PUMPS[11])
    bias_grad, gain_grad = total.finish(512, 512)
    settle_back(0, bias_grad, gain_grad, number_full)
    begin_all_but(17)
    m.biasing[0:1] = bias_grad
    m.scaling[0:1] = gain_grad

    @pl.loop(0, 4)
    def _(row):
        for parity in range(2):

            @chunks(band, 32)
            def _(spot):
                lane = pl.ds(pl.multiple_of(row * 512, 512), 512)
                value = field_grad(
                    0, m.e[ha_rows(parity, spot), lane], m.a[1 + row, parity, spot, :]
                )
                put(m.uh, (ha_rows(parity, spot), lane), value)

    add_narrower()
    pump(1)

    def pixel_row(row):
        lane = pl.ds(pl.multiple_of(row * 512, 512), 512)
        lhs = jnp.concatenate([m.uh[0, :, lane], m.uh[1, :, lane]], 0)
        for part_cols in (slice(0, 512), slice(512, 1024)):
            result = product(lhs, m.wn[part_cols, :], True)
            even = jnp.where(lax.rem(row, 2) == 0, 1.0, 0.0)
            shortcut = m.d2[pl.ds(pl.multiple_of((row // 2) * band, band), band), part_cols]
            for parity in range(2):
                value = result[parity * band : parity * band + band]
                if parity == 0:
                    value = value + shortcut * even
                for frame in range(depth):
                    for k in range(4):
                        m.xs[
                            part_cols.start // 128 + k, frame, row, pl.ds(parity, 8, stride=2), :
                        ] = value[frame * 8 : frame * 8 + 8, k * 128 : k * 128 + 128]

    for part_rows in ((0, 2), (2, 4)):
        pl.loop(*part_rows)(pixel_row)
        for row in range(*part_rows):
            for k, lane in enumerate(lanes):
                store(m.xs.at[k, :, row], m.pixels.at[:, row, :, lane], m.row_sem.at[row])
        if part_rows[0] == 0:
            pump(1)
    for name in ("scaling", "biasing", "amplitudes", "baselines"):
        store(getattr(m, name), getattr(m, name + "_h"))
    pump(None)
    for copy in stores:
        copy.wait()
    for row in range(4):
        wait_row(row)

    @pl.when(below)
    def _():
        pltpu.make_async_remote_copy(
            src_ref=m.a.at[4],
            dst_ref=m.a.at[0],
            send_sem=m.halo_s.at[0],
            recv_sem=m.halo_r.at[0],
            device_id=(f, lax.rem(r + 1, rows)),
            device_id_type=MESH,
        ).wait_send()


def chain(
    x, place_of, length_of, wn, ks, we, wsk, wcr, wer, kst, wex, taps, kern, wce, gain, bias, wide_gain,
    wide_bias, slopes, call,
):
    frames, rows = lax.axis_size("frames"), lax.axis_size("rows")
    depth = x.shape[0]
    band, pad = depth * 8, -(-depth // 16) * 16
    half = 2 * band
    span = band + 16
    levels = int(math.log2(frames // 2))
    b_count = 2 ** (levels // 2)
    a_count = frames // 2 // b_count
    thin = 512 // frames
    blocks = (2, a_count, b_count, thin)
    unit = (a_count, b_count, thin, 512)
    copies = 6 + 2 * (a_count + b_count - 2)
    ring = 3
    hbm, smem = pl.BlockSpec(memory_space=pl.ANY), pl.BlockSpec(memory_space=pltpu.SMEM)

    inputs = dict(
        x=(x, hbm), slope_h=(slopes, hbm), wn_h=(wn, hbm), wsk_h=(wsk, hbm), ks_h=(ks, hbm),
        we_h=(we, hbm), wcr_h=(wcr, hbm), wce_h=(wce, hbm), kern_h=(kern, hbm), wer_h=(wer, hbm),
        kst_h=(kst, hbm), wex_h=(wex, hbm), taps_in_h=(taps, hbm), gain_h=(gain, hbm),
        bias_h=(bias, hbm), wide_gain_h=(wide_gain, hbm), wide_bias_h=(wide_bias, hbm),
        place_of=(place_of, smem), length_of=(length_of, smem),
    )

    def wide_of(*shape):
        return jax.ShapeDtypeStruct(shape, jnp.float32)

    kept = dict(
        xb=(2, 4 * half, 1024), pc=(2, 5, band, 1536), h2=(2, half, 512), uh=(2, half, 2048),
        squashed=(2, half, 512), mixed=(2, 3, 4, band, 384), gc2=(2, half, 2048),
        gk=(2, 3, half, 128), ga2=(2, half, 512),
        gb=(2, 3, band, 1024),
    )
    outputs = dict(
        layer_output=(wide_of(depth, 2, 8, 2048), hbm), pixels=(wide_of(depth, 4, 16, 1024), hbm),
        scaling_h=(wide_of(4, 512), hbm), biasing_h=(wide_of(4, 512), hbm),
        amplitudes_h=(wide_of(3, 2048), hbm), baselines_h=(wide_of(3, 2048), hbm),
        narrower=(wide_of(2, *blocks, 128), hbm), strider=(wide_of(9, *blocks, 128), hbm),
        widener=(wide_of(*blocks, 512), hbm), shortcut=(wide_of(2, *blocks, 512), hbm),
        squeezer=(wide_of(4, *blocks, 128), hbm), restorer=(wide_of(*blocks, 512), hbm),
        pack=(wide_of(2, *blocks, 128), hbm),
    )

    def f32(*shape):
        return pltpu.VMEM(shape, jnp.float32)

    def b16(*shape):
        return pltpu.VMEM(shape, jnp.bfloat16)

    def sems(*shape):
        return pltpu.SemaphoreType.DMA(shape)

    scratch = dict(
        wn=b16(1024, 512), wsk=b16(1024, 2048), ks=b16(3, 1536, 512), we=b16(512, 2048),
        wcr=b16(2048, 512), wce=b16(512, 2048), kern=b16(3, 3, 384, 128),
        xs=f32(8, depth, 4, 16, 128), a=f32(5, 2, band, 512), b=f32(half, 512), c=f32(half, 2048),
        s=f32(half, 2048), d=f32(half, 512), hid=f32(half, 512),
        merged=f32(half, 512), e=f32(half, 2048),
        slope=f32(2, depth, 8, 2048), d2=f32(half, 2048), back=f32(half, 512), eg=f32(half, 512),
        b_halo=f32(band, 512),
        back_halo=f32(band, 512), source=f32(3, 4, span, 128), grad_pad=f32(2, 4, span, 128),
        mixed_grad=f32(2, span, 128), grad_sides=b16(2, 4, span, 384), gate_all=f32(band, 512),
        edge=f32(3, 2, pad, 512), gate=f32(pad, 512),
        gate_part=f32(pad, 512), pooled=f32(pad, 32), follow=f32(pad, 384), tap_in=f32(pad, 384),
        tap_slots=f32(rows, pad, 384), tap_near=f32(rows, 8, 384), gate_slots=f32(rows, pad, 512),
        gate_near=f32(rows, 8, 512), stat=f32(4, 8, 2048), vec=f32(48, 2048), ar_in=f32(2, 48, 128),
        ar_part=f32(2, 48, 128), ar_out=f32(48, 128), ar_rows_a=f32(rows, 32, 128), ar_rows_b=f32(rows, 48, 128),
        ar_frames_a=f32(frames, 32, 128), ar_frames_b=f32(frames, 48, 128), ar_rs=sems(2, rows), ar_rr=sems(2, rows),
        ar_fs=sems(2, max(frames, 16)), ar_fr=sems(2, max(frames, 16)),
        ar_small=f32(2, 16, 8, 128), rows_s=sems(2, 2 * rows),
        rows_r=sems(2, 2 * rows), ring_s=sems(2, 8), ring_r=sems(2, 8), halo_s=sems(3),
        halo_r=sems(3), condenser=f32(32, 512), stencil=f32(32, 384), exciter=f32(32, 512),
        temporal=f32(3, 384), wer=b16(32, 512), kst=b16(288, 32), wex=b16(32, 512),
        taps_in=b16(3, 384), taps=f32(3, 384), gain=f32(4, 512), bias=f32(4, 512),
        wide_gain=f32(3, 2048), wide_bias=f32(3, 2048), before16=f32(pad, 128),
        after16=f32(pad, 128), before_band=f32(band, 128), after_band=f32(band, 128),
        scaling=f32(4, 512), biasing=f32(4, 512), amplitudes=f32(3, 2048), baselines=f32(3, 2048),
        g_own=f32(3, 2, *unit), g_away=f32(3, *unit), g_near=f32(3, 2, *unit),
        g_first_p=f32(ring, b_count - 1, a_count, thin, 512),
        g_first_q=f32(ring, a_count - 1, b_count, thin, 512),
        g_second_p=f32(3, a_count - 1, thin, 512), g_second_q=f32(3, b_count - 1, thin, 512),
        g_third=f32(2, 3, 2, thin, 128), g_fourth=f32(2, 3, thin, 128),
        g_rows=f32(ring, 2, a_count, b_count, thin, 128), g_both=f32(3, a_count, b_count, thin, 128),
        g_first_z=f32(3, a_count - 1, b_count, thin, 128),
        g_second_z=f32(3, b_count - 1, thin, 128),
        g_send=sems(3, ring, copies), g_recv=sems(3, ring, copies),
        load_sem=sems(20), store_sem=sems(8), row_sem=sems(4),
    )
    for name in kept:
        scratch[name] = b16(*kept[name])
    names = list(inputs) + list(outputs) + list(scratch)
    results = pl.pallas_call(
        lambda *refs: chain_kernel(names, (frames, rows, depth, a_count, b_count), *refs),
        out_shape=[shape for shape, _ in outputs.values()],
        in_specs=[spec for _, spec in inputs.values()],
        out_specs=[spec for _, spec in outputs.values()],
        scratch_shapes=list(scratch.values()),
        compiler_params=pltpu.CompilerParams(
            collective_id=call, has_side_effects=True, vmem_limit_bytes=VMEM_BYTES
        ),
    )(*[value for value, _ in inputs.values()])
    return SimpleNamespace(**dict(zip(outputs, results)))


def finish_kernel(count, *refs):
    pack, refs = refs[0], refs[1:]
    sources, refs = refs[:count], refs[count:]
    targets, refs = refs[:count], refs[count:]
    condenser, stencil, exciter, temporal, kernels, tail = refs[:6]
    held, in_sems, out_sems = refs[6:-2], refs[-2], refs[-1]
    first = [
        pltpu.make_async_copy(source, block, in_sems.at[k])
        for k, (source, block) in enumerate(zip(sources, held))
    ]
    first.append(pltpu.make_async_copy(pack, tail, in_sems.at[count]))
    for copy in first:
        copy.start()
    second = []

    def put_out(source, target):
        copy = pltpu.make_async_copy(source, target, out_sems.at[len(second)])
        copy.start()
        second.append(copy)

    for copy, block, target in zip(first, held, targets):
        copy.wait()
        put_out(block, target)
    first[-1].wait()
    for tap in range(27):
        kernels[tap] = tail[tap * 32 : tap * 32 + 32, :]
    for q in range(4):
        condenser[:, q * 128 : q * 128 + 128] = tail[864 + q * 8 : 872 + q * 8, :]
    exciter[...] = tail[928:960, :]
    for tap in range(9):
        start, lane = 896 + tap // 4 * 8, tap % 4 * 32
        stencil[tap] = tail[start : start + 8, lane : lane + 32]
    temporal[...] = tail[920:923, :96]
    for copy in second:
        copy.wait()


def finish(pack, arrays):
    hbm, vmem = pl.BlockSpec(memory_space=pl.ANY), pl.BlockSpec(memory_space=pltpu.VMEM)
    shapes = [array.shape for array in arrays]
    shapes += [(8, 512), (9, 8, 32), (32, 128), (3, 96), (27, 32, 128)]
    count = len(arrays)
    return pl.pallas_call(
        lambda *refs: finish_kernel(count, *refs),
        out_shape=[jax.ShapeDtypeStruct(shape, jnp.float32) for shape in shapes],
        in_specs=[hbm] * (count + 1),
        out_specs=[hbm] * count + [vmem] * 5,
        scratch_shapes=[
            pltpu.VMEM(shape, jnp.float32) for shape in [pack.shape, *shapes[:count]]
        ]
        + [pltpu.SemaphoreType.DMA((count + 1,)), pltpu.SemaphoreType.DMA((count,))],
        compiler_params=pltpu.CompilerParams(vmem_limit_bytes=VMEM_BYTES),
    )(pack, *arrays)


def shards(
    input_feature_maps,
    sequence_slot_lookup,
    sequence_span_lookup,
    opening_reducer,
    downsampling_filter,
    opening_expander,
    skip_projection,
    closing_reducer,
    excite_reducer,
    excite_spatial_filter,
    excite_expander,
    time_taps,
    spatial_filters,
    closing_expander,
    narrow_norm_gains,
    narrow_norm_biases,
    wide_norm_gains,
    wide_norm_biases,
    loss_slope_wrt_final,
):
    k = chain(
        input_feature_maps,
        sequence_slot_lookup,
        sequence_span_lookup,
        opening_reducer,
        downsampling_filter.reshape(3, 1536, 512),
        opening_expander,
        skip_projection,
        closing_reducer,
        excite_reducer.T,
        excite_spatial_filter.reshape(288, 32),
        excite_expander,
        time_taps,
        spatial_filters.reshape(3, 3, 384, 128),
        closing_expander,
        narrow_norm_gains,
        narrow_norm_biases,
        wide_norm_gains,
        wide_norm_biases,
        loss_slope_wrt_final,
        0,
    )
    results = finish(
        k.pack.reshape(-1, 128),
        (
            k.layer_output,
            k.pixels,
            k.narrower.reshape(opening_reducer.shape[0], -1),
            k.strider.reshape(downsampling_filter.shape[:-1] + (-1,)),
            k.widener.reshape(opening_expander.shape[0], -1),
            k.shortcut.reshape(skip_projection.shape[0], -1),
            k.squeezer.reshape(closing_reducer.shape[0], -1),
            k.restorer.reshape(closing_expander.shape[0], -1),
            k.scaling_h,
            k.biasing_h,
            k.amplitudes_h,
            k.baselines_h,
        ),
    )
    condenser, stencil, exciter, temporal, kernels = results[12:]
    return (
        *results[:7],
        condenser.T,
        stencil.transpose(0, 2, 1).reshape(excite_spatial_filter.shape[:-1] + (-1,)),
        exciter,
        temporal,
        kernels.transpose(0, 2, 1).reshape(spatial_filters.shape[:-1] + (-1,)),
        *results[7:12],
    )


def solution(mesh):
    return jax.shard_map(
        shards,
        mesh=mesh,
        in_specs=(
            P("frames", "rows", None, None),
            P("frames"),
            P("frames"),
            P(),
            P(),
            P(),
            P(),
            P(),
            P(),
            P(),
            P(),
            P(),
            P(),
            P(),
            P(),
            P(),
            P(),
            P(),
            P("frames", "rows", None, None),
        ),
        out_specs=(
            P("frames", "rows", None, None),
            P("frames", "rows", None, None),
            P(None, "rows"),
            P(None, None, None, "rows"),
            P(None, "rows"),
            P(None, "rows"),
            P(None, "rows"),
            P(None, "rows"),
            P(None, None, None, "rows"),
            P(None, "rows"),
            P(None, "rows"),
            P(None, None, None, None, "rows"),
            P(None, "rows"),
            P(),
            P(),
            P(),
            P(),
        ),
        check_vma=False,
    )
```

```python
import itertools
import math
from types import SimpleNamespace

import jax
import jax.numpy as jnp
from jax import lax
from jax.experimental import pallas as pl
from jax.experimental.pallas import tpu as pltpu
from jax.sharding import PartitionSpec as P

MESH = pl.DeviceIdType.MESH
EPSILON = 1e-05
VMEM_BYTES = 65400 * 2**10


def split(value):
    high = value.astype(jnp.bfloat16)
    return high, (value - high.astype(jnp.float32)).astype(jnp.bfloat16)


def put(pair_ref, index, value):
    high, low = split(value)
    pair_ref[(0,) + index] = high
    pair_ref[(1,) + index] = low


def product(stacked, weights, turned=False):
    result = lax.dot_general(
        stacked,
        weights,
        (((1,), (1 if turned else 0,)), ((), ())),
        preferred_element_type=jnp.float32,
    )
    half = result.shape[0] // 2
    return result[:half] + result[half:]


def small_product(value, weights, turned=False):
    return product(jnp.concatenate(split(value), 0), weights, turned)


def small_outer(left, right):
    def one(a, b):
        return lax.dot_general(
            a, b, (((0,), (0,)), ((), ())), preferred_element_type=jnp.float32
        )

    (a, b), (c, d) = split(left), split(right)
    return one(a, c) + one(a, d) + one(b, c)


def slope(value):
    logistic = jax.nn.sigmoid(value)
    return logistic * (1.0 + value * (1.0 - logistic))


def silu(value):
    return value * jax.nn.sigmoid(value)


def folded(value):
    return jnp.sum(value.reshape(-1, 8, value.shape[-1]), axis=0)


def moved_down(value):
    place = lax.broadcasted_iota(jnp.int32, value.shape, 0)
    return jnp.where(lax.rem(place, 8) == 0, 0.0, pltpu.roll(value, 1, 0))


def moved_up(value):
    place = lax.broadcasted_iota(jnp.int32, value.shape, 0)
    return jnp.where(lax.rem(place, 8) == 7, 0.0, pltpu.roll(value, value.shape[0] - 1, 0))


def chunks(total, step):
    def bind(body):
        @pl.loop(0, total // step)
        def _(place):
            body(pl.ds(pl.multiple_of(place * step, step), step))

    return bind


PUMPS = (1, 1, 1, 1, 1, 1, 1, 1, 1, 1, 1, 1)


def chain_kernel(names, dims, *refs):
    frames, rows, depth, a_count, b_count = dims
    m = SimpleNamespace(**dict(zip(names, refs)))
    f = lax.axis_index("frames")
    r = lax.axis_index("rows")
    after_f, before_f = lax.rem(f + 1, frames), lax.rem(f + frames - 1, frames)
    band = depth * 8
    half = 2 * band
    number_half = float(half * frames * rows)
    number_full = 4.0 * number_half
    above, below = r > 0, r < rows - 1
    above_one, below_one = jnp.where(above, 1.0, 0.0), jnp.where(below, 1.0, 0.0)
    wide = 2048

    loads = []

    def load(source, target, sem=None):
        if sem is None:
            sem = m.load_sem.at[len(loads)]
            loads.append(sem)
        copy = pltpu.make_async_copy(source, target, sem)
        copy.start()
        return copy

    def wait_row(row):
        block = m.xs.at[:, :, row]
        pltpu.make_async_copy(block, block, m.row_sem.at[row]).wait()

    lanes = [slice(k * 128, k * 128 + 128) for k in range(8)]

    def load_row(row):
        [
            load(m.x.at[:, row, :, lane], m.xs.at[k, :, row], m.row_sem.at[row])
            for k, lane in enumerate(lanes)
        ]

    for row in (3, 0, 1, 2):
        load_row(row)
    small_loads = [
        load(getattr(m, name + "_h"), getattr(m, name))
        for name in (
            "wer", "kst", "wex", "taps_in", "gain", "bias", "wide_gain", "wide_bias"
        )
    ]
    wn_load = load(m.wn_h, m.wn)
    wsk_load = load(m.wsk_h, m.wsk)
    ks_load = load(m.ks_h, m.ks)
    we_load = load(m.we_h, m.we)
    wcr_load = load(m.wcr_h, m.wcr)
    wce_load = load(m.wce_h, m.wce)
    kern_load = load(m.kern_h, m.kern)
    slope_loads = [load(m.slope_h.at[:, row], m.slope.at[row]) for row in range(2)]

    barrier = pltpu.get_barrier_semaphore()
    partners = [(f, lax.rem(r + step, rows)) for step in range(1, rows)]
    partners += [(lax.rem(f + step, frames), r) for step in range(1, frames)]
    for other in (after_f, before_f):
        partners += [(other, lax.rem(r + step, rows)) for step in range(1, rows)]
    if frames == 8:
        for chip_step in range(1, frames // 2):
            other = lax.rem(f + 2 * chip_step, frames)
            partners += [(other, lax.rem(r + step, rows)) for step in range(1, rows)]
    for partner in partners:
        pl.semaphore_signal(barrier, inc=1, device_id=partner, device_id_type=MESH)
    pl.semaphore_wait(barrier, len(partners))

    sent = []

    def send(source, target, send_sem, recv_sem, device):
        copy = pltpu.make_async_remote_copy(
            src_ref=source,
            dst_ref=target,
            send_sem=send_sem,
            recv_sem=recv_sem,
            device_id=device,
            device_id_type=MESH,
        )
        copy.start()
        return copy

    class Sum:
        count = 0

        def __init__(self, pieces):
            self.set = Sum.count % 2
            Sum.count += 1
            place = 0
            for piece in pieces:
                for k in range(piece.shape[1] // 128):
                    m.ar_in[self.set, place : place + 1, :] = piece[:, k * 128 : k * 128 + 128]
                    place += 1
            self.size = -(-place // 8) * 8
            half_f, core_f = f // 2, lax.rem(f, 2)
            self.first = (
                (m.ar_rows_a, m.ar_rows_b), m.ar_rs, m.ar_rr, r, rows, lambda other: (f, other)
            )
            self.second = (
                (m.ar_frames_a, m.ar_frames_b), m.ar_fs, m.ar_fr, f, frames, lambda other: (other, r)
            )
            if frames == 8 and self.size == 8:
                self.first = (
                    *self.first[:3], core_f, 2, lambda other: (f - core_f + other, r)
                )
                self.second = (
                    (m.ar_small.at[0], m.ar_small.at[1]), m.ar_fs, m.ar_fr,
                    half_f * rows + r, frames // 2 * rows,
                    lambda other: (other // rows * 2 + core_f, lax.rem(other, rows)),
                )
            self.copies = self.spread(m.ar_in, *self.first)

        def spread(self, source, slots, send_sem, recv_sem, me, count, device):
            piece = source.at[self.set, pl.ds(0, self.size)]
            copies = []
            for step in range(1, count):
                copies.append(
                    send(
                        piece,
                        slots[self.set].at[step, pl.ds(0, self.size)],
                        send_sem.at[self.set, step],
                        recv_sem.at[self.set, step],
                        device(lax.rem(me + step, count)),
                    )
                )
            return copies

        def gather(self, source, slots, send_sem, recv_sem, me, count, device):
            for copy in self.copies:
                copy.wait_recv()
            slots = slots[self.set]
            slots[0, : self.size] = source[self.set, : self.size]
            total = slots[me, : self.size]
            for other in range(1, count):
                spot = lax.rem(me + count - other, count)
                total = total + slots[spot, : self.size]
            return total

        def middle(self):
            first = self.copies
            m.ar_part[self.set, : self.size] = self.gather(m.ar_in, *self.first)
            self.copies = self.spread(m.ar_part, *self.second)
            for copy in first:
                copy.wait_send()

        def finish(self, *sizes):
            m.ar_out[: self.size] = self.gather(m.ar_part, *self.second)
            for copy in self.copies:
                copy.wait_send()
            results, place = [], 0
            for size in sizes:
                parts = []
                for k in range(size // 128):
                    parts.append(m.ar_out[place : place + 1, :])
                    place += 1
                results.append(jnp.concatenate(parts, axis=1))
            return results

        def all(self, *sizes):
            self.middle()
            return self.finish(*sizes)

    def settle(k, totals, squares, number, gain, bias):
        size = totals.shape[1]
        center = totals / number
        spread = lax.rsqrt(squares / number - center * center + EPSILON)
        scale = spread * gain
        m.vec[6 * k : 6 * k + 1, :size] = center
        m.vec[6 * k + 1 : 6 * k + 2, :size] = spread
        m.vec[6 * k + 2 : 6 * k + 3, :size] = scale
        m.vec[6 * k + 3 : 6 * k + 4, :size] = bias - center * scale

    def settle_back(k, bias_grad, gain_grad, number):
        size = bias_grad.shape[1]
        m.vec[6 * k + 4 : 6 * k + 5, :size] = bias_grad / number
        m.vec[6 * k + 5 : 6 * k + 6, :size] = gain_grad / number

    def vec(k, which, cols=slice(0, 512)):
        return m.vec[6 * k + which : 6 * k + which + 1, cols]

    def affine(k, value, cols=slice(0, 512)):
        return value * vec(k, 2, cols) + vec(k, 3, cols)

    def normed(k, value, cols=slice(0, 512)):
        return (value - vec(k, 0, cols)) * vec(k, 1, cols)

    def field_grad(k, grads, value, cols=slice(0, 512)):
        return vec(k, 2, cols) * (
            grads - vec(k, 4, cols) - normed(k, value, cols) * vec(k, 5, cols)
        )

    def clear():
        m.stat[...] = jnp.zeros_like(m.stat)

    def collect(k, value, cols=slice(0, 512)):
        m.stat[k, :, cols] = m.stat[k, :, cols] + folded(value)

    def collected(k, size=512):
        return jnp.sum(m.stat[k, :, :size], axis=0, keepdims=True)

    def column_tiles(body):
        @pl.loop(0, wide // 512)
        def _(place):
            body(pl.ds(pl.multiple_of(place * 512, 512), 512))

    c = lax.rem(f, 2)
    ib = lax.rem(f // 2, b_count)
    ia = f // (2 * b_count)
    flip1 = r + 1 - 2 * lax.rem(r, 2)
    flip2 = lax.rem(r + 2, rows)
    core = (f + 1 - 2 * c, r)
    thin = 512 // frames

    def a_peer(step):
        other = lax.rem(ia + step, a_count)
        return other, ((other * b_count + ib) * 2 + c, r)

    def b_peer(step):
        other = lax.rem(ib + step, b_count)
        return other, ((ia * b_count + other) * 2 + c, r)

    def add_blocks(target, source, lead=()):
        for index in itertools.product(*[range(size) for size in lead]):
            into, other = target.at[index], source.at[index]

            size = min(thin, 32 if into.shape[-1] > 128 else 64)

            @pl.loop(0, thin // size)
            def _(place):
                spot = pl.ds(pl.multiple_of(place * size, size), size)
                into[spot, :] = into[spot, :] + other[spot, :]

    def column_part(index):
        return pl.ds(pl.multiple_of(index * 128, 128), 128)

    ring = m.g_rows.shape[0]

    def unit_steps(fill, out, turn, kind):
        two, three, deep = turn % 2, turn % 3, turn % ring
        own, away, near = m.g_own.at[kind, two], m.g_away.at[kind], m.g_near.at[kind, two]
        bank = [m.g_send.at[kind, deep], m.g_recv.at[kind, deep]]
        used = [0]

        def go(source, target, device):
            spot = used[0]
            used[0] += 1
            return send(source, target, bank[0].at[spot], bank[1].at[spot], device)

        def done(copies):
            for copy in copies:
                copy.wait_recv()
            for copy in copies:
                copy.wait_send()

        def over_axis(count, peer, pick, buffer, lead):
            copies = []
            for step in range(1, count):
                other, device = peer(step)
                copies.append(go(pick(other), buffer.at[step - 1], device))
            yield
            done(copies)
            for step in range(2, count):
                add_blocks(buffer.at[0], buffer.at[step - 1], lead)

        def over_a(pick, buffer, lead):
            yield from over_axis(a_count, a_peer, pick, buffer, lead)
            add_blocks(buffer.at[0], pick(ia), lead)

        def over_b(pick, buffer, lead):
            yield from over_axis(b_count, b_peer, pick, buffer, lead)
            add_blocks(buffer.at[0], pick(ib), lead)

        def over_rows(pick, buffer, last, lead):
            copies = [go(pick(lax.rem(flip1, 2) + 2 * k), buffer.at[k], (f, flip1)) for k in range(2)]
            yield
            done(copies)
            for k in range(2):
                add_blocks(buffer.at[k], pick(lax.rem(r, 2) + 2 * k), lead)
            copies = [go(buffer.at[1 - r // 2], last, (f, flip2))]
            yield
            done(copies)
            add_blocks(last, buffer.at[r // 2], lead)

        fill(away, 1 - c)
        copies = [go(away, near, core)]
        fill(own, c)
        yield
        done(copies)
        add_blocks(own, near, (a_count, b_count))
        if kind == 0:
            first, second = m.g_first_p.at[deep], m.g_second_p.at[three]
            yield from over_b(lambda i: own.at[:, i], first, (a_count,))
            yield from over_a(lambda i: first.at[0, i], second, ())
        if kind == 1:
            first, second = m.g_first_q.at[deep], m.g_second_q.at[three]
            yield from over_a(lambda i: own.at[i], first, (b_count,))
            yield from over_b(lambda i: first.at[0, i], second, ())
        if kind < 2:
            final = m.g_fourth.at[kind, three]
            yield from over_rows(
                lambda i: second.at[0, :, column_part(i)], m.g_third.at[kind, three], final, ()
            )
        else:
            both = m.g_both.at[three]
            yield from over_rows(
                lambda i: own.at[:, :, :, column_part(i)],
                m.g_rows.at[deep],
                both,
                (a_count, b_count),
            )
            first, second = m.g_first_z.at[three], m.g_second_z.at[three]
            yield from over_a(lambda i: both.at[i], first, (b_count,))
            yield from over_b(lambda i: first.at[0, i], second, ())
            final = second.at[0]
        orders = ((b_count, b_peer), (a_count, a_peer))
        (one_count, one_peer), (two_count, two_peer) = orders[:: 1 if kind == 0 else -1]
        local = pltpu.make_async_copy(final, out.at[c, ia, ib], bank[1].at[used[0]])
        used[0] += 1
        local.start()
        copies = []
        for step in range(1, one_count):
            _, device = one_peer(step)
            copies.append(go(final, out.at[c, ia, ib], device))
        yield
        local.wait()
        done(copies)
        copies = []
        field = out.at[c, ia] if kind == 0 else out.at[c, :, ib]
        for step in range(1, two_count):
            _, device = two_peer(step)
            copies.append(go(field, field, device))
        yield
        done(copies)
        copies = [go(out.at[c], out.at[c], core)]
        yield
        done(copies)

    units, active, begun = [], [], [0]

    def advance():
        kept = []
        for age, group in active:
            group = [unit for unit in group if next(unit, active) is not active]
            if group:
                kept.append((age + 1, group))
        active[:] = kept
        if units:
            group = []
            for kind in range(3):
                if units:
                    fill, out = units.pop(0)
                    group.append(unit_steps(fill, out, begun[0], kind))
            begun[0] += 1
            for unit in group:
                next(unit)
            active.append((1, group))

    def pump(count):
        if count is None:
            while units or active:
                advance()
        else:
            for _ in range(count):
                advance()

    def begin_all_but(count):
        while len(units) > count:
            advance()

    def outer(left, right):
        def one(a, b):
            return lax.dot_general(
                a, b, (((0,), (0,)), ((), ())), preferred_element_type=jnp.float32
            )

        (high, low), (grad_high, grad_low) = left, right
        both = one(high, jnp.concatenate([grad_high, grad_low], 1))
        size = grad_high.shape[1]
        return both[:, :size] + both[:, size:] + one(low, grad_high)

    def blocks(value):
        return value.reshape(a_count, b_count, thin, value.shape[-1])

    def filler(left, right):
        def fill(target, which):
            start = pl.multiple_of(which * 256, 256)
            target[...] = blocks(
                outer([left(k, start) for k in range(2)], [right(k) for k in range(2)])
            )

        return fill

    def lanes_of(ref, quarter):
        def pick(k):
            return jnp.concatenate(
                [ref[k, :, z * 512 + quarter * 128 : z * 512 + quarter * 128 + 128] for z in range(4)],
                1,
            )

        return pick

    def whole(ref):
        return lambda k: ref[k]

    def rows_from(ref, base):
        return lambda k, start: ref[k, :, pl.ds(base + start, 256)]

    def out_lanes(ref, quarter):
        return ref.at[:, :, :, :, pl.ds(quarter * 128, 128)]

    def add_restorer():
        for quarter in range(4):
            units.append(
                (
                    filler(rows_from(m.squashed, 0), lanes_of(m.gc2, quarter)),
                    out_lanes(m.restorer, quarter),
                )
            )

    def add_widener():
        for quarter in range(4):
            units.append(
                (
                    filler(rows_from(m.h2, 0), lanes_of(m.uh, quarter)),
                    out_lanes(m.widener, quarter),
                )
            )

    def add_shortcut():
        def sampled(base):
            def pick(k, start):
                lane = pl.ds(base + start, 256)
                return jnp.concatenate(
                    [m.xb[k, pl.ds(row * half, band), lane] for row in (0, 2)], 0
                )

            return pick

        for quarter in range(4):
            for place in range(2):
                units.append(
                    (
                        filler(sampled(place * 512), lanes_of(m.gc2, quarter)),
                        out_lanes(m.shortcut.at[place], quarter),
                    )
                )

    def add_squeezer():
        for place in range(4):
            units.append(
                (filler(rows_from(m.uh, place * 512), whole(m.ga2)), m.squeezer.at[place])
            )

    def add_strider():
        def tapped(dy, base):
            def pick(k, start):
                lane = pl.ds(base + start, 256)
                return jnp.concatenate([m.pc[k, dy + 2 * i, :, lane] for i in range(2)], 0)

            return pick

        def grads(k):
            return jnp.concatenate([m.gb[k, i, :, 0:512] for i in range(2)], 0)

        for dy in range(3):
            for dx in range(3):
                units.append((filler(tapped(dy, dx * 512), grads), m.strider.at[dy * 3 + dx]))

    def add_narrower():
        def grads(k):
            return jnp.concatenate([m.uh[k, :, i * 512 : i * 512 + 512] for i in range(4)], 0)

        for place in range(2):
            units.append(
                (filler(rows_from(m.xb, place * 512), grads), m.narrower.at[place])
            )

    def one_hot(shape, places):
        row = lax.broadcasted_iota(jnp.int32, shape, 0)
        lane = lax.broadcasted_iota(jnp.int32, shape, 1)
        return jnp.where(row == places(lane), 1.0, 0.0).astype(jnp.bfloat16)

    def add_pack():
        def put_rows(start, z, value):
            spot = start % 64 // 16
            m.xs[z * 2 + start // 512, start % 512 // 64, spot : spot + 2] = value.reshape(2, 16, 128)

        for k in range(3):
            left = [m.gk[p, k] for p in range(2)]
            for dy in range(3):
                right = [
                    jnp.concatenate([m.mixed[p, k, i + dy] for i in range(2)], 0) for p in range(2)
                ]
                value = outer(left, right)
                for dx in range(3):
                    for z in range(4):
                        put_rows(
                            ((k * 3 + dy) * 3 + dx) * 32,
                            z,
                            value[z * 32 : z * 32 + 32, dx * 128 : dx * 128 + 128],
                        )

        def tap_places(lane):
            inside = lax.rem(lane, 128)
            return jnp.where(inside < 96, lax.div(lane, 128) * 96 + inside, -1)

        temporal = small_product(
            jnp.concatenate([m.temporal[...], jnp.zeros((5, 384), jnp.float32)], 0),
            one_hot((384, 512), tap_places),
        )
        for z in range(4):
            own_lanes = slice(z * 128, z * 128 + 128)
            eight = slice(z * 8, z * 8 + 8)
            put_rows(
                864,
                z,
                jnp.concatenate(
                    [m.condenser[eight, q * 128 : q * 128 + 128] for q in range(4)], 0
                ),
            )
            put_rows(
                896,
                z,
                jnp.concatenate(
                    [m.stencil[eight, q * 128 : q * 128 + 128] for q in range(3)]
                    + [temporal[:, own_lanes]],
                    0,
                ),
            )
            put_rows(928, z, m.exciter[:, own_lanes])

        for place in range(2):

            def fill(target, which, place=place):
                for lt in range(4):
                    value = m.xs[lt * 2 + place, pl.ds(which * 4, 4)]
                    target[:, :, :, lt * 128 : lt * 128 + 128] = blocks(value.reshape(256, 128))

            units.append((fill, m.pack.at[place]))


    for frame in range(depth):
        for mask, tall, flat_mask in (
            (m.place_of[frame] > 0, m.before_band, m.before16),
            (m.place_of[frame] < m.length_of[frame] - 1, m.after_band, m.after16),
        ):
            one = jnp.where(mask, 1.0, 0.0)
            tall[frame * 8 : frame * 8 + 8, :] = jnp.full((8, 128), one)
            flat_mask[frame : frame + 1, :] = jnp.full((1, 128), one)
    for flat_mask in (m.before16, m.after16):
        flat_mask[depth:, :] = jnp.zeros((flat_mask.shape[0] - depth, 128), jnp.float32)
    clear()

    @pl.when(r == 0)
    def _():
        m.a[0] = jnp.zeros(m.a.shape[1:], jnp.float32)

    @pl.when(r == rows - 1)
    def _():
        m.b_halo[...] = jnp.zeros_like(m.b_halo)
        m.back_halo[...] = jnp.zeros_like(m.back_halo)

    for buffers in (m.source, m.grad_pad):
        for k in range(buffers.shape[0]):

            @pl.when(r == 0)
            def _():
                buffers[k, 0] = jnp.zeros(buffers.shape[2:], jnp.float32)

            @pl.when(r == rows - 1)
            def _():
                buffers[k, 3] = jnp.zeros(buffers.shape[2:], jnp.float32)

    def reduce_row(row):
        @pl.loop(0, depth // 2)
        def _(pair):
            for parity in range(2):
                spot = pl.ds(parity, 8, stride=2)
                place = pl.multiple_of(row * half + parity * band + pair * 16, 16)
                for k, lane in enumerate(lanes):
                    value = jnp.concatenate(
                        [m.xs[k, 2 * pair, row, spot, :], m.xs[k, 2 * pair + 1, row, spot, :]], 0
                    )
                    put(m.xb, (pl.ds(place, 16), lane), value)

        place = pl.ds(pl.multiple_of(row * half, half), half)
        result = product(jnp.concatenate([m.xb[0, place, :], m.xb[1, place, :]], 0), m.wn[...])
        m.a[1 + row] = result.reshape(2, band, 512)
        collect(0, result)
        collect(1, result * result)

    wait_row(3)
    wn_load.wait()
    reduce_row(3)

    @pl.when(below)
    def _():
        send(m.a.at[4], m.a.at[0], m.halo_s.at[0], m.halo_r.at[0], (f, r + 1))

    for row in range(3):
        wait_row(row)

    @pl.loop(0, 3)
    def _(row):
        reduce_row(row)

    total = Sum([collected(0), collected(1)])
    clear()
    wsk_load.wait()

    def shortcut_tile(cols):
        lhs = jnp.concatenate(
            [m.xb[k, pl.ds(row * half, band), :] for k in range(2) for row in (0, 2)], 0
        )
        result = product(lhs, m.wsk[:, cols])
        m.s[:, cols] = result
        collect(2, result, cols)
        collect(3, result * result, cols)

    @pl.loop(0, 2)
    def _(place):
        shortcut_tile(pl.ds(pl.multiple_of(place * 512, 512), 512))

    total.middle()

    @pl.loop(2, 4)
    def _(place):
        shortcut_tile(pl.ds(pl.multiple_of(place * 512, 512), 512))

    totals, squares = total.finish(512, 512)
    for copy in small_loads:
        copy.wait()
    m.taps[...] = m.taps_in[...].astype(jnp.float32)
    settle(0, totals, squares, number_full, m.gain[0:1], m.bias[0:1])

    def activate(row, keep):
        @chunks(band, 32)
        def _(spot):
            for parity in range(2):
                value = silu(affine(0, m.a[row, parity, spot, :]))
                if keep is not None:
                    value = value * keep
                if parity == 0:
                    put(m.pc, (row, spot, slice(512, 1024)), value)
                else:
                    put(m.pc, (row, spot, slice(1024, 1536)), value)
                    put(m.pc, (row, spot, slice(0, 512)), moved_down(value))

    @pl.loop(1, 5)
    def _(row):
        activate(row, None)

    @pl.when(above)
    def _():
        pltpu.make_async_remote_copy(
            src_ref=m.a.at[4],
            dst_ref=m.a.at[0],
            send_sem=m.halo_s.at[0],
            recv_sem=m.halo_r.at[0],
            device_id=(f, lax.rem(r + 1, rows)),
            device_id_type=MESH,
        ).wait_recv()

    activate(0, above_one)
    ks_load.wait()

    def strided(dy):
        return product(
            jnp.concatenate([m.pc[k, dy + 2 * i] for k in range(2) for i in range(2)], 0), m.ks[dy]
        )

    m.b[...] = strided(0)
    m.b[...] = m.b[...] + strided(1)
    result = m.b[...] + strided(2)
    m.b[...] = result
    collect(0, result)
    collect(1, result * result)

    @pl.when(above)
    def _():
        send(
            m.b.at[pl.ds(0, band)], m.b_halo, m.halo_s.at[1], m.halo_r.at[1], (f, r - 1)
        )

    totals, squares, totals_p, squares_p = Sum(
        [collected(0), collected(1), collected(2, wide), collected(3, wide)]
    ).all(512, 512, wide, wide)
    clear()
    settle(1, totals, squares, number_half, m.gain[1:2], m.bias[1:2])
    settle(5, totals_p, squares_p, number_half, m.wide_gain[1:2], m.wide_bias[1:2])

    @chunks(half, 32)
    def _(spot):
        put(m.h2, (spot, slice(None)), silu(affine(1, m.b[spot, :])))

    we_load.wait()

    @column_tiles
    def _(cols):
        result = product(jnp.concatenate([m.h2[0], m.h2[1]], 0), m.we[:, cols])
        m.c[:, cols] = result
        collect(0, result, cols)
        collect(1, result * result, cols)

    totals, squares = Sum([collected(0, wide), collected(1, wide)]).all(wide, wide)
    clear()
    settle(4, totals, squares, number_half, m.wide_gain[0:1], m.wide_bias[0:1])

    def first_sum(spot, cols):
        return affine(4, m.c[spot, cols], cols) + affine(5, m.s[spot, cols], cols)

    @column_tiles
    def _(cols):
        @chunks(half, 32)
        def _(spot):
            value = silu(first_sum(spot, cols))
            put(m.uh, (spot, cols), value)

    wcr_load.wait()
    result = product(jnp.concatenate([m.uh[0], m.uh[1]], 0), m.wcr[...])
    m.d[...] = result
    collect(0, result)
    collect(1, result * result)
    totals, squares = Sum([collected(0), collected(1)]).all(512, 512)
    clear()
    settle(2, totals, squares, number_half, m.gain[2:3], m.bias[2:3])

    @chunks(half, 32)
    def _(spot):
        m.hid[spot, :] = silu(affine(2, m.d[spot, :]))

    m.edge[...] = jnp.zeros_like(m.edge)
    for row in range(2):
        block = m.hid[row * band : row * band + band, :]
        column = lax.rem(lax.broadcasted_iota(jnp.int32, block.shape, 0), 8)
        for k, value in enumerate(
            (block, jnp.where(column == 0, block, 0.0), jnp.where(column == 7, block, 0.0))
        ):
            m.edge[k, row, :depth] = jnp.sum(value.reshape(depth, 8, 512), axis=1)
    pad = m.edge.shape[2]
    reduced = small_product(m.edge[...].reshape(6 * pad, 512), m.wer[...], True)

    def part(kind, row):
        start = (kind * 2 + row) * pad
        return reduced[start : start + pad]

    taps = []
    for dy in range(3):
        for dx in range(3):
            by_row = []
            for row in range(2):
                value = part(0, row)
                if dx == 0:
                    value = value - part(2, row)
                if dx == 2:
                    value = value - part(1, row)
                by_row.append(value)
            if dy == 0:
                by_row[1] = by_row[1] * below_one
            if dy == 2:
                by_row[0] = by_row[0] * above_one
            taps.append(by_row[0] + by_row[1])
    taps.append(jnp.zeros((pad, 96), jnp.float32))
    m.tap_in[...] = jnp.concatenate(taps, 1)

    def rows_sum(source, slots, near, near_slots, toward, sems):
        copies = []
        for step in range(1, rows):
            copies.append(
                send(
                    source,
                    slots.at[step],
                    m.rows_s.at[sems, step],
                    m.rows_r.at[sems, step],
                    (f, lax.rem(r + step, rows)),
                )
            )
        for step in range(rows):
            copies.append(
                send(
                    source.at[near],
                    near_slots.at[step],
                    m.rows_s.at[sems, rows + step],
                    m.rows_r.at[sems, rows + step],
                    (toward, lax.rem(r + step, rows)),
                )
            )
        slots[0] = source[...]
        for copy in copies:
            copy.wait_recv()
        total = slots[r]
        other_total = near_slots[r]
        for other in range(1, rows):
            spot = lax.rem(r + rows - other, rows)
            total = total + slots[spot]
            other_total = other_total + near_slots[spot]
        for copy in copies:
            copy.wait_send()
        return total, other_total

    current, later = rows_sum(
        m.tap_in, m.tap_slots, pl.ds(0, 8), m.tap_near, before_f, 0
    )
    place = lax.broadcasted_iota(jnp.int32, current.shape, 0)
    follow = pltpu.roll(current, pad - 1, 0)
    follow = jnp.where(place == depth - 1, later[0:1], follow)
    after16 = m.after16[...]
    before16 = m.before16[...]
    follow = jnp.where(place < depth, follow, 0.0) * jnp.concatenate([after16] * 3, 1)
    m.follow[...] = follow
    area = float(16 * rows)
    pooled = (
        (small_product(follow[:, :288], m.kst[...]) - current[:, 128:160])
        * after16[:, :32]
        / area
    )
    m.pooled[...] = pooled
    m.gate[...] = jax.nn.sigmoid(small_product(pooled, m.wex[...]))
    for frame in range(depth):
        m.gate_all[frame * 8 : frame * 8 + 8, :] = jnp.broadcast_to(
            1.0 + m.gate[frame : frame + 1, :], (8, 512)
        )

    def halo(field, sems, pumps=0):
        own, first, last = pl.ds(8, band), pl.ds(8, 8), pl.ds(band, 8)
        low, high = pl.ds(0, 8), pl.ds(band + 8, 8)
        moves = [
            (field.at[pl.ds(1, 2), last], field.at[pl.ds(1, 2), low], (after_f, r), None, None),
            (field.at[pl.ds(1, 2), first], field.at[pl.ds(1, 2), high], (before_f, r), None, None),
            (field.at[2, own], field.at[0, own], (f, r + 1), below, above),
            (field.at[1, own], field.at[3, own], (f, r - 1), above, below),
            (field.at[2, last], field.at[0, low], (after_f, r + 1), below, above),
            (field.at[1, last], field.at[3, low], (after_f, r - 1), above, below),
            (field.at[2, first], field.at[0, high], (before_f, r + 1), below, above),
            (field.at[1, first], field.at[3, high], (before_f, r - 1), above, below),
        ]
        copies = []
        for k, (source, target, device, able, arriving) in enumerate(moves):
            copies.append(
                pltpu.make_async_remote_copy(
                    src_ref=source,
                    dst_ref=target,
                    send_sem=m.ring_s.at[sems % 2, k],
                    recv_sem=m.ring_r.at[sems % 2, k],
                    device_id=device,
                    device_id_type=MESH,
                )
            )
        for copy, move in zip(copies, moves):
            if move[3] is None:
                copy.start()
            else:
                pl.when(move[3])(copy.start)
        pump(pumps)
        for copy, move in zip(copies, moves):
            if move[4] is None:
                copy.wait_recv()
            else:
                pl.when(move[4])(copy.wait_recv)
        for copy, move in zip(copies, moves):
            if move[3] is None:
                copy.wait_send()
            else:
                pl.when(move[3])(copy.wait_send)

    own = pl.ds(8, band)
    previous, following = pl.ds(0, band), pl.ds(16, band)
    before_band = m.before_band[...]
    after_band = m.after_band[...]

    def sides(value):
        return jnp.concatenate([moved_down(value), value, moved_up(value)], 1)

    m.merged[:, 0:128] = jnp.concatenate(
        [m.hid[i * band : i * band + band, 0:128] * m.gate_all[:, 0:128] for i in range(2)], 0
    )
    kern_load.wait()
    for k in range(3):
        cols = slice((k + 1) * 128, (k + 2) * 128)
        for i in range(2):
            rows_i = slice(i * band, i * band + band)
            value = m.hid[rows_i, cols] * m.gate_all[:, cols]
            if k > 0:
                value = value + m.merged[rows_i, k * 128 : (k + 1) * 128]
            m.source[k, 1 + i, own] = value
        halo(m.source.at[k], k)
        tap = [m.taps[i : i + 1, k * 128 : (k + 1) * 128] for i in range(3)]
        for i in range(4):
            mixed = (
                tap[0] * before_band * m.source[k, i, previous]
                + tap[1] * m.source[k, i, own]
                + tap[2] * after_band * m.source[k, i, following]
            )
            put(m.mixed, (k, i), sides(mixed))
        result = jnp.zeros((half, 128), jnp.float32)
        for dy in range(3):
            lhs = jnp.concatenate([m.mixed[p, k, i + dy] for p in range(2) for i in range(2)], 0)
            result = result + product(lhs, m.kern[k, dy])
        m.merged[:, cols] = result

    result = m.merged[...]
    collect(0, result)
    collect(1, result * result)
    totals, squares = Sum([collected(0), collected(1)]).all(512, 512)
    clear()
    settle(3, totals, squares, number_half, m.gain[3:4], m.bias[3:4])

    @chunks(half, 32)
    def _(spot):
        put(m.squashed, (spot, slice(None)), silu(affine(3, m.merged[spot, :])))

    wce_load.wait()

    @column_tiles
    def _(cols):
        result = product(jnp.concatenate([m.squashed[0], m.squashed[1]], 0), m.wce[:, cols])
        m.e[:, cols] = result
        collect(0, result, cols)
        collect(1, result * result, cols)

    totals, squares = Sum([collected(0, wide), collected(1, wide)]).all(wide, wide)
    clear()
    settle(6, totals, squares, number_half, m.wide_gain[2:3], m.wide_bias[2:3])

    for copy in slope_loads:
        copy.wait()

    @column_tiles
    def _(cols):
        for row in range(2):

            @pl.loop(0, depth // 4)
            def _(part_place):
                block = pl.ds(pl.multiple_of(part_place * 4, 4), 4)
                spot = pl.ds(pl.multiple_of(row * band + part_place * 32, 32), 32)
                raw = m.e[spot, cols]
                value = (
                    affine(6, raw, cols)
                    + m.uh[0, spot, cols].astype(jnp.float32)
                    + m.uh[1, spot, cols].astype(jnp.float32)
                )
                logistic = jax.nn.sigmoid(value)
                grads = m.slope[row, block, :, cols].reshape(32, 512) * (
                    logistic * (1.0 + value * (1.0 - logistic))
                )
                m.slope[row, block, :, cols] = (value * logistic).reshape(4, 8, 512)
                m.d2[spot, cols] = grads
                collect(0, grads, cols)
                collect(1, grads * normed(6, raw, cols), cols)

    stores = []

    def store(source, target, sem=None):
        copy = pltpu.make_async_copy(source, target, m.store_sem.at[len(stores)] if sem is None else sem)
        copy.start()
        if sem is None:
            stores.append(copy)

    for row in range(2):
        store(m.slope.at[row], m.layer_output.at[:, row])

    bias_grad, gain_grad = Sum([collected(0, wide), collected(1, wide)]).all(wide, wide)
    clear()
    settle_back(6, bias_grad, gain_grad, number_half)
    m.baselines[2:3] = bias_grad
    m.amplitudes[2:3] = gain_grad

    @column_tiles
    def _(cols):
        @chunks(half, 32)
        def _(spot):
            put(m.gc2, (spot, cols), field_grad(6, m.d2[spot, cols], m.e[spot, cols], cols))


    def back_through(pair, weights, raw, k):
        m.back[...] = product(jnp.concatenate([pair[0], pair[1]], 0), weights[...], True)

        @chunks(half, 32)
        def _(spot):
            value = raw[spot, :]
            grads = m.back[spot, :] * slope(affine(k, value))
            m.back[spot, :] = grads
            collect(0, grads)
            collect(1, grads * normed(k, value))

    back_through(m.gc2, m.wce, m.merged, 3)
    add_restorer()
    total = Sum([collected(0), collected(1)])
    pump(PUMPS[0])
    bias_grad, gain_grad = total.all(512, 512)
    clear()
    settle_back(3, bias_grad, gain_grad, number_half)
    m.biasing[3:4] = bias_grad
    m.scaling[3:4] = gain_grad
    merged_grad = field_grad(3, m.back[...], m.merged[...])
    m.eg[...] = merged_grad

    for k in (2, 1, 0):
        cols = slice((k + 1) * 128, (k + 2) * 128)
        grads = m.eg[:, cols]
        if k < 2:
            grads = grads + m.eg[:, (k + 2) * 128 : (k + 3) * 128]
        put(m.gk, (k,), grads)
        for i in range(2):
            m.grad_pad[k % 2, 1 + i, own] = grads[i * band : i * band + band]
        halo(m.grad_pad.at[k % 2], 3 + k, PUMPS[1 + k])
        for i in range(4):
            put(m.grad_sides, (i,), sides(m.grad_pad[k % 2, i]))
        result = jnp.zeros((2 * (band + 16), 128), jnp.float32)
        for dy in range(3):
            lhs = jnp.concatenate([m.grad_sides[p, i + dy] for p in range(2) for i in range(2)], 0)
            for dx in range(3):
                result = result + product(
                    lhs[:, dx * 128 : dx * 128 + 128],
                    m.kern[k, 2 - dy, (2 - dx) * 128 : (3 - dx) * 128, :],
                    True,
                )
        span = band + 16
        tap = [m.taps[i : i + 1, k * 128 : (k + 1) * 128] for i in range(3)]
        tap_grads = [0.0, 0.0, 0.0]
        for i in range(2):
            m.mixed_grad[i] = result[i * span : i * span + span]
            middle = m.mixed_grad[i, own]
            for j, value in enumerate(
                (
                    middle * before_band * m.source[k, 1 + i, previous],
                    middle * m.source[k, 1 + i, own],
                    middle * after_band * m.source[k, 1 + i, following],
                )
            ):
                tap_grads[j] = tap_grads[j] + jnp.sum(value, axis=0, keepdims=True)
            m.eg[i * band : i * band + band, cols] = (
                tap[2] * before_band * m.mixed_grad[i, previous]
                + tap[1] * middle
                + tap[0] * after_band * m.mixed_grad[i, following]
            )
        for j in range(3):
            m.temporal[j : j + 1, k * 128 : (k + 1) * 128] = tap_grads[j]


    gate = m.gate[...]
    m.gate_part[...] = jnp.zeros_like(m.gate_part)
    touched = m.eg[...] * m.hid[...]
    touched = jnp.sum(touched.reshape(2 * depth, 8, 512), axis=1)
    m.gate_part[:depth] = touched[:depth] + touched[depth:]
    m.gate_part[...] = m.gate_part[...] * gate * (1.0 - gate)
    current, earlier = rows_sum(
        m.gate_part, m.gate_slots, pl.ds(pad - 8, 8), m.gate_near, after_f, 1
    )
    place = lax.broadcasted_iota(jnp.int32, current.shape, 0)
    last_row = depth - 1 - (pad - 8)
    shifted = jnp.where(place == 0, earlier[last_row : last_row + 1], pltpu.roll(current, 1, 0))
    pooled_grads = small_product(jnp.concatenate([current, shifted], 0), m.wex[...], True) / area
    motion = pooled_grads[:pad] * after16[:, :32]
    motion_before = pooled_grads[pad:] * before16[:, :32]
    spread = small_product(motion_before, m.kst[...], True)

    def tap_value(dy, dx):
        start = (dy * 3 + dx) * 32
        return spread[:, start : start + 32]

    values = []
    by_row = []
    for row in range(2):
        columns = []
        for dx in range(3):
            if row == 0:
                value = tap_value(0, dx) + tap_value(1, dx)
                value = value + tap_value(2, dx) * above_one
            else:
                value = tap_value(1, dx) + tap_value(2, dx)
                value = value + tap_value(0, dx) * below_one
            columns.append(value)
        by_row.append(columns)
    for kind in range(3):
        for row in range(2):
            d0, d1, d2 = by_row[row]
            value = (d0 + d1 + d2, d0 + d1, d1 + d2)[kind]
            values.append(value - motion)
    reduced_grad = jnp.concatenate(values, 0)
    m.e[: 6 * pad, :512] = small_product(reduced_grad, m.wer[...])

    for row in range(2):

        @pl.loop(0, depth)
        def _(frame):
            spot = pl.ds(pl.multiple_of(row * band + frame * 8, 8), 8)

            def edge_line(kind):
                return m.e[pl.ds((kind * 2 + row) * pad + frame, 1), 0:512]

            column = lax.broadcasted_iota(jnp.int32, (8, 512), 0)
            extra = jnp.where(
                column == 0,
                edge_line(1),
                jnp.where(column == 7, edge_line(2), edge_line(0)),
            )
            raw = m.d[spot, :]
            grads = m.eg[spot, :] * m.gate_all[pl.ds(pl.multiple_of(frame * 8, 8), 8), :] + extra
            grads = grads * slope(affine(2, raw))
            m.back[spot, :] = grads
            collect(0, grads)
            collect(1, grads * normed(2, raw))

    total = Sum([collected(0), collected(1)])
    m.exciter[...] = small_outer(m.pooled[...], m.gate_part[...])
    m.stencil[...] = small_outer(motion, m.follow[...]) * (1.0 / rows)
    edges = jnp.concatenate([m.edge[0] - m.edge[1] - m.edge[2], m.edge[1], m.edge[2]], 0)
    m.condenser[...] = small_outer(reduced_grad, edges.reshape(6 * pad, 512))
    add_pack()
    pump(PUMPS[4])
    bias_grad, gain_grad = total.all(512, 512)
    clear()
    settle_back(2, bias_grad, gain_grad, number_half)
    m.biasing[2:3] = bias_grad
    m.scaling[2:3] = gain_grad

    @chunks(half, 32)
    def _(spot):
        put(m.ga2, (spot, slice(None)), field_grad(2, m.back[spot, :], m.d[spot, :]))


    @column_tiles
    def _(cols):
        m.e[:, cols] = product(jnp.concatenate([m.ga2[0], m.ga2[1]], 0), m.wcr[cols, :], True)

        @chunks(half, 32)
        def _(spot):
            grads = (m.d2[spot, cols] + m.e[spot, cols]) * slope(first_sum(spot, cols))
            m.d2[spot, cols] = grads
            collect(0, grads, cols)
            collect(1, grads * normed(4, m.c[spot, cols], cols), cols)
            collect(2, grads * normed(5, m.s[spot, cols], cols), cols)

    add_squeezer()
    total = Sum([collected(0, wide), collected(1, wide), collected(2, wide)])
    pump(PUMPS[5])
    total.middle()
    pump(PUMPS[6])
    bias_grad, gain_c, gain_p = total.finish(wide, wide, wide)
    clear()
    settle_back(4, bias_grad, gain_c, number_half)
    settle_back(5, bias_grad, gain_p, number_half)
    for k in range(2):
        m.baselines[k : k + 1] = bias_grad
    m.amplitudes[0:1] = gain_c
    m.amplitudes[1:2] = gain_p

    begin_all_but(0)

    @column_tiles
    def _(cols):
        @chunks(half, 32)
        def _(spot):
            grads = m.d2[spot, cols]
            put(m.uh, (spot, cols), field_grad(4, grads, m.c[spot, cols], cols))
            put(m.gc2, (spot, cols), field_grad(5, grads, m.s[spot, cols], cols))

    back_through(m.uh, m.we, m.b, 1)

    @pl.when(above)
    def _():
        send(
            m.back.at[pl.ds(0, band)], m.back_halo, m.halo_s.at[2], m.halo_r.at[2], (f, r - 1)
        )

    total = Sum([collected(0), collected(1)])
    clear()
    add_widener()
    add_shortcut()
    pump(PUMPS[7])

    for cols in (slice(0, 512), slice(512, 1024)):
        if cols.start:
            total.middle()
            pump(PUMPS[8])
        m.d2[:, cols] = product(jnp.concatenate([m.gc2[0], m.gc2[1]], 0), m.wsk[cols, :], True)

    bias_grad, gain_grad = total.finish(512, 512)
    settle_back(1, bias_grad, gain_grad, number_half)
    m.biasing[1:2] = bias_grad
    m.scaling[1:2] = gain_grad

    def strided_grad(row, spot, value):
        put(m.gb, (row, spot, slice(0, 512)), value)
        put(m.gb, (row, spot, slice(512, 1024)), moved_up(value))

    for row in range(2):

        @chunks(band, 32)
        def _(spot):
            place = pl.ds(pl.multiple_of(row * band + spot.start, 32), 32)
            strided_grad(row, spot, field_grad(1, m.back[place, :], m.b[place, :]))

    @pl.when(below)
    def _():
        for k, (source, target) in enumerate(((m.b, m.b_halo), (m.back, m.back_halo))):
            pltpu.make_async_remote_copy(
                src_ref=source.at[pl.ds(0, band)],
                dst_ref=target,
                send_sem=m.halo_s.at[1 + k],
                recv_sem=m.halo_r.at[1 + k],
                device_id=(f, lax.rem(r + 1, rows)),
                device_id_type=MESH,
            ).wait_recv()

    @chunks(band, 32)
    def _(spot):
        value = field_grad(1, m.back_halo[spot, :], m.b_halo[spot, :])
        strided_grad(2, spot, value * below_one)


    add_strider()
    pump(PUMPS[9])

    def gb_rows(first, variant):
        lanes = slice(variant * 512, variant * 512 + 512)
        return jnp.concatenate([m.gb[k, first + i, :, lanes] for k in range(2) for i in range(2)], 0)

    def tap_weights(dy, dx):
        return m.ks[dy, dx * 512 : dx * 512 + 512, :]

    @pl.when(above)
    def _():
        for k, source in enumerate((m.b, m.back)):
            pltpu.make_async_remote_copy(
                src_ref=source.at[pl.ds(0, band)],
                dst_ref=m.back_halo,
                send_sem=m.halo_s.at[1 + k],
                recv_sem=m.halo_r.at[1 + k],
                device_id=(f, lax.rem(r + 1, rows)),
                device_id_type=MESH,
            ).wait_send()

    def ha_rows(parity, spot):
        return pl.ds(pl.multiple_of(parity * band + spot.start, 32), 32)

    plan = {
        (0, 0): [(0, 0, 1, 1)],
        (1, 0): [(0, 0, 1, 2), (0, 1, 1, 0)],
        (0, 1): [(0, 0, 2, 1), (1, 0, 0, 1)],
        (1, 1): [(0, 0, 2, 2), (1, 0, 0, 2), (0, 1, 2, 0), (1, 1, 0, 0)],
    }
    for (parity, odd), terms in plan.items():
        result = None
        for first, variant, dy, dx in terms:
            value = product(gb_rows(first, variant), tap_weights(dy, dx), True)
            result = value if result is None else result + value
        m.back[...] = result
        for i in range(2):
            row = 2 * i + odd

            @chunks(band, 32)
            def _(spot):
                place = pl.ds(pl.multiple_of(i * band + spot.start, 32), 32)
                raw = m.a[1 + row, parity, spot, :]
                grads = m.back[place, :] * slope(affine(0, raw))
                m.e[ha_rows(parity, spot), row * 512 : row * 512 + 512] = grads
                collect(0, grads)
                collect(1, grads * normed(0, raw))

    total = Sum([collected(0), collected(1)])
    pump(PUMPS[10])
    total.middle()
    pump(PUMPS[11])
    bias_grad, gain_grad = total.finish(512, 512)
    settle_back(0, bias_grad, gain_grad, number_full)
    begin_all_but(17)
    m.biasing[0:1] = bias_grad
    m.scaling[0:1] = gain_grad

    @pl.loop(0, 4)
    def _(row):
        for parity in range(2):

            @chunks(band, 32)
            def _(spot):
                lane = pl.ds(pl.multiple_of(row * 512, 512), 512)
                value = field_grad(
                    0, m.e[ha_rows(parity, spot), lane], m.a[1 + row, parity, spot, :]
                )
                put(m.uh, (ha_rows(parity, spot), lane), value)

    add_narrower()
    pump(1)

    def pixel_row(row):
        lane = pl.ds(pl.multiple_of(row * 512, 512), 512)
        lhs = jnp.concatenate([m.uh[0, :, lane], m.uh[1, :, lane]], 0)
        for part_cols in (slice(0, 512), slice(512, 1024)):
            result = product(lhs, m.wn[part_cols, :], True)
            even = jnp.where(lax.rem(row, 2) == 0, 1.0, 0.0)
            shortcut = m.d2[pl.ds(pl.multiple_of((row // 2) * band, band), band), part_cols]
            for parity in range(2):
                value = result[parity * band : parity * band + band]
                if parity == 0:
                    value = value + shortcut * even
                for frame in range(depth):
                    for k in range(4):
                        m.xs[
                            part_cols.start // 128 + k, frame, row, pl.ds(parity, 8, stride=2), :
                        ] = value[frame * 8 : frame * 8 + 8, k * 128 : k * 128 + 128]

    for part_rows in ((0, 2), (2, 4)):
        pl.loop(*part_rows)(pixel_row)
        for row in range(*part_rows):
            for k, lane in enumerate(lanes):
                store(m.xs.at[k, :, row], m.pixels.at[:, row, :, lane], m.row_sem.at[row])
        if part_rows[0] == 0:
            pump(1)
    for name in ("scaling", "biasing", "amplitudes", "baselines"):
        store(getattr(m, name), getattr(m, name + "_h"))
    pump(None)
    for copy in stores:
        copy.wait()
    for row in range(4):
        wait_row(row)

    @pl.when(below)
    def _():
        pltpu.make_async_remote_copy(
            src_ref=m.a.at[4],
            dst_ref=m.a.at[0],
            send_sem=m.halo_s.at[0],
            recv_sem=m.halo_r.at[0],
            device_id=(f, lax.rem(r + 1, rows)),
            device_id_type=MESH,
        ).wait_send()


def chain(
    x, place_of, length_of, wn, ks, we, wsk, wcr, wer, kst, wex, taps, kern, wce, gain, bias, wide_gain,
    wide_bias, slopes, call,
):
    frames, rows = lax.axis_size("frames"), lax.axis_size("rows")
    depth = x.shape[0]
    band, pad = depth * 8, -(-depth // 16) * 16
    half = 2 * band
    span = band + 16
    levels = int(math.log2(frames // 2))
    b_count = 2 ** (levels // 2)
    a_count = frames // 2 // b_count
    thin = 512 // frames
    blocks = (2, a_count, b_count, thin)
    unit = (a_count, b_count, thin, 512)
    copies = 6 + 2 * (a_count + b_count - 2)
    ring = 3
    hbm, smem = pl.BlockSpec(memory_space=pl.ANY), pl.BlockSpec(memory_space=pltpu.SMEM)

    inputs = dict(
        x=(x, hbm), slope_h=(slopes, hbm), wn_h=(wn, hbm), wsk_h=(wsk, hbm), ks_h=(ks, hbm),
        we_h=(we, hbm), wcr_h=(wcr, hbm), wce_h=(wce, hbm), kern_h=(kern, hbm), wer_h=(wer, hbm),
        kst_h=(kst, hbm), wex_h=(wex, hbm), taps_in_h=(taps, hbm), gain_h=(gain, hbm),
        bias_h=(bias, hbm), wide_gain_h=(wide_gain, hbm), wide_bias_h=(wide_bias, hbm),
        place_of=(place_of, smem), length_of=(length_of, smem),
    )

    def wide_of(*shape):
        return jax.ShapeDtypeStruct(shape, jnp.float32)

    kept = dict(
        xb=(2, 4 * half, 1024), pc=(2, 5, band, 1536), h2=(2, half, 512), uh=(2, half, 2048),
        squashed=(2, half, 512), mixed=(2, 3, 4, band, 384), gc2=(2, half, 2048),
        gk=(2, 3, half, 128), ga2=(2, half, 512),
        gb=(2, 3, band, 1024),
    )
    outputs = dict(
        layer_output=(wide_of(depth, 2, 8, 2048), hbm), pixels=(wide_of(depth, 4, 16, 1024), hbm),
        scaling_h=(wide_of(4, 512), hbm), biasing_h=(wide_of(4, 512), hbm),
        amplitudes_h=(wide_of(3, 2048), hbm), baselines_h=(wide_of(3, 2048), hbm),
        narrower=(wide_of(2, *blocks, 128), hbm), strider=(wide_of(9, *blocks, 128), hbm),
        widener=(wide_of(*blocks, 512), hbm), shortcut=(wide_of(2, *blocks, 512), hbm),
        squeezer=(wide_of(4, *blocks, 128), hbm), restorer=(wide_of(*blocks, 512), hbm),
        pack=(wide_of(2, *blocks, 128), hbm),
    )

    def f32(*shape):
        return pltpu.VMEM(shape, jnp.float32)

    def b16(*shape):
        return pltpu.VMEM(shape, jnp.bfloat16)

    def sems(*shape):
        return pltpu.SemaphoreType.DMA(shape)

    scratch = dict(
        wn=b16(1024, 512), wsk=b16(1024, 2048), ks=b16(3, 1536, 512), we=b16(512, 2048),
        wcr=b16(2048, 512), wce=b16(512, 2048), kern=b16(3, 3, 384, 128),
        xs=f32(8, depth, 4, 16, 128), a=f32(5, 2, band, 512), b=f32(half, 512), c=f32(half, 2048),
        s=f32(half, 2048), d=f32(half, 512), hid=f32(half, 512),
        merged=f32(half, 512), e=f32(half, 2048),
        slope=f32(2, depth, 8, 2048), d2=f32(half, 2048), back=f32(half, 512), eg=f32(half, 512),
        b_halo=f32(band, 512),
        back_halo=f32(band, 512), source=f32(3, 4, span, 128), grad_pad=f32(2, 4, span, 128),
        mixed_grad=f32(2, span, 128), grad_sides=b16(2, 4, span, 384), gate_all=f32(band, 512),
        edge=f32(3, 2, pad, 512), gate=f32(pad, 512),
        gate_part=f32(pad, 512), pooled=f32(pad, 32), follow=f32(pad, 384), tap_in=f32(pad, 384),
        tap_slots=f32(rows, pad, 384), tap_near=f32(rows, 8, 384), gate_slots=f32(rows, pad, 512),
        gate_near=f32(rows, 8, 512), stat=f32(4, 8, 2048), vec=f32(48, 2048), ar_in=f32(2, 48, 128),
        ar_part=f32(2, 48, 128), ar_out=f32(48, 128), ar_rows_a=f32(rows, 32, 128), ar_rows_b=f32(rows, 48, 128),
        ar_frames_a=f32(frames, 32, 128), ar_frames_b=f32(frames, 48, 128), ar_rs=sems(2, rows), ar_rr=sems(2, rows),
        ar_fs=sems(2, max(frames, 16)), ar_fr=sems(2, max(frames, 16)),
        ar_small=f32(2, 16, 8, 128), rows_s=sems(2, 2 * rows),
        rows_r=sems(2, 2 * rows), ring_s=sems(2, 8), ring_r=sems(2, 8), halo_s=sems(3),
        halo_r=sems(3), condenser=f32(32, 512), stencil=f32(32, 384), exciter=f32(32, 512),
        temporal=f32(3, 384), wer=b16(32, 512), kst=b16(288, 32), wex=b16(32, 512),
        taps_in=b16(3, 384), taps=f32(3, 384), gain=f32(4, 512), bias=f32(4, 512),
        wide_gain=f32(3, 2048), wide_bias=f32(3, 2048), before16=f32(pad, 128),
        after16=f32(pad, 128), before_band=f32(band, 128), after_band=f32(band, 128),
        scaling=f32(4, 512), biasing=f32(4, 512), amplitudes=f32(3, 2048), baselines=f32(3, 2048),
        g_own=f32(3, 2, *unit), g_away=f32(3, *unit), g_near=f32(3, 2, *unit),
        g_first_p=f32(ring, b_count - 1, a_count, thin, 512),
        g_first_q=f32(ring, a_count - 1, b_count, thin, 512),
        g_second_p=f32(3, a_count - 1, thin, 512), g_second_q=f32(3, b_count - 1, thin, 512),
        g_third=f32(2, 3, 2, thin, 128), g_fourth=f32(2, 3, thin, 128),
        g_rows=f32(ring, 2, a_count, b_count, thin, 128), g_both=f32(3, a_count, b_count, thin, 128),
        g_first_z=f32(3, a_count - 1, b_count, thin, 128),
        g_second_z=f32(3, b_count - 1, thin, 128),
        g_send=sems(3, ring, copies), g_recv=sems(3, ring, copies),
        load_sem=sems(20), store_sem=sems(8), row_sem=sems(4),
    )
    for name in kept:
        scratch[name] = b16(*kept[name])
    names = list(inputs) + list(outputs) + list(scratch)
    results = pl.pallas_call(
        lambda *refs: chain_kernel(names, (frames, rows, depth, a_count, b_count), *refs),
        out_shape=[shape for shape, _ in outputs.values()],
        in_specs=[spec for _, spec in inputs.values()],
        out_specs=[spec for _, spec in outputs.values()],
        scratch_shapes=list(scratch.values()),
        compiler_params=pltpu.CompilerParams(
            collective_id=call, has_side_effects=True, vmem_limit_bytes=VMEM_BYTES
        ),
    )(*[value for value, _ in inputs.values()])
    return SimpleNamespace(**dict(zip(outputs, results)))


def finish_kernel(count, *refs):
    pack, refs = refs[0], refs[1:]
    sources, refs = refs[:count], refs[count:]
    targets, refs = refs[:count], refs[count:]
    condenser, stencil, exciter, temporal, kernels, tail = refs[:6]
    held, in_sems, out_sems = refs[6:-2], refs[-2], refs[-1]
    first = [
        pltpu.make_async_copy(source, block, in_sems.at[k])
        for k, (source, block) in enumerate(zip(sources, held))
    ]
    first.append(pltpu.make_async_copy(pack, tail, in_sems.at[count]))
    for copy in first:
        copy.start()
    second = []

    def put_out(source, target):
        copy = pltpu.make_async_copy(source, target, out_sems.at[len(second)])
        copy.start()
        second.append(copy)

    for copy, block, target in zip(first, held, targets):
        copy.wait()
        put_out(block, target)
    first[-1].wait()
    for tap in range(27):
        kernels[tap] = tail[tap * 32 : tap * 32 + 32, :]
    for q in range(4):
        condenser[:, q * 128 : q * 128 + 128] = tail[864 + q * 8 : 872 + q * 8, :]
    exciter[...] = tail[928:960, :]
    for tap in range(9):
        start, lane = 896 + tap // 4 * 8, tap % 4 * 32
        stencil[tap] = tail[start : start + 8, lane : lane + 32]
    temporal[...] = tail[920:923, :96]
    for copy in second:
        copy.wait()


def finish(pack, arrays):
    hbm, vmem = pl.BlockSpec(memory_space=pl.ANY), pl.BlockSpec(memory_space=pltpu.VMEM)
    shapes = [array.shape for array in arrays]
    shapes += [(8, 512), (9, 8, 32), (32, 128), (3, 96), (27, 32, 128)]
    count = len(arrays)
    return pl.pallas_call(
        lambda *refs: finish_kernel(count, *refs),
        out_shape=[jax.ShapeDtypeStruct(shape, jnp.float32) for shape in shapes],
        in_specs=[hbm] * (count + 1),
        out_specs=[hbm] * count + [vmem] * 5,
        scratch_shapes=[
            pltpu.VMEM(shape, jnp.float32) for shape in [pack.shape, *shapes[:count]]
        ]
        + [pltpu.SemaphoreType.DMA((count + 1,)), pltpu.SemaphoreType.DMA((count,))],
        compiler_params=pltpu.CompilerParams(vmem_limit_bytes=VMEM_BYTES),
    )(pack, *arrays)


def shards(
    input_feature_maps,
    sequence_slot_lookup,
    sequence_span_lookup,
    opening_reducer,
    downsampling_filter,
    opening_expander,
    skip_projection,
    closing_reducer,
    excite_reducer,
    excite_spatial_filter,
    excite_expander,
    time_taps,
    spatial_filters,
    closing_expander,
    narrow_norm_gains,
    narrow_norm_biases,
    wide_norm_gains,
    wide_norm_biases,
    loss_slope_wrt_final,
):
    k = chain(
        input_feature_maps,
        sequence_slot_lookup,
        sequence_span_lookup,
        opening_reducer,
        downsampling_filter.reshape(3, 1536, 512),
        opening_expander,
        skip_projection,
        closing_reducer,
        excite_reducer.T,
        excite_spatial_filter.reshape(288, 32),
        excite_expander,
        time_taps,
        spatial_filters.reshape(3, 3, 384, 128),
        closing_expander,
        narrow_norm_gains,
        narrow_norm_biases,
        wide_norm_gains,
        wide_norm_biases,
        loss_slope_wrt_final,
        0,
    )
    results = finish(
        k.pack.reshape(-1, 128),
        (
            k.layer_output,
            k.pixels,
            k.narrower.reshape(opening_reducer.shape[0], -1),
            k.strider.reshape(downsampling_filter.shape[:-1] + (-1,)),
            k.widener.reshape(opening_expander.shape[0], -1),
            k.shortcut.reshape(skip_projection.shape[0], -1),
            k.squeezer.reshape(closing_reducer.shape[0], -1),
            k.restorer.reshape(closing_expander.shape[0], -1),
            k.scaling_h,
            k.biasing_h,
            k.amplitudes_h,
            k.baselines_h,
        ),
    )
    condenser, stencil, exciter, temporal, kernels = results[12:]
    return (
        *results[:7],
        condenser.T,
        stencil.transpose(0, 2, 1).reshape(excite_spatial_filter.shape[:-1] + (-1,)),
        exciter,
        temporal,
        kernels.transpose(0, 2, 1).reshape(spatial_filters.shape[:-1] + (-1,)),
        *results[7:12],
    )


def solution(mesh):
    return jax.shard_map(
        shards,
        mesh=mesh,
        in_specs=(
            P("frames", "rows", None, None),
            P("frames"),
            P("frames"),
            P(),
            P(),
            P(),
            P(),
            P(),
            P(),
            P(),
            P(),
            P(),
            P(),
            P(),
            P(),
            P(),
            P(),
            P(),
            P("frames", "rows", None, None),
        ),
        out_specs=(
            P("frames", "rows", None, None),
            P("frames", "rows", None, None),
            P(None, "rows"),
            P(None, None, None, "rows"),
            P(None, "rows"),
            P(None, "rows"),
            P(None, "rows"),
            P(None, "rows"),
            P(None, None, None, "rows"),
            P(None, "rows"),
            P(None, "rows"),
            P(None, None, None, None, "rows"),
            P(None, "rows"),
            P(),
            P(),
            P(),
            P(),
        ),
        check_vma=False,
    )
```
